32 devices in a mesh: parts: 2 (over y), tile: 4 (over z), shot: 4 (over x, core).
Axes of the slice: x: 2, y: 2, z: 4, core: 2. Of those that a mesh axis runs over, the one named last changes fastest.
Arguments:
- velocity: bfloat16 [128, 32, 128], P(('parts', 'tile'), 'shot'), parts along dimension 0, may hold values from 0.14941406 to 0.44921875
- density: bfloat16 [128, 32, 128], P(('parts', 'tile'), 'shot'), parts along dimension 0, may hold values from 1.796875 to 2.59375
- wave_now: bfloat16 [8, 64, 32, 128], P(('parts', 'shot'), 'tile'), parts along dimension 0, may hold values from -6 to 6
- wave_before: bfloat16 [8, 64, 32, 128], P(('parts', 'shot'), 'tile'), parts along dimension 0, may hold values from -6 to 6
- adjoint_end: bfloat16 [8, 64, 32, 128], P(('parts', 'shot'), 'tile'), parts along dimension 0, may hold values from -6 to 6
- adjoint_after: bfloat16 [8, 64, 32, 128], P(('parts', 'shot'), 'tile'), parts along dimension 0, may hold values from -6 to 6
- source_cell: int32 [8], P(('parts', 'shot')), parts along dimension 0, may hold values from 0 to 262143, as said below
- source_wave: float32 [8, 4], P(('parts', 'shot')), parts along dimension 0, may hold values from -8 to 8
- receiver_cell: int32 [8, 256], P(('parts', 'shot')), parts along dimension 0, may hold values from 0 to 262143, as said below
- residual_traces: float32 [8, 4, 256], P(('parts', 'shot')), parts along dimension 0, may hold values from -6 to 6
- aperture: int32 [8, 2], P(('parts', 'shot')), parts along dimension 0, may hold values from -1 to 3, as said below
Outputs:
- gradient: float32 [128, 32, 128], P(('parts', 'tile'), 'shot'), parts along dimension 0
- wave_end: bfloat16 [8, 64, 32, 128], P(('parts', 'shot'), 'tile'), parts along dimension 0
- adjoint_start: bfloat16 [8, 64, 32, 128], P(('parts', 'shot'), 'tile'), parts along dimension 0
The draws below stay inside these ranges and needn't reach their ends.
There are 2 independent parts, one for each index of `parts`. The reference program is written for one: setup_inputs(seed, part) draws one part's arguments, and reference() takes and returns one part's arrays. A program takes and returns all parts, laid end to end along the dimension named above; each array names one. Nothing has to cross between parts.
Inputs may be any that keep to these rules, and one draw needn't show every extreme that they name: `aperture`: row s lists a run of consecutive tile numbers, 1 to 2 of them, followed by -1 entries. `source_cell`: the flat index x * 32 * 128 + y * 128 + z of the shot's source cell, whose x lies in a tile of the shot's aperture. `receiver_cell`: flat indices as for source_cell, each in a tile of the shot's aperture; a cell may repeat.
All inputs are finite; a program needn't handle non-finite values.
Results may differ from the reference program's by a relative error of at most 0.001.
Values may be sent and summed in bfloat16 or wider, within the bound.
No kernel may reach another device: no remote copies, remote signals or barrier semaphores. Data moves between devices by JAX's collectives and lax.ppermute only.
A program may use at most 64 MiB of HBM per device.

```python
import jax
import jax.numpy as jnp
from jax import lax

CX = 16
NY = 32
NZ = 128
STEPS = 4
NREC = 256
SHOTS = 4
NX = 64
APER = 2


def aperture_layout(key):
    tile_count = NX // CX
    start_key, length_key, order_key = jax.random.split(key, 3)
    order = jax.random.permutation(order_key, SHOTS).astype(jnp.int32)
    first_row = order[0]
    last_row = order[1]
    lengths = jax.random.randint(length_key, (SHOTS,), APER // 2, APER + 1)
    lengths = lengths.at[first_row].set(APER // 2).at[last_row].set(APER)
    starts = jax.random.randint(start_key, (SHOTS,), 0, tile_count - lengths + 1)
    starts = starts.at[first_row].set(0).at[last_row].set(tile_count - APER)
    return (starts.astype(jnp.int32), lengths.astype(jnp.int32), first_row, last_row)


def cells_in_aperture(key, starts, lengths, how_many):
    pick_key, row_key, column_key, depth_key = jax.random.split(key, 4)
    tile_pick = starts[:, None] + jax.random.randint(pick_key, (SHOTS, how_many), 0, lengths[:, None])
    row_x = tile_pick * CX + jax.random.randint(row_key, (SHOTS, how_many), 0, CX)
    column_y = jax.random.randint(column_key, (SHOTS, how_many), 0, NY)
    depth_z = jax.random.randint(depth_key, (SHOTS, how_many), 0, NZ)
    return ((row_x * NY + column_y) * NZ + depth_z).astype(jnp.int32)


def draw_aperture(key, part):
    starts, lengths, first_row, last_row = aperture_layout(key)
    slot_range = jnp.arange(APER, dtype=jnp.int32)
    tile_list = starts[:, None] + slot_range[None, :]
    return jnp.where(slot_range[None, :] < lengths[:, None], tile_list, -1).astype(jnp.int32)


def draw_source_cell(key, part):
    starts, lengths, first_row, last_row = aperture_layout(key)
    key = jax.random.fold_in(key, 5)
    placed = cells_in_aperture(key, starts, lengths, 1)[:, 0]
    return placed.at[first_row].set(0).at[last_row].set(NX * NY * NZ - 1).astype(jnp.int32)


def draw_receiver_cell(key, part):
    starts, lengths, first_row, last_row = aperture_layout(key)
    key = jax.random.fold_in(key, 7)
    placed = cells_in_aperture(key, starts, lengths, NREC)
    return placed.at[first_row, 0].set(0).at[last_row, NREC - 1].set(NX * NY * NZ - 1).astype(jnp.int32)


def wave_modes(key, salt_number):
    mode_key = jax.random.fold_in(key, salt_number)
    length_key, sign_key, phase_key, advance_key = jax.random.split(mode_key, 4)
    wave_lengths = jax.random.uniform(length_key, (3, SHOTS, 4), jnp.float32, 30.0, 60.0)
    wave_signs = jnp.where(jax.random.bernoulli(sign_key, 0.5, (3, SHOTS, 4)), 1.0, -1.0)
    wave_numbers = wave_signs * (2.0 * jnp.pi) / wave_lengths
    phase_angles = jax.random.uniform(phase_key, (SHOTS, 4), jnp.float32, 0.0, 2.0 * jnp.pi)
    phase_steps = jax.random.uniform(advance_key, (SHOTS, 4), jnp.float32, 0.02, 0.1)
    return (wave_numbers, phase_angles, phase_steps)


def wave_field(wave_numbers, phase_angles, amplitude, offset_value):
    x_cells = jnp.arange(NX, dtype=jnp.float32)[None, :, None, None]
    y_cells = jnp.arange(NY, dtype=jnp.float32)[None, None, :, None]
    z_cells = jnp.arange(NZ, dtype=jnp.float32)[None, None, None, :]
    summed_field = jnp.full((SHOTS, NX, NY, NZ), offset_value, jnp.float32)
    for component in range(4):
        along_x = wave_numbers[0, :, component][:, None, None, None] * x_cells
        along_y = wave_numbers[1, :, component][:, None, None, None] * y_cells
        along_z = wave_numbers[2, :, component][:, None, None, None] * z_cells
        phase_now = phase_angles[:, component][:, None, None, None]
        summed_field = summed_field + amplitude * jnp.cos(along_x + along_y + along_z + phase_now)
    return summed_field


def draw_wave_now(key, part):
    wave_numbers, phase_angles, phase_steps = wave_modes(key, 1)
    key = jax.random.fold_in(key, 11)
    rough_part = 0.015 * jnp.clip(jax.random.normal(key, (SHOTS, NX, NY, NZ), jnp.float32), -5.0, 5.0)
    smooth_part = wave_field(wave_numbers, phase_angles, 1.2, 0.0)
    return (smooth_part + rough_part).astype(jnp.bfloat16)


def draw_wave_before(key, part):
    wave_numbers, phase_angles, phase_steps = wave_modes(key, 1)
    key = jax.random.fold_in(key, 13)
    rough_part = 0.015 * jnp.clip(jax.random.normal(key, (SHOTS, NX, NY, NZ), jnp.float32), -5.0, 5.0)
    smooth_part = wave_field(wave_numbers, phase_angles - phase_steps, 1.2, 0.0)
    return (smooth_part + rough_part).astype(jnp.bfloat16)


def draw_adjoint_end(key, part):
    wave_numbers, phase_angles, phase_steps = wave_modes(key, 2)
    key = jax.random.fold_in(key, 17)
    rough_part = 0.015 * jnp.clip(jax.random.normal(key, (SHOTS, NX, NY, NZ), jnp.float32), -5.0, 5.0)
    smooth_part = wave_field(wave_numbers, phase_angles, 1.2, 0.0)
    return (smooth_part + rough_part).astype(jnp.bfloat16)


def draw_adjoint_after(key, part):
    wave_numbers, phase_angles, phase_steps = wave_modes(key, 2)
    key = jax.random.fold_in(key, 19)
    rough_part = 0.015 * jnp.clip(jax.random.normal(key, (SHOTS, NX, NY, NZ), jnp.float32), -5.0, 5.0)
    smooth_part = wave_field(wave_numbers, phase_angles + phase_steps, 1.2, 0.0)
    return (smooth_part + rough_part).astype(jnp.bfloat16)


def levels(key, shape, cuts, low, largest):
    level = 1.0
    for dim, blocks in cuts:
        steps = jax.random.uniform(jax.random.fold_in(jax.random.fold_in(key, 6), dim), (blocks,), jnp.float32, low / len(cuts), largest / len(cuts))
        level = level * jnp.repeat(jnp.exp(steps), shape[dim] // blocks).reshape((-1,) + (1,) * (len(shape) - 1 - dim))
    return level


def noise(rng, shape, spread, bound, pieces=(), held_as=jnp.bfloat16):
    entries = spread * jax.random.normal(rng, shape, jnp.float32)
    if pieces:
        entries = entries * levels(rng, shape, pieces, -0.22, 0.18)
    return jnp.clip(entries, -bound, bound).astype(held_as)


def setup_inputs(seed: int = 0, part: int = 0) -> dict:
    seeds = jax.random.split(jax.random.key(seed), 12)
    part_keys = jax.random.split(jax.random.fold_in(seeds[11], part), 12)
    velocity = jnp.clip(0.14941406 + 0.2998047 * jax.random.uniform(part_keys[0], (NX, NY, NZ), jnp.float32) ** levels(part_keys[0], (NX, NY, NZ), ((0, 4), (1, 4)), -0.2, 0.2), 0.14941406, 0.44921875).astype(jnp.bfloat16)
    density = jnp.clip(1.796875 + 0.796875 * jax.random.uniform(part_keys[1], (NX, NY, NZ), jnp.float32) ** levels(part_keys[1], (NX, NY, NZ), ((0, 4), (1, 4)), -0.2, 0.2), 1.796875, 2.59375).astype(jnp.bfloat16)
    wave_now = draw_wave_now(jax.random.fold_in(jax.random.fold_in(seeds[11], part), 71), part)
    wave_before = draw_wave_before(jax.random.fold_in(jax.random.fold_in(seeds[11], part), 71), part)
    adjoint_end = draw_adjoint_end(jax.random.fold_in(jax.random.fold_in(seeds[11], part), 71), part)
    adjoint_after = draw_adjoint_after(jax.random.fold_in(jax.random.fold_in(seeds[11], part), 71), part)
    source_cell = draw_source_cell(jax.random.fold_in(jax.random.fold_in(seeds[11], part), 71), part)
    source_wave = noise(part_keys[7], (SHOTS, STEPS), 2.0, 8.0, ((0, 4),), jnp.float32)
    receiver_cell = draw_receiver_cell(jax.random.fold_in(jax.random.fold_in(seeds[11], part), 71), part)
    residual_traces = noise(part_keys[9], (SHOTS, STEPS, NREC), 1.0, 6.0, ((0, 4),), jnp.float32)
    aperture = draw_aperture(jax.random.fold_in(jax.random.fold_in(seeds[11], part), 71), part)
    return dict(velocity=velocity, density=density, wave_now=wave_now, wave_before=wave_before, adjoint_end=adjoint_end, adjoint_after=adjoint_after, source_cell=source_cell, source_wave=source_wave, receiver_cell=receiver_cell, residual_traces=residual_traces, aperture=aperture)


SECOND_COEFFS = (-205.0 / 72.0, 8.0 / 5.0, -1.0 / 5.0, 8.0 / 315.0, -1.0 / 560.0)
FIRST_COEFFS = (4.0 / 5.0, -1.0 / 5.0, 4.0 / 105.0, -1.0 / 280.0)


def shifted(padded, which_axis, offset_cells):
    leading = padded.ndim - 3
    starts = [0] * padded.ndim
    limits = list(padded.shape)
    for position in range(3):
        starts[leading + position] = 4
        limits[leading + position] = padded.shape[leading + position] - 4
    starts[leading + which_axis] += offset_cells
    limits[leading + which_axis] += offset_cells
    return lax.slice(padded, starts, limits)


def first_diff(padded, which_axis):
    result = 0.0
    for offset_cells in range(1, 5):
        result = result + FIRST_COEFFS[offset_cells - 1] * (shifted(padded, which_axis, offset_cells) - shifted(padded, which_axis, -offset_cells))
    return result


def operate(padded, slopes):
    summed = 3.0 * SECOND_COEFFS[0] * shifted(padded, 0, 0)
    for which_axis in range(3):
        second_term = 0.0
        first_term = 0.0
        for offset_cells in range(1, 5):
            plus_side = shifted(padded, which_axis, offset_cells)
            minus_side = shifted(padded, which_axis, -offset_cells)
            second_term = second_term + SECOND_COEFFS[offset_cells] * (plus_side + minus_side)
            first_term = first_term + FIRST_COEFFS[offset_cells - 1] * (plus_side - minus_side)
        summed = summed + second_term - slopes[which_axis] * first_term
    return summed


def reference(velocity, density, wave_now, wave_before, adjoint_end, adjoint_after, source_cell, source_wave, receiver_cell, residual_traces, aperture):
    speed_cells = velocity.astype(jnp.float32)
    courant_sq = speed_cells * speed_cells
    log_density = jnp.log(density.astype(jnp.float32))
    padded_log = jnp.pad(log_density, 4)
    slopes = tuple(first_diff(padded_log, which_axis) for which_axis in range(3))
    tile_of_row = jnp.arange(NX, dtype=jnp.int32) // CX
    grid_shape = (NX, NY, NZ)

    def one_shot(gradient, inputs):
        now_field, before_field, end_field, after_field, source_index, wavelet, receiver_index, traces, aperture_row = inputs
        active = jnp.any(aperture_row[:, None] == tile_of_row[None, :], axis=0).astype(jnp.float32)[:, None, None]
        previous = before_field.astype(jnp.float32)
        current = now_field.astype(jnp.float32)
        stored = []
        for step_index in range(STEPS):
            applied = operate(jnp.pad(current, 4), slopes)
            updated = 2.0 * current - previous + courant_sq * applied
            updated = updated.reshape(-1).at[source_index].add(wavelet[step_index]).reshape(grid_shape) * active
            stored.append(applied)
            previous, current = current, updated
        adjoint_later = after_field.astype(jnp.float32)
        adjoint = end_field.astype(jnp.float32)
        imaging = jnp.zeros(grid_shape, jnp.float32)
        for step_index in range(STEPS, 0, -1):
            applied = operate(jnp.pad(adjoint, 4), slopes)
            updated = 2.0 * adjoint - adjoint_later + courant_sq * applied
            updated = updated.reshape(-1).at[receiver_index].add(traces[step_index - 1]).reshape(grid_shape) * active
            imaging = imaging + updated * stored[step_index - 1]
            adjoint_later, adjoint = adjoint, updated
        gradient = gradient + 2.0 * speed_cells * imaging
        return gradient, (current.astype(jnp.bfloat16), adjoint.astype(jnp.bfloat16))

    gradient, outputs = lax.scan(one_shot, jnp.zeros(grid_shape, jnp.float32), (wave_now, wave_before, adjoint_end, adjoint_after, source_cell, source_wave, receiver_cell, residual_traces, aperture))
    return gradient, outputs[0], outputs[1]
```

```python
import jax
import jax.numpy as jnp
from jax import lax
from jax.experimental import pallas as pl
from jax.experimental.pallas import tpu as pltpu
from jax.sharding import PartitionSpec as P

FIRST = (672.0, -168.0, 32.0, -3.0)
SECOND = (8064.0, -1008.0, 128.0, -9.0)
CENTRE = -3.0 * 14350.0
SCALE = 5040.0
STEPS = 4
HALO = 4
PAD = 8
VMEM_BYTES = 24 * 1024 * 1024


def vmem():
    return pl.BlockSpec(memory_space=pltpu.VMEM)


def smem():
    return pl.BlockSpec(memory_space=pltpu.SMEM)


def two_terms(values):
    high = values.astype(jnp.bfloat16)
    low = (values - high.astype(jnp.float32)).astype(jnp.bfloat16)
    return high, low


def is_active(aperture_ref, tile):
    found = aperture_ref[0, 0] == tile
    for slot in range(1, aperture_ref.shape[1]):
        found = found | (aperture_ref[0, slot] == tile)
    return found & (tile >= 0)


def layout(aperture_ref, cx):
    tiles = lax.axis_size("tile")
    tile = lax.axis_index("tile")
    even = lax.rem(tile, 2) == 0
    left = is_active(aperture_ref, tile - 1) & (tile > 0)
    right = is_active(aperture_ref, tile + 1) & (tile < tiles - 1)
    own = is_active(aperture_ref, tile)
    a_tile = jnp.where(even, tile + 1, tile - 1)
    b_tile = jnp.where(even, tile - 1, tile + 1)
    a_at = jnp.where(even, 2 * cx, 0)
    b_at = jnp.where(even, 0, 2 * cx)
    a_here = (a_tile >= 0) & (a_tile < tiles)
    b_here = (b_tile >= 0) & (b_tile < tiles)
    a_on = jnp.where(even, right, left)
    b_on = jnp.where(even, left, right)
    return tile, own, left, right, (a_at, a_here, a_on), (b_at, b_here, b_on)


def bounds(step, left, right, cx):
    reach = (STEPS - 1 - step) * HALO
    low = jnp.where(left, cx - reach, cx) // HALO
    high = jnp.where(right, 2 * cx + reach, 2 * cx) // HALO
    return low, high


def setup_kernel(cx, cells_ref, traces_ref, weights_ref, add_ref):
    ny, nz = 32, 128
    rows = lax.broadcasted_iota(jnp.int32, (2 * nz, 2 * nz), 0)
    cols = lax.broadcasted_iota(jnp.int32, (2 * nz, 2 * nz), 1)
    ahead = lax.rem(rows, nz) - lax.rem(cols, nz)
    first = jnp.zeros((2 * nz, 2 * nz), jnp.float32)
    second = jnp.zeros((2 * nz, 2 * nz), jnp.float32)
    for k in range(1, 5):
        first = jnp.where(ahead == k, FIRST[k - 1], jnp.where(ahead == -k, -FIRST[k - 1], first))
        second = jnp.where((ahead == k) | (ahead == -k), SECOND[k - 1], second)
    weights_ref[...] = jnp.where(cols < nz, first, second).astype(jnp.bfloat16)

    tile = lax.axis_index("tile")
    count = cells_ref.shape[1]
    cells = cells_ref[...]
    at_row = cells // nz - (tile - 1) * (cx * ny)
    at_z = lax.rem(cells, nz)
    depth = lax.broadcasted_iota(jnp.int32, (nz, count), 0)
    depth_hot = jnp.where(depth == at_z, 1.0, 0.0).astype(jnp.bfloat16)
    depth_hot = jnp.concatenate([depth_hot, depth_hot], axis=1)
    block = HALO * ny
    row = lax.broadcasted_iota(jnp.int32, (block, count), 0)
    base = 0
    for step in range(STEPS):
        reach = (STEPS - 1 - step) * HALO
        layers = cx + 2 * reach
        trace = traces_ref[0, pl.ds(STEPS - 1 - step, 1), :]
        high = trace.astype(jnp.bfloat16).astype(jnp.float32)
        low = trace - high

        def body(c, carry, base=base, reach=reach, high=high, low=low):
            hot = at_row == row + (cx - reach + c * HALO) * ny
            spread = jnp.concatenate([jnp.where(hot, high, 0.0), jnp.where(hot, low, 0.0)], axis=1).astype(jnp.bfloat16)
            value = lax.dot_general(spread, depth_hot, (((1,), (1,)), ((), ())), preferred_element_type=jnp.float32)
            add_ref[pl.ds(base + c * HALO, HALO)] = value.reshape(HALO, ny, nz)
            return carry

        lax.fori_loop(0, layers // HALO, body, 0)
        base += layers


def differences(buf, i0, weights, ny):
    nz = buf.shape[2]
    middle = buf[pl.ds(i0, HALO), PAD : PAD + ny, :]
    high, low = two_terms(middle.reshape(HALO * ny, nz))
    along_z = jnp.dot(jnp.concatenate([high, low], axis=1), weights, preferred_element_type=jnp.float32)
    along_z = along_z.reshape(HALO, ny, 2 * nz)
    out = []
    for j in range(HALO):
        sums = along_z[j, :, nz:]
        firsts = []
        for axis in range(2):
            first = None
            for k in range(1, 5):
                if axis == 0:
                    plus = buf[i0 + j + k, PAD : PAD + ny, :]
                    minus = buf[i0 + j - k, PAD : PAD + ny, :]
                else:
                    plus = buf[i0 + j, PAD + k : PAD + k + ny, :]
                    minus = buf[i0 + j, PAD - k : PAD - k + ny, :]
                sums = sums + SECOND[k - 1] * (plus + minus)
                term = FIRST[k - 1] * (plus - minus)
                first = term if first is None else first + term
            firsts.append(first)
        firsts.append(along_z[j, :, :nz])
        out.append((middle[j], sums, firsts))
    return out


def march(step, cur, prev, slopes_ref, courant_ref, weights, span, cx, ny, use):
    def body(c, carry):
        i0 = c * HALO
        for j, (centre, sums, firsts) in enumerate(differences(cur, i0, weights, ny)):
            applied = CENTRE * centre + sums
            for axis in range(3):
                applied = applied - slopes_ref[axis, i0 + j] * firsts[axis]
            updated = 2.0 * centre - prev[i0 + j, PAD : PAD + ny, :] + courant_ref[i0 + j] * applied
            updated = use(c, j, applied, updated)
            prev[i0 + j, PAD : PAD + ny, :] = updated
        return carry

    lax.fori_loop(span[0], span[1], body, 0)


def fill(buf, at, rows_ref, first_row, cx, ny, nz, keep):
    part = rows_ref[pl.ds(first_row, cx * ny), :].astype(jnp.float32)
    if keep is not None:
        part = jnp.where(keep, part, 0.0)
    buf[pl.ds(at, cx), PAD : PAD + ny, :] = part.reshape(cx, ny, nz)


def fill_fields(now, before, own_now, own_before, from_a, from_b, side_a, side_b, cx, ny, nz):
    zero = jnp.zeros((3 * cx, PAD, nz), jnp.float32)
    for buf in (now, before):
        buf[:, 0:PAD, :] = zero
        buf[:, PAD + ny : 2 * PAD + ny, :] = zero
    fill(now, cx, own_now, 0, cx, ny, nz, None)
    fill(before, cx, own_before, 0, cx, ny, nz, None)
    for ref, (at, here, on) in ((from_a, side_a), (from_b, side_b)):
        fill(now, at, ref, 0, cx, ny, nz, here)
        fill(before, at, ref, cx * ny, cx, ny, nz, on)


def clear_sides(buf, left, right, cx, ny, nz):
    zero = jnp.zeros((HALO, ny, nz), jnp.float32)

    @pl.when(jnp.logical_not(left))
    def _():
        buf[cx - HALO : cx, PAD : PAD + ny, :] = zero

    @pl.when(jnp.logical_not(right))
    def _():
        buf[2 * cx : 2 * cx + HALO, PAD : PAD + ny, :] = zero


def forward_kernel(
    cx, ny, nz, order, aperture_ref, source_ref, wavelet_ref, *refs
):
    model_refs = refs[: len(order)]
    weights_ref, own_now, own_before, from_a, from_b = refs[len(order) : len(order) + 5]
    slopes_ref, courant_ref, stored_ref, end_ref, gain_ref, log_buf, now, before = refs[len(order) + 5 :]
    tile, own, left, right, side_a, side_b = layout(aperture_ref, cx)
    shot = lax.axis_index("shot")
    sides = ((cx, None), (side_a[0], side_a[1]), (side_b[0], side_b[1]))
    block_rows = ny // len(order)
    size = cx * block_rows

    @pl.when(jnp.logical_not(own))
    def _():
        end_ref[...] = jnp.zeros_like(end_ref)

    @pl.when(own)
    def _():
        zero = jnp.zeros((3 * cx, PAD, nz), jnp.float32)
        log_buf[:, 0:PAD, :] = zero
        log_buf[:, PAD + ny : 2 * PAD + ny, :] = zero
        for ref, mask in zip(model_refs, order):
            y0 = pl.multiple_of((shot ^ mask) * block_rows, block_rows)
            for place, (at, here) in enumerate(sides):
                base = place * 2 * size
                speed = ref[pl.ds(base, size), :].astype(jnp.float32)
                courant = (speed * speed) * (1.0 / SCALE)
                courant_ref[pl.ds(at, cx), pl.ds(y0, block_rows), :] = courant.reshape(cx, block_rows, nz)
                if here is None:
                    gain = speed * (2.0 / SCALE)
                    gain_ref[:, pl.ds(y0, block_rows), :] = gain.reshape(cx, block_rows, nz)
                logs = jnp.log(ref[pl.ds(base + size, size), :].astype(jnp.float32))
                if here is not None:
                    logs = jnp.where(here, logs, 0.0)
                log_buf[pl.ds(at, cx), pl.ds(PAD + y0, block_rows), :] = logs.reshape(cx, block_rows, nz)
        fill_fields(now, before, own_now, own_before, from_a, from_b, side_a, side_b, cx, ny, nz)
        weights = weights_ref[...]

        def slope_body(c, carry):
            i0 = c * HALO
            for j, (centre, sums, firsts) in enumerate(differences(log_buf, i0, weights, ny)):
                for axis in range(3):
                    slopes_ref[axis, i0 + j] = firsts[axis] * (1.0 / 140.0)
            return carry

        span = bounds(0, left, right, cx)
        lax.fori_loop(span[0], span[1], slope_body, 0)

        cell = source_ref[0]
        layer = cell // (ny * nz) - (tile - 1) * cx
        row = lax.rem(cell // nz, ny)
        depth = lax.rem(cell, nz)
        lanes = lax.broadcasted_iota(jnp.int32, (1, nz), 1)
        bufs = (now, before)
        for step in range(STEPS):
            cur, prev = bufs[step % 2], bufs[(step + 1) % 2]
            span = bounds(step, left, right, cx)

            def use(c, j, applied, updated, step=step):
                inner = (c >= cx // HALO) & (c < 2 * cx // HALO)
                at = jnp.where(inner, c * HALO - cx, cx)
                stored_ref[step, at + j] = applied
                return updated

            march(step, cur, prev, slopes_ref, courant_ref, weights, span, cx, ny, use)
            inside = (layer >= span[0] * HALO) & (layer < span[1] * HALO)
            value = wavelet_ref[0, step]

            @pl.when(inside)
            def _(prev=prev, value=value):
                old = prev[layer, pl.ds(PAD + row, 1), :]
                prev[layer, pl.ds(PAD + row, 1), :] = old + jnp.where(lanes == depth, value, 0.0)

            if step == 0:
                clear_sides(cur, left, right, cx, ny, nz)
        last = bufs[STEPS % 2]
        end_ref[...] = last[cx : 2 * cx, PAD : PAD + ny, :].reshape(cx * ny, nz).astype(jnp.bfloat16)


def adjoint_kernel(
    cx, ny, nz, order, aperture_ref, gain_ref, weights_ref, slopes_ref, courant_ref, stored_ref, add_ref, own_now, own_before,
    from_a, from_b, sums_ref, start_ref, now, before, image,
):
    tile, own, left, right, side_a, side_b = layout(aperture_ref, cx)
    shot = lax.axis_index("shot")
    block_rows = ny // len(order)

    @pl.when(jnp.logical_not(own))
    def _():
        start_ref[...] = jnp.zeros_like(start_ref)
        sums_ref[...] = jnp.zeros_like(sums_ref)

    @pl.when(own)
    def _():
        fill_fields(now, before, own_now, own_before, from_a, from_b, side_a, side_b, cx, ny, nz)
        weights = weights_ref[...]
        bufs = (now, before)
        base = 0
        for step in range(STEPS):
            cur, prev = bufs[step % 2], bufs[(step + 1) % 2]
            span = bounds(step, left, right, cx)
            reach = (STEPS - 1 - step) * HALO

            def use(c, j, applied, updated, step=step, base=base, reach=reach):
                updated = updated + add_ref[base + reach - cx + c * HALO + j]
                inner = (c >= cx // HALO) & (c < 2 * cx // HALO)
                at = jnp.where(inner, c * HALO - cx, cx)
                term = updated * stored_ref[STEPS - 1 - step, at + j]
                image[at + j] = term if step == 0 else image[at + j] + term
                return updated

            march(step, cur, prev, slopes_ref, courant_ref, weights, span, cx, ny, use)
            if step == 0:
                clear_sides(cur, left, right, cx, ny, nz)
            base += cx + 2 * reach
        last = bufs[STEPS % 2]
        start_ref[...] = last[cx : 2 * cx, PAD : PAD + ny, :].reshape(cx * ny, nz).astype(jnp.bfloat16)
        for place, mask in enumerate(order):
            y0 = pl.multiple_of((shot ^ mask) * block_rows, block_rows)
            gain = gain_ref[:, pl.ds(y0, block_rows), :]
            sums_ref[place] = (gain * image[0:cx, pl.ds(y0, block_rows), :]).reshape(cx * block_rows, nz)


def pairs(axis_sizes, kind):
    tiles, shots = axis_sizes
    found = []
    for tile in range(tiles):
        other = tile ^ 1 if kind == "a" else ((tile + 1) ^ 1) - 1
        for shot in range(shots):
            here = tile * shots + shot
            if 0 <= other < tiles:
                found.append((here, other * shots + shot))
            elif shots % 2 == 0:
                found.append((here, tile * shots + (shot ^ 1)))
    return found


def local(
    velocity, density, wave_now, wave_before, adjoint_end, adjoint_after, source_cell, source_wave, receiver_cell, residual_traces,
    aperture,
):
    cx, _, nz = velocity.shape
    ny = wave_now.shape[2]
    shots = lax.axis_size("shot")
    tiles = lax.axis_size("tile")
    rows = cx * ny
    params = pltpu.CompilerParams(vmem_limit_bytes=VMEM_BYTES)

    def swap(x, kind):
        return lax.ppermute(x, ("tile", "shot"), pairs((tiles, shots), kind))

    def cross(x, mask):
        return lax.ppermute(x, "shot", [(i, i ^ mask) for i in range(shots)])

    model = jnp.concatenate([velocity.reshape(-1, nz), density.reshape(-1, nz)], axis=0)
    model_a, model_b = swap(model, "a"), swap(model, "b")
    forward = jnp.concatenate([wave_now.reshape(rows, nz), wave_before.reshape(rows, nz)], axis=0)
    forward_a, forward_b = swap(forward, "a"), swap(forward, "b")
    adjoint = jnp.concatenate([adjoint_end.reshape(rows, nz), adjoint_after.reshape(rows, nz)], axis=0)
    adjoint_a, adjoint_b = swap(adjoint, "a"), swap(adjoint, "b")

    held = [(0, jnp.concatenate([model, model_a, model_b], axis=0))]
    mask = shots // 2
    while mask:
        if len(held) > 1:
            moved = cross(jnp.stack([block for _, block in held]), mask)
            held = held + [(m ^ mask, moved[i]) for i, (m, _) in enumerate(held)]
        else:
            held = held + [(mask, cross(held[0][1], mask))]
        mask //= 2

    added_layers = sum(cx + 2 * (STEPS - 1 - step) * HALO for step in range(STEPS))
    weights, added = pl.pallas_call(
        lambda *refs: setup_kernel(cx, *refs),
        out_shape=(
            jax.ShapeDtypeStruct((2 * nz, 2 * nz), jnp.bfloat16),
            jax.ShapeDtypeStruct((added_layers, ny, nz), jnp.float32),
        ),
        in_specs=[vmem()] * 2,
        out_specs=(vmem(), vmem()),
        compiler_params=params,
        name="receivers",
    )(receiver_cell, residual_traces)

    order = tuple(m for m, _ in held)
    field = pltpu.VMEM((3 * cx, 2 * PAD + ny, nz), jnp.float32)
    slopes, courant, stored, wave_end, gain = pl.pallas_call(
        lambda *refs: forward_kernel(cx, ny, nz, order, *refs),
        out_shape=(
            jax.ShapeDtypeStruct((3, 3 * cx, ny, nz), jnp.float32),
            jax.ShapeDtypeStruct((3 * cx, ny, nz), jnp.float32),
            jax.ShapeDtypeStruct((STEPS, cx + HALO, ny, nz), jnp.float32),
            jax.ShapeDtypeStruct((rows, nz), jnp.bfloat16),
            jax.ShapeDtypeStruct((cx, ny, nz), jnp.float32),
        ),
        in_specs=[smem()] * 3 + [vmem()] * (len(order) + 5),
        out_specs=(vmem(),) * 5,
        scratch_shapes=[field, field, field],
        compiler_params=params,
        name="forward",
    )(
        aperture, source_cell, source_wave, *[block for _, block in held], weights,
        wave_now.reshape(rows, nz), wave_before.reshape(rows, nz), forward_a, forward_b,
    )

    bits = []
    mask = 1
    while mask < shots:
        bits.append(mask)
        mask *= 2
    sum_order = [0]
    for bit in reversed(bits):
        sum_order = sum_order + [m | bit for m in sum_order]
    sum_order = tuple(sum_order)
    block = cx * (ny // shots)
    sums, adjoint_start = pl.pallas_call(
        lambda *refs: adjoint_kernel(cx, ny, nz, sum_order, *refs),
        out_shape=(
            jax.ShapeDtypeStruct((shots, block, nz), jnp.float32),
            jax.ShapeDtypeStruct((rows, nz), jnp.bfloat16),
        ),
        in_specs=[smem()] + [vmem()] * 10,
        out_specs=(vmem(),) * 2,
        scratch_shapes=[field, field, pltpu.VMEM((cx + HALO, ny, nz), jnp.float32)],
        compiler_params=params,
        name="adjoint",
    )(
        aperture, gain, weights, slopes, courant, stored, added, adjoint_end.reshape(rows, nz), adjoint_after.reshape(rows, nz),
        adjoint_a, adjoint_b,
    )
    for bit in bits:
        half = sums.shape[0] // 2
        sums = sums[:half] + cross(sums[half:], bit)
    gradient = sums[0].reshape(cx, ny // shots, nz)
    return gradient, wave_end.reshape(wave_now.shape), adjoint_start.reshape(wave_now.shape)


def solution(mesh):
    stored = P(("parts", "tile"), "shot", None)
    field = P(("parts", "shot"), "tile", None, None)
    return jax.shard_map(
        local,
        mesh=mesh,
        in_specs=(
            stored, stored, field, field, field, field, P(("parts", "shot")), P(("parts", "shot"), None),
            P(("parts", "shot"), None), P(("parts", "shot"), None, None), P(("parts", "shot"), None),
        ),
        out_specs=(stored, field, field),
        check_vma=False,
    )
```

```python
import jax
import jax.numpy as jnp
from jax import lax
from jax.experimental import pallas as pl
from jax.experimental.pallas import tpu as pltpu
from jax.sharding import PartitionSpec as P

FIRST = (672.0, -168.0, 32.0, -3.0)
SECOND = (8064.0, -1008.0, 128.0, -9.0)
CENTRE = -3.0 * 14350.0
SCALE = 5040.0
STEPS = 4
HALO = 4
PAD = 8
VMEM_BYTES = 24 * 1024 * 1024


def vmem():
    return pl.BlockSpec(memory_space=pltpu.VMEM)


def smem():
    return pl.BlockSpec(memory_space=pltpu.SMEM)


def two_terms(values):
    high = values.astype(jnp.bfloat16)
    low = (values - high.astype(jnp.float32)).astype(jnp.bfloat16)
    return high, low


def is_active(aperture_ref, tile):
    found = aperture_ref[0, 0] == tile
    for slot in range(1, aperture_ref.shape[1]):
        found = found | (aperture_ref[0, slot] == tile)
    return found & (tile >= 0)


def layout(aperture_ref, cx):
    tiles = lax.axis_size("tile")
    tile = lax.axis_index("tile")
    even = lax.rem(tile, 2) == 0
    left = is_active(aperture_ref, tile - 1) & (tile > 0)
    right = is_active(aperture_ref, tile + 1) & (tile < tiles - 1)
    own = is_active(aperture_ref, tile)
    a_tile = jnp.where(even, tile + 1, tile - 1)
    b_tile = jnp.where(even, tile - 1, tile + 1)
    a_at = jnp.where(even, 2 * cx, 0)
    b_at = jnp.where(even, 0, 2 * cx)
    a_here = (a_tile >= 0) & (a_tile < tiles)
    b_here = (b_tile >= 0) & (b_tile < tiles)
    a_on = jnp.where(even, right, left)
    b_on = jnp.where(even, left, right)
    return tile, own, left, right, (a_at, a_here, a_on), (b_at, b_here, b_on)


def bounds(step, left, right, cx):
    reach = (STEPS - 1 - step) * HALO
    low = jnp.where(left, cx - reach, cx) // HALO
    high = jnp.where(right, 2 * cx + reach, 2 * cx) // HALO
    return low, high


def setup_kernel(cx, cells_ref, traces_ref, *refs):
    parts, (weights_ref, add_ref, joined_ref) = refs[:-3], refs[-3:]
    ny, nz = add_ref.shape[2:]
    size = parts[0].shape[0]
    for number, part in enumerate(parts):
        joined_ref[number * size : (number + 1) * size, :] = part[...]
    rows = lax.broadcasted_iota(jnp.int32, (2 * nz, 2 * nz), 0)
    cols = lax.broadcasted_iota(jnp.int32, (2 * nz, 2 * nz), 1)
    ahead = lax.rem(rows, nz) - lax.rem(cols, nz)
    first = jnp.zeros((2 * nz, 2 * nz), jnp.float32)
    second = jnp.zeros((2 * nz, 2 * nz), jnp.float32)
    for k in range(1, 5):
        first = jnp.where(ahead == k, FIRST[k - 1], jnp.where(ahead == -k, -FIRST[k - 1], first))
        second = jnp.where((ahead == k) | (ahead == -k), SECOND[k - 1], second)
    weights_ref[...] = jnp.where(cols < nz, first, second).astype(jnp.bfloat16)

    tile = lax.axis_index("tile")
    count = cells_ref.shape[1]
    cells = cells_ref[...]
    reach = (STEPS - 1) * HALO
    at_row = cells // nz - (tile * cx - reach) * ny
    at_z = lax.rem(cells, nz)
    depth = lax.broadcasted_iota(jnp.int32, (nz, count), 0)
    deep = depth == at_z
    values = []
    for step in range(STEPS):
        trace = traces_ref[0, pl.ds(STEPS - 1 - step, 1), :]
        high = trace.astype(jnp.bfloat16).astype(jnp.float32)
        values += [jnp.where(deep, high, 0.0), jnp.where(deep, trace - high, 0.0)]
    values = jnp.concatenate(values, axis=0).astype(jnp.bfloat16)
    chunk = 2 * HALO
    row = lax.broadcasted_iota(jnp.int32, (chunk * ny, count), 0)

    def body(c, carry):
        hot = jnp.where(at_row == row + c * (chunk * ny), 1.0, 0.0).astype(jnp.bfloat16)
        found = lax.dot_general(hot, values, (((1,), (1,)), ((), ())), preferred_element_type=jnp.float32)
        for step in range(STEPS):
            both = found[:, 2 * step * nz : (2 * step + 1) * nz] + found[:, (2 * step + 1) * nz : (2 * step + 2) * nz]
            add_ref[step, pl.ds(c * chunk, chunk)] = both.reshape(chunk, ny, nz)
        return carry

    lax.fori_loop(0, (cx + 2 * reach) // chunk, body, 0)


def differences(buf, i0, weights, ny):
    nz = buf.shape[2]
    middle = buf[pl.ds(i0, HALO), PAD : PAD + ny, :]
    high, low = two_terms(middle.reshape(HALO * ny, nz))
    along_z = jnp.dot(jnp.concatenate([high, low], axis=1), weights, preferred_element_type=jnp.float32)
    along_z = along_z.reshape(HALO, ny, 2 * nz)
    out = []
    for j in range(HALO):
        sums = along_z[j, :, nz:]
        firsts = []
        for axis in range(2):
            first = None
            for k in range(1, 5):
                if axis == 0:
                    plus = buf[i0 + j + k, PAD : PAD + ny, :]
                    minus = buf[i0 + j - k, PAD : PAD + ny, :]
                else:
                    plus = buf[i0 + j, PAD + k : PAD + k + ny, :]
                    minus = buf[i0 + j, PAD - k : PAD - k + ny, :]
                sums = sums + SECOND[k - 1] * (plus + minus)
                term = FIRST[k - 1] * (plus - minus)
                first = term if first is None else first + term
            firsts.append(first)
        firsts.append(along_z[j, :, :nz])
        out.append((middle[j], sums, firsts))
    return out


def march(step, cur, prev, slopes_ref, courant_ref, weights, span, cx, ny, use):
    def body(c, carry):
        i0 = c * HALO
        for j, (centre, sums, firsts) in enumerate(differences(cur, i0, weights, ny)):
            applied = CENTRE * centre + sums
            for axis in range(3):
                applied = applied - slopes_ref[axis, i0 + j] * firsts[axis]
            updated = 2.0 * centre - prev[i0 + j, PAD : PAD + ny, :] + courant_ref[i0 + j] * applied
            updated = use(c, j, applied, updated)
            prev[i0 + j, PAD : PAD + ny, :] = updated
        return carry

    lax.fori_loop(span[0], span[1], body, 0)


def fill(buf, at, rows_ref, first_row, cx, ny, nz, keep):
    part = rows_ref[pl.ds(first_row, cx * ny), :].astype(jnp.float32)
    if keep is not None:
        part = jnp.where(keep, part, 0.0)
    buf[pl.ds(at, cx), PAD : PAD + ny, :] = part.reshape(cx, ny, nz)


def fill_fields(now, before, own_now, own_before, from_a, from_b, side_a, side_b, cx, ny, nz):
    zero = jnp.zeros((3 * cx, PAD, nz), jnp.float32)
    for buf in (now, before):
        buf[:, 0:PAD, :] = zero
        buf[:, PAD + ny : 2 * PAD + ny, :] = zero
    fill(now, cx, own_now, 0, cx, ny, nz, None)
    fill(before, cx, own_before, 0, cx, ny, nz, None)
    for ref, (at, here, on) in ((from_a, side_a), (from_b, side_b)):
        fill(now, at, ref, 0, cx, ny, nz, here)
        fill(before, at, ref, cx * ny, cx, ny, nz, on)


def clear_sides(buf, left, right, cx, ny, nz):
    zero = jnp.zeros((HALO, ny, nz), jnp.float32)

    @pl.when(jnp.logical_not(left))
    def _():
        buf[cx - HALO : cx, PAD : PAD + ny, :] = zero

    @pl.when(jnp.logical_not(right))
    def _():
        buf[2 * cx : 2 * cx + HALO, PAD : PAD + ny, :] = zero


def forward_kernel(cx, ny, nz, shots, blocks, aperture_ref, source_ref, wavelet_ref, *refs):
    model_refs = refs[: len(blocks)]
    weights_ref, own_now, own_before, from_a, from_b = refs[len(blocks) : len(blocks) + 5]
    slopes_ref, courant_ref, stored_ref, end_ref, gain_ref, log_buf, now, before = refs[len(blocks) + 5 :]
    tile, own, left, right, side_a, side_b = layout(aperture_ref, cx)
    shot = lax.axis_index("shot")
    sides = ((cx, None), (side_a[0], side_a[1]), (side_b[0], side_b[1]))
    block_rows = ny // shots
    size = cx * block_rows

    @pl.when(jnp.logical_not(own))
    def _():
        end_ref[...] = jnp.zeros_like(end_ref)

    @pl.when(own)
    def _():
        zero = jnp.zeros((3 * cx, PAD, nz), jnp.float32)
        log_buf[:, 0:PAD, :] = zero
        log_buf[:, PAD + ny : 2 * PAD + ny, :] = zero
        for ref, held in zip(model_refs, blocks):
            for number, (mask, place) in enumerate(held):
                y0 = pl.multiple_of((shot ^ mask) * block_rows, block_rows)
                at, here = sides[place]
                base = number * 2 * size
                speed = ref[pl.ds(base, size), :].astype(jnp.float32)
                courant = (speed * speed) * (1.0 / SCALE)
                courant_ref[pl.ds(at, cx), pl.ds(y0, block_rows), :] = courant.reshape(cx, block_rows, nz)
                if here is None:
                    gain = speed * (2.0 / SCALE)
                    gain_ref[:, pl.ds(y0, block_rows), :] = gain.reshape(cx, block_rows, nz)
                logs = jnp.log(ref[pl.ds(base + size, size), :].astype(jnp.float32))
                if here is not None:
                    logs = jnp.where(here, logs, 0.0)
                log_buf[pl.ds(at, cx), pl.ds(PAD + y0, block_rows), :] = logs.reshape(cx, block_rows, nz)
        fill_fields(now, before, own_now, own_before, from_a, from_b, side_a, side_b, cx, ny, nz)
        weights = weights_ref[...]

        def slope_body(c, carry):
            i0 = c * HALO
            for j, (centre, sums, firsts) in enumerate(differences(log_buf, i0, weights, ny)):
                for axis in range(3):
                    slopes_ref[axis, i0 + j] = firsts[axis] * (1.0 / 140.0)
            return carry

        span = bounds(0, left, right, cx)
        lax.fori_loop(span[0], span[1], slope_body, 0)

        cell = source_ref[0]
        layer = cell // (ny * nz) - (tile - 1) * cx
        row = lax.rem(cell // nz, ny)
        depth = lax.rem(cell, nz)
        lanes = lax.broadcasted_iota(jnp.int32, (1, nz), 1)
        bufs = (now, before)
        for step in range(STEPS):
            cur, prev = bufs[step % 2], bufs[(step + 1) % 2]
            span = bounds(step, left, right, cx)

            def use(c, j, applied, updated, step=step):
                inner = (c >= cx // HALO) & (c < 2 * cx // HALO)
                at = jnp.where(inner, c * HALO - cx, cx)
                stored_ref[step, at + j] = applied
                return updated

            march(step, cur, prev, slopes_ref, courant_ref, weights, span, cx, ny, use)
            inside = (layer >= span[0] * HALO) & (layer < span[1] * HALO)
            value = wavelet_ref[0, step]

            @pl.when(inside)
            def _(prev=prev, value=value):
                old = prev[layer, pl.ds(PAD + row, 1), :]
                prev[layer, pl.ds(PAD + row, 1), :] = old + jnp.where(lanes == depth, value, 0.0)

            if step == 0:
                clear_sides(cur, left, right, cx, ny, nz)
        last = bufs[STEPS % 2]
        end_ref[...] = last[cx : 2 * cx, PAD : PAD + ny, :].reshape(cx * ny, nz).astype(jnp.bfloat16)


def adjoint_kernel(
    cx, ny, nz, order, aperture_ref, gain_ref, weights_ref, slopes_ref, courant_ref, stored_ref, add_ref, own_now, own_before,
    from_a, from_b, sums_ref, start_ref, now, before, image,
):
    tile, own, left, right, side_a, side_b = layout(aperture_ref, cx)
    shot = lax.axis_index("shot")
    block_rows = ny // len(order)

    @pl.when(jnp.logical_not(own))
    def _():
        start_ref[...] = jnp.zeros_like(start_ref)
        sums_ref[...] = jnp.zeros_like(sums_ref)

    @pl.when(own)
    def _():
        fill_fields(now, before, own_now, own_before, from_a, from_b, side_a, side_b, cx, ny, nz)
        weights = weights_ref[...]
        bufs = (now, before)
        for step in range(STEPS):
            cur, prev = bufs[step % 2], bufs[(step + 1) % 2]
            span = bounds(step, left, right, cx)

            def use(c, j, applied, updated, step=step):
                updated = updated + add_ref[step, c * HALO + j - (cx - (STEPS - 1) * HALO)]
                inner = (c >= cx // HALO) & (c < 2 * cx // HALO)
                at = jnp.where(inner, c * HALO - cx, cx)
                term = updated * stored_ref[STEPS - 1 - step, at + j]
                image[at + j] = term if step == 0 else image[at + j] + term
                return updated

            march(step, cur, prev, slopes_ref, courant_ref, weights, span, cx, ny, use)
            if step == 0:
                clear_sides(cur, left, right, cx, ny, nz)
        last = bufs[STEPS % 2]
        start_ref[...] = last[cx : 2 * cx, PAD : PAD + ny, :].reshape(cx * ny, nz).astype(jnp.bfloat16)
        for place, mask in enumerate(order):
            y0 = pl.multiple_of((shot ^ mask) * block_rows, block_rows)
            gain = gain_ref[:, pl.ds(y0, block_rows), :]
            sums_ref[place] = (gain * image[0:cx, pl.ds(y0, block_rows), :]).reshape(cx * block_rows, nz)


def pairs(axis_sizes, kind):
    tiles, shots = axis_sizes
    found = []
    for tile in range(tiles):
        other = tile ^ 1 if kind == "a" else ((tile + 1) ^ 1) - 1
        for shot in range(shots):
            here = tile * shots + shot
            if 0 <= other < tiles:
                found.append((here, other * shots + shot))
            elif shots % 2 == 0:
                found.append((here, tile * shots + (shot ^ 1)))
    return found


def local(
    velocity, density, wave_now, wave_before, adjoint_end, adjoint_after, source_cell, source_wave, receiver_cell, residual_traces,
    aperture,
):
    cx, _, nz = velocity.shape
    ny = wave_now.shape[2]
    shots = lax.axis_size("shot")
    tiles = lax.axis_size("tile")
    rows = cx * ny
    params = pltpu.CompilerParams(vmem_limit_bytes=VMEM_BYTES)

    def swap(x, kind):
        return lax.ppermute(x, ("tile", "shot"), pairs((tiles, shots), kind))

    def cross(x, mask):
        return lax.ppermute(x, "shot", [(i, i ^ mask) for i in range(shots)])

    model = jnp.concatenate([velocity.reshape(-1, nz), density.reshape(-1, nz)], axis=0)
    model_a, model_b = swap(model, "a"), swap(model, "b")
    forward = jnp.concatenate([wave_now.reshape(rows, nz), wave_before.reshape(rows, nz)], axis=0)
    high = shots // 2
    near = [([(0, 0)], model), ([(0, 1)], model_a), ([(0, 2)], model_b)]
    late = []
    if high:
        model_c = cross(model, high)
        forward_a, forward_b = swap(forward, "a"), swap(forward, "b")
        near.append(([(high, 0)], model_c))
        late.append(([(high, 1), (high, 2)], cross(jnp.concatenate([model_a, model_b], axis=0), high)))
    else:
        forward_a, forward_b = swap(forward, "a"), swap(forward, "b")
    mask = high // 2
    adjoint = jnp.concatenate([adjoint_end.reshape(rows, nz), adjoint_after.reshape(rows, nz)], axis=0)
    adjoint_a, adjoint_b = swap(adjoint, "a"), swap(adjoint, "b")

    weights, added, joined = pl.pallas_call(
        lambda *refs: setup_kernel(cx, *refs),
        out_shape=(
            jax.ShapeDtypeStruct((2 * nz, 2 * nz), jnp.bfloat16),
            jax.ShapeDtypeStruct((STEPS, cx + 2 * (STEPS - 1) * HALO, ny, nz), jnp.float32),
            jax.ShapeDtypeStruct((len(near) * model.shape[0], nz), jnp.bfloat16),
        ),
        in_specs=[vmem()] * (2 + len(near)),
        out_specs=(vmem(),) * 3,
        compiler_params=params,
        cost_estimate=pl.CostEstimate(flops=2 * 10**9, bytes_accessed=4 * 2**20, transcendentals=0),
        name="receivers",
    )(receiver_cell, residual_traces, *[block for _, block in near])

    near = [([name for names, _ in near for name in names], joined)]
    while mask:
        moved = []
        for group in (near, late):
            names = [(m ^ mask, place) for held, _ in group for m, place in held]
            array = group[0][1] if len(group) == 1 else jnp.concatenate([block for _, block in group], axis=0)
            moved.append((names, cross(array, mask)))
        near, late = near + moved[:1], late + moved[1:]
        mask //= 2
    held = near + late

    field = pltpu.VMEM((3 * cx, 2 * PAD + ny, nz), jnp.float32)
    blocks = tuple(tuple(names) for names, _ in held)
    slopes, courant, stored, wave_end, gain = pl.pallas_call(
        lambda *refs: forward_kernel(cx, ny, nz, shots, blocks, *refs),
        out_shape=(
            jax.ShapeDtypeStruct((3, 3 * cx, ny, nz), jnp.float32),
            jax.ShapeDtypeStruct((3 * cx, ny, nz), jnp.float32),
            jax.ShapeDtypeStruct((STEPS, cx + HALO, ny, nz), jnp.float32),
            jax.ShapeDtypeStruct((rows, nz), jnp.bfloat16),
            jax.ShapeDtypeStruct((cx, ny, nz), jnp.float32),
        ),
        in_specs=[smem()] * 3 + [vmem()] * (len(held) + 5),
        out_specs=(vmem(),) * 5,
        scratch_shapes=[field, field, field],
        compiler_params=params,
        cost_estimate=pl.CostEstimate(flops=5 * 10**9, bytes_accessed=8 * 2**20, transcendentals=0),
        name="forward",
    )(
        aperture, source_cell, source_wave, *[block for _, block in held], weights,
        wave_now.reshape(rows, nz), wave_before.reshape(rows, nz), forward_a, forward_b,
    )

    bits = []
    mask = 1
    while mask < shots:
        bits.append(mask)
        mask *= 2
    sum_order = [0]
    for bit in reversed(bits):
        sum_order = sum_order + [m | bit for m in sum_order]
    sum_order = tuple(sum_order)
    block = cx * (ny // shots)
    sums, adjoint_start = pl.pallas_call(
        lambda *refs: adjoint_kernel(cx, ny, nz, sum_order, *refs),
        out_shape=(
            jax.ShapeDtypeStruct((shots, block, nz), jnp.float32),
            jax.ShapeDtypeStruct((rows, nz), jnp.bfloat16),
        ),
        in_specs=[smem()] + [vmem()] * 10,
        out_specs=(vmem(),) * 2,
        scratch_shapes=[field, field, pltpu.VMEM((cx + HALO, ny, nz), jnp.float32)],
        compiler_params=params,
        cost_estimate=pl.CostEstimate(flops=5 * 10**9, bytes_accessed=8 * 2**20, transcendentals=0),
        name="adjoint",
    )(
        aperture, gain, weights, slopes, courant, stored, added, adjoint_end.reshape(rows, nz), adjoint_after.reshape(rows, nz),
        adjoint_a, adjoint_b,
    )
    for bit in bits:
        half = sums.shape[0] // 2
        sums = sums[:half] + cross(sums[half:], bit)
    gradient = sums[0].reshape(cx, ny // shots, nz)
    return gradient, wave_end.reshape(wave_now.shape), adjoint_start.reshape(wave_now.shape)


def solution(mesh):
    stored = P(("parts", "tile"), "shot", None)
    field = P(("parts", "shot"), "tile", None, None)
    return jax.shard_map(
        local,
        mesh=mesh,
        in_specs=(
            stored, stored, field, field, field, field, P(("parts", "shot")), P(("parts", "shot"), None),
            P(("parts", "shot"), None), P(("parts", "shot"), None, None), P(("parts", "shot"), None),
        ),
        out_specs=(stored, field, field),
        check_vma=False,
    )
```

```python
import jax
import jax.numpy as jnp
from jax import lax
from jax.experimental import pallas as pl
from jax.experimental.pallas import tpu as pltpu
from jax.sharding import PartitionSpec as P

FIRST = (672.0, -168.0, 32.0, -3.0)
SECOND = (8064.0, -1008.0, 128.0, -9.0)
CENTRE_Z = -43008.0
CENTRE_Y = -42.0
SCALE = 5040.0
STEPS = 4
HALO = 4
VMEM_BYTES = 24 * 1024 * 1024


def vmem():
    return pl.BlockSpec(memory_space=pltpu.VMEM)


def smem():
    return pl.BlockSpec(memory_space=pltpu.SMEM)


def two_terms(values):
    high = values.astype(jnp.bfloat16)
    low = (values - high.astype(jnp.float32)).astype(jnp.bfloat16)
    return high, low


def is_active(aperture_ref, tile):
    found = aperture_ref[0, 0] == tile
    for slot in range(1, aperture_ref.shape[1]):
        found = found | (aperture_ref[0, slot] == tile)
    return found & (tile >= 0)


def layout(aperture_ref, cx):
    tiles = lax.axis_size("tile")
    tile = lax.axis_index("tile")
    even = lax.rem(tile, 2) == 0
    left = is_active(aperture_ref, tile - 1) & (tile > 0)
    right = is_active(aperture_ref, tile + 1) & (tile < tiles - 1)
    own = is_active(aperture_ref, tile)
    a_tile = jnp.where(even, tile + 1, tile - 1)
    b_tile = jnp.where(even, tile - 1, tile + 1)
    a_at = jnp.where(even, 2 * cx, 0)
    b_at = jnp.where(even, 0, 2 * cx)
    a_here = (a_tile >= 0) & (a_tile < tiles)
    b_here = (b_tile >= 0) & (b_tile < tiles)
    a_on = jnp.where(even, right, left)
    b_on = jnp.where(even, left, right)
    return tile, own, left, right, (a_at, a_here, a_on), (b_at, b_here, b_on)


def difference_matrix(shape, along, across, block, centre):
    ahead = lax.rem(along, block) - lax.rem(across, block)
    first = jnp.zeros(shape, jnp.float32)
    second = jnp.where(ahead == 0, centre, 0.0)
    for k in range(1, 5):
        first = jnp.where(ahead == k, FIRST[k - 1], jnp.where(ahead == -k, -FIRST[k - 1], first))
        second = jnp.where((ahead == k) | (ahead == -k), SECOND[k - 1], second)
    return first, second


def setup_kernel(cx, cells_ref, traces_ref, *refs):
    parts, (along_z_ref, along_y_ref, add_ref, joined_ref) = refs[:-4], refs[-4:]
    ny, nz = add_ref.shape[2:]
    size = parts[0].shape[0]
    for number, part in enumerate(parts):
        joined_ref[number * size : (number + 1) * size, :] = part[...]

    shape = along_z_ref.shape
    rows, cols = (lax.broadcasted_iota(jnp.int32, shape, d) for d in range(2))
    first, second = difference_matrix(shape, rows, cols, nz, CENTRE_Z)
    along_z_ref[...] = jnp.where(cols < nz, first, second).astype(jnp.bfloat16)
    shape = along_y_ref.shape
    rows, cols = (lax.broadcasted_iota(jnp.int32, shape, d) for d in range(2))
    first, second = difference_matrix(shape, cols, rows, ny, CENTRE_Y)
    here = lax.rem(rows, shape[1]) // ny == cols // ny
    along_y_ref[...] = jnp.where(here, jnp.where(rows < shape[1], first, second), 0.0).astype(jnp.bfloat16)

    tile = lax.axis_index("tile")
    count = cells_ref.shape[1]
    cells = cells_ref[...]
    reach = (STEPS - 1) * HALO
    at_row = cells // nz - (tile * cx - reach) * ny
    at_z = lax.rem(cells, nz)
    depth = lax.broadcasted_iota(jnp.int32, (nz, count), 0)
    deep = depth == at_z
    tile = lax.axis_index("tile")
    count = cells_ref.shape[1]
    cells = cells_ref[...]
    reach = (STEPS - 1) * HALO
    at_row = cells // nz - (tile * cx - reach) * ny
    at_z = lax.rem(cells, nz)
    depth = lax.broadcasted_iota(jnp.int32, (nz, count), 0)
    deep = depth == at_z
    values = []
    for step in range(STEPS):
        trace = traces_ref[0, pl.ds(STEPS - 1 - step, 1), :]
        high = trace.astype(jnp.bfloat16).astype(jnp.float32)
        values += [jnp.where(deep, high, 0.0), jnp.where(deep, trace - high, 0.0)]
    values = jnp.concatenate(values, axis=0).astype(jnp.bfloat16)
    chunk = 2 * HALO
    row = lax.broadcasted_iota(jnp.int32, (chunk * ny, count), 0)

    def body(c, carry):
        hot = jnp.where(at_row == row + c * (chunk * ny), 1.0, 0.0).astype(jnp.bfloat16)
        found = lax.dot_general(hot, values, (((1,), (1,)), ((), ())), preferred_element_type=jnp.float32)
        for step in range(STEPS):
            both = found[:, 2 * step * nz : (2 * step + 1) * nz] + found[:, (2 * step + 1) * nz : (2 * step + 2) * nz]
            add_ref[step, pl.ds(c * chunk, chunk)] = both.reshape(chunk, ny, nz)
        return carry

    lax.fori_loop(0, (cx + 2 * reach) // chunk, body, 0)


def matrix_differences(buf, i0, layers, along_z, along_y):
    ny, nz = buf.shape[1:]
    both = jnp.concatenate(two_terms(buf[pl.ds(i0, layers)].reshape(layers * ny, nz)), axis=1)
    from_z = jnp.dot(both, along_z, preferred_element_type=jnp.float32)
    size = along_y.shape[1]
    half = along_y.shape[0] // 2
    first_y, second = [], []
    for base in range(0, layers * ny, size):
        from_y = jnp.dot(along_y, both[base : base + size], preferred_element_type=jnp.float32)
        first_y.append(from_y[:size, :nz] + from_y[:size, nz:])
        if half == size:
            second.append(from_y[size:, :nz] + from_y[size:, nz:] + from_z[base : base + size, nz:])
    shape = (layers, ny, nz)
    first_y, first_z = jnp.concatenate(first_y, axis=0), from_z[:, :nz]
    if not second:
        return first_y.reshape(shape), first_z.reshape(shape), None
    return first_y.reshape(shape), first_z.reshape(shape), jnp.concatenate(second, axis=0).reshape(shape)


def layer_differences(buf, i, summed):
    first = None
    for k in range(1, 5):
        plus, minus = buf[i + k], buf[i - k]
        if summed is not None:
            summed = summed + SECOND[k - 1] * (plus + minus)
        term = FIRST[k - 1] * (plus - minus)
        first = term if first is None else first + term
    return first, summed


def on_segments(step, left, right, cx, work):
    work(cx, cx, True)
    reach = (STEPS - 1 - step) * HALO
    if reach:

        def body(number, carry):
            base = jnp.where(left & (number == 0), cx - reach, 2 * cx)
            work(pl.multiple_of(base, HALO), reach, False)
            return carry

        lax.fori_loop(0, left.astype(jnp.int32) + right.astype(jnp.int32), body, 0)


def march(cur, prev, slopes_ref, courant_ref, along_z, along_y, i0, layers, use):
    first_y, first_z, second = matrix_differences(cur, i0, layers, along_z, along_y)
    for j in range(layers):
        i = i0 + j
        first_x, applied = layer_differences(cur, i, second[j])
        applied = applied - slopes_ref[0, i] * first_x - slopes_ref[1, i] * first_y[j] - slopes_ref[2, i] * first_z[j]
        prev[i] = use(i, j, applied, 2.0 * cur[i] - prev[i] + courant_ref[i] * applied)


def fill(buf, at, rows_ref, first_row, cx, ny, nz, keep):
    part = rows_ref[pl.ds(first_row, cx * ny), :].astype(jnp.float32)
    if keep is not None:
        part = jnp.where(keep, part, 0.0)
    buf[pl.ds(at, cx)] = part.reshape(cx, ny, nz)


def fill_fields(now, before, own_now, own_before, from_a, from_b, side_a, side_b, cx, ny, nz):
    fill(now, cx, own_now, 0, cx, ny, nz, None)
    fill(before, cx, own_before, 0, cx, ny, nz, None)
    for ref, (at, here, on) in ((from_a, side_a), (from_b, side_b)):
        fill(now, at, ref, 0, cx, ny, nz, here)
        fill(before, at, ref, cx * ny, cx, ny, nz, on)


def clear_sides(buf, left, right, cx):
    zero = jnp.zeros((HALO,) + buf.shape[1:], jnp.float32)

    @pl.when(jnp.logical_not(left))
    def _():
        buf[cx - HALO : cx] = zero

    @pl.when(jnp.logical_not(right))
    def _():
        buf[2 * cx : 2 * cx + HALO] = zero


def forward_kernel(cx, ny, nz, shots, blocks, aperture_ref, source_ref, wavelet_ref, *refs):
    model_refs = refs[: len(blocks)]
    along_z_ref, along_y_ref, own_now, own_before, from_a, from_b = refs[len(blocks) : len(blocks) + 6]
    slopes_ref, courant_ref, stored_ref, end_ref, gain_ref, log_buf, now, before = refs[len(blocks) + 6 :]
    tile, own, left, right, side_a, side_b = layout(aperture_ref, cx)
    shot = lax.axis_index("shot")
    sides = ((cx, None), (side_a[0], side_a[1]), (side_b[0], side_b[1]))
    block_rows = ny // shots
    size = cx * block_rows

    @pl.when(jnp.logical_not(own))
    def _():
        end_ref[...] = jnp.zeros_like(end_ref)

    @pl.when(own)
    def _():
        for ref, held in zip(model_refs, blocks):
            for number, (mask, place) in enumerate(held):
                y0 = pl.multiple_of((shot ^ mask) * block_rows, block_rows)
                at, here = sides[place]
                base = number * 2 * size
                speed = ref[pl.ds(base, size), :].astype(jnp.float32)
                courant = (speed * speed) * (1.0 / SCALE)
                courant_ref[pl.ds(at, cx), pl.ds(y0, block_rows), :] = courant.reshape(cx, block_rows, nz)
                if here is None:
                    gain = speed * (2.0 / SCALE)
                    gain_ref[:, pl.ds(y0, block_rows), :] = gain.reshape(cx, block_rows, nz)
                logs = jnp.log(ref[pl.ds(base + size, size), :].astype(jnp.float32))
                if here is not None:
                    logs = jnp.where(here, logs, 0.0)
                log_buf[pl.ds(at, cx), pl.ds(y0, block_rows), :] = logs.reshape(cx, block_rows, nz)
        fill_fields(now, before, own_now, own_before, from_a, from_b, side_a, side_b, cx, ny, nz)
        along_z, along_y = along_z_ref[...], along_y_ref[...]

        def slopes(i0, layers, inner):
            first_y, first_z, _ = matrix_differences(
                log_buf, i0, layers, along_z, along_y
            )
            for j in range(layers):
                slopes_ref[0, i0 + j] = layer_differences(log_buf, i0 + j, None)[0] * (1.0 / 140.0)
                slopes_ref[1, i0 + j] = first_y[j] * (1.0 / 140.0)
                slopes_ref[2, i0 + j] = first_z[j] * (1.0 / 140.0)

        on_segments(0, left, right, cx, slopes)

        cell = source_ref[0]
        layer = cell // (ny * nz) - (tile - 1) * cx
        row = lax.rem(cell // nz, ny)
        depth = lax.rem(cell, nz)
        lanes = lax.broadcasted_iota(jnp.int32, (1, nz), 1)
        bufs = (now, before)
        for step in range(STEPS):
            cur, prev = bufs[step % 2], bufs[(step + 1) % 2]

            def work(i0, layers, inner, cur=cur, prev=prev, step=step):
                def use(i, j, applied, updated):
                    if inner:
                        stored_ref[step, j] = applied
                    return updated

                march(cur, prev, slopes_ref, courant_ref, along_z, along_y, i0, layers, use)

            on_segments(step, left, right, cx, work)
            reach = (STEPS - 1 - step) * HALO
            low = jnp.where(left, cx - reach, cx)
            high = jnp.where(right, 2 * cx + reach, 2 * cx)
            value = wavelet_ref[0, step]

            @pl.when((layer >= low) & (layer < high))
            def _(prev=prev, value=value):
                old = prev[layer, pl.ds(row, 1), :]
                prev[layer, pl.ds(row, 1), :] = old + jnp.where(lanes == depth, value, 0.0)

            if step == 0:
                clear_sides(cur, left, right, cx)
        end_ref[...] = bufs[STEPS % 2][cx : 2 * cx].reshape(cx * ny, nz)


def adjoint_kernel(
    cx, ny, nz, order, aperture_ref, gain_ref, along_z_ref, along_y_ref, slopes_ref, courant_ref, stored_ref, add_ref, own_now,
    own_before, from_a, from_b, sums_ref, start_ref, now, before, image,
):
    tile, own, left, right, side_a, side_b = layout(aperture_ref, cx)
    shot = lax.axis_index("shot")
    block_rows = ny // len(order)

    @pl.when(jnp.logical_not(own))
    def _():
        start_ref[...] = jnp.zeros_like(start_ref)
        sums_ref[...] = jnp.zeros_like(sums_ref)

    @pl.when(own)
    def _():
        fill_fields(now, before, own_now, own_before, from_a, from_b, side_a, side_b, cx, ny, nz)
        along_z, along_y = along_z_ref[...], along_y_ref[...]
        bufs = (now, before)
        for step in range(STEPS):
            cur, prev = bufs[step % 2], bufs[(step + 1) % 2]

            def work(i0, layers, inner, cur=cur, prev=prev, step=step):
                def use(i, j, applied, updated):
                    updated = updated + add_ref[step, i - (cx - (STEPS - 1) * HALO)]
                    if inner:
                        term = updated * stored_ref[STEPS - 1 - step, j]
                        image[j] = term if step == 0 else image[j] + term
                    return updated

                march(cur, prev, slopes_ref, courant_ref, along_z, along_y, i0, layers, use)

            on_segments(step, left, right, cx, work)
            if step == 0:
                clear_sides(cur, left, right, cx)
        start_ref[...] = bufs[STEPS % 2][cx : 2 * cx].reshape(cx * ny, nz)
        for place, mask in enumerate(order):
            y0 = pl.multiple_of((shot ^ mask) * block_rows, block_rows)
            gain = gain_ref[:, pl.ds(y0, block_rows), :]
            sums_ref[place] = (gain * image[:, pl.ds(y0, block_rows), :]).reshape(cx * block_rows, nz)


def pairs(axis_sizes, kind):
    tiles, shots = axis_sizes
    found = []
    for tile in range(tiles):
        other = tile ^ 1 if kind == "a" else ((tile + 1) ^ 1) - 1
        for shot in range(shots):
            here = tile * shots + shot
            if 0 <= other < tiles:
                found.append((here, other * shots + shot))
            elif shots % 2 == 0:
                found.append((here, tile * shots + (shot ^ 1)))
    return found


def local(
    velocity, density, wave_now, wave_before, adjoint_end, adjoint_after, source_cell, source_wave, receiver_cell, residual_traces,
    aperture,
):
    cx, _, nz = velocity.shape
    ny = wave_now.shape[2]
    shots = lax.axis_size("shot")
    tiles = lax.axis_size("tile")
    rows = cx * ny
    params = pltpu.CompilerParams(vmem_limit_bytes=VMEM_BYTES)

    def swap(x, kind):
        return lax.ppermute(x, ("tile", "shot"), pairs((tiles, shots), kind))

    def cross(x, mask):
        return lax.ppermute(x, "shot", [(i, i ^ mask) for i in range(shots)])

    model = jnp.concatenate([velocity.reshape(-1, nz), density.reshape(-1, nz)], axis=0)
    model_a, model_b = swap(model, "a"), swap(model, "b")
    forward = jnp.concatenate([wave_now.reshape(rows, nz), wave_before.reshape(rows, nz)], axis=0)
    high = shots // 2
    near = [([(0, 0)], model), ([(0, 1)], model_a), ([(0, 2)], model_b)]
    late = []
    if high:
        model_c = cross(model, high)
        forward_a, forward_b = swap(forward, "a"), swap(forward, "b")
        near.append(([(high, 0)], model_c))
        late.append(([(high, 1), (high, 2)], cross(jnp.concatenate([model_a, model_b], axis=0), high)))
    else:
        forward_a, forward_b = swap(forward, "a"), swap(forward, "b")
    mask = high // 2
    adjoint = jnp.concatenate([adjoint_end.reshape(rows, nz), adjoint_after.reshape(rows, nz)], axis=0)
    adjoint_a, adjoint_b = swap(adjoint, "a"), swap(adjoint, "b")

    along_z, along_y, added, joined = pl.pallas_call(
        lambda *refs: setup_kernel(cx, *refs),
        out_shape=(
            jax.ShapeDtypeStruct((2 * nz, 2 * nz), jnp.bfloat16),
            jax.ShapeDtypeStruct((2 * HALO * ny, HALO * ny), jnp.bfloat16),
            jax.ShapeDtypeStruct((STEPS, cx + 2 * (STEPS - 1) * HALO, ny, nz), jnp.float32),
            jax.ShapeDtypeStruct((len(near) * model.shape[0], nz), jnp.bfloat16),
        ),
        in_specs=[vmem()] * (2 + len(near)),
        out_specs=(vmem(),) * 4,
        compiler_params=params,
        cost_estimate=pl.CostEstimate(flops=2 * 10**9, bytes_accessed=4 * 2**20, transcendentals=0),
        name="receivers",
    )(receiver_cell, residual_traces, *[block for _, block in near])

    near = [([name for names, _ in near for name in names], joined)]
    while mask:
        moved = []
        for group in (near, late):
            names = [(m ^ mask, place) for held, _ in group for m, place in held]
            array = group[0][1] if len(group) == 1 else jnp.concatenate([block for _, block in group], axis=0)
            moved.append((names, cross(array, mask)))
        near, late = near + moved[:1], late + moved[1:]
        mask //= 2
    held = near + late

    field = pltpu.VMEM((3 * cx, ny, nz), jnp.float32)
    blocks = tuple(tuple(names) for names, _ in held)
    slopes, courant, stored, wave_end, gain = pl.pallas_call(
        lambda *refs: forward_kernel(cx, ny, nz, shots, blocks, *refs),
        out_shape=(
            jax.ShapeDtypeStruct((3, 3 * cx, ny, nz), jnp.float32),
            jax.ShapeDtypeStruct((3 * cx, ny, nz), jnp.float32),
            jax.ShapeDtypeStruct((STEPS, cx, ny, nz), jnp.float32),
            jax.ShapeDtypeStruct((rows, nz), jnp.float32),
            jax.ShapeDtypeStruct((cx, ny, nz), jnp.float32),
        ),
        in_specs=[smem()] * 3 + [vmem()] * (len(held) + 6),
        out_specs=(vmem(),) * 5,
        scratch_shapes=[field, field, field],
        compiler_params=params,
        cost_estimate=pl.CostEstimate(flops=5 * 10**9, bytes_accessed=8 * 2**20, transcendentals=0),
        name="forward",
    )(
        aperture, source_cell, source_wave, *[block for _, block in held], along_z, along_y,
        wave_now.reshape(rows, nz), wave_before.reshape(rows, nz), forward_a, forward_b,
    )

    bits = []
    mask = 1
    while mask < shots:
        bits.append(mask)
        mask *= 2
    sum_order = [0]
    for bit in reversed(bits):
        sum_order = sum_order + [m | bit for m in sum_order]
    sum_order = tuple(sum_order)
    block = cx * (ny // shots)
    sums, adjoint_start = pl.pallas_call(
        lambda *refs: adjoint_kernel(cx, ny, nz, sum_order, *refs),
        out_shape=(
            jax.ShapeDtypeStruct((shots, block, nz), jnp.float32),
            jax.ShapeDtypeStruct((rows, nz), jnp.float32),
        ),
        in_specs=[smem()] + [vmem()] * 11,
        out_specs=(vmem(),) * 2,
        scratch_shapes=[field, field, pltpu.VMEM((cx, ny, nz), jnp.float32)],
        compiler_params=params,
        cost_estimate=pl.CostEstimate(flops=5 * 10**9, bytes_accessed=8 * 2**20, transcendentals=0),
        name="adjoint",
    )(
        aperture, gain, along_z, along_y, slopes, courant, stored, added, adjoint_end.reshape(rows, nz), adjoint_after.reshape(rows, nz),
        adjoint_a, adjoint_b,
    )
    for bit in bits:
        half = sums.shape[0] // 2
        sums = sums[:half] + cross(sums[half:], bit)
    gradient = sums[0].reshape(cx, ny // shots, nz)
    ends = [x.astype(jnp.bfloat16).reshape(wave_now.shape) for x in (wave_end, adjoint_start)]
    return gradient, ends[0], ends[1]


def solution(mesh):
    stored = P(("parts", "tile"), "shot", None)
    field = P(("parts", "shot"), "tile", None, None)
    return jax.shard_map(
        local,
        mesh=mesh,
        in_specs=(
            stored, stored, field, field, field, field, P(("parts", "shot")), P(("parts", "shot"), None),
            P(("parts", "shot"), None), P(("parts", "shot"), None, None), P(("parts", "shot"), None),
        ),
        out_specs=(stored, field, field),
        check_vma=False,
    )
```

```python
import jax
import jax.numpy as jnp
from jax import lax
from jax.experimental import pallas as pl
from jax.experimental.pallas import tpu as pltpu
from jax.sharding import PartitionSpec as P

FIRST = (672.0, -168.0, 32.0, -3.0)
SECOND = (8064.0, -1008.0, 128.0, -9.0)
CENTRE_Z = -43008.0
CENTRE_Y = -42.0
SCALE = 5040.0
STEPS = 4
PACK_BYTES = 56 * 1024 * 1024
HALO = 4
VMEM_BYTES = 24 * 1024 * 1024


def vmem():
    return pl.BlockSpec(memory_space=pltpu.VMEM)


def smem():
    return pl.BlockSpec(memory_space=pltpu.SMEM)


def two_terms(values):
    high = values.astype(jnp.bfloat16)
    low = (values - high.astype(jnp.float32)).astype(jnp.bfloat16)
    return high, low


def is_active(aperture_ref, tile):
    found = aperture_ref[0, 0] == tile
    for slot in range(1, aperture_ref.shape[1]):
        found = found | (aperture_ref[0, slot] == tile)
    return found & (tile >= 0)


def layout(aperture_ref, cx):
    tiles = lax.axis_size("tile")
    tile = lax.axis_index("tile")
    even = lax.rem(tile, 2) == 0
    left = is_active(aperture_ref, tile - 1) & (tile > 0)
    right = is_active(aperture_ref, tile + 1) & (tile < tiles - 1)
    own = is_active(aperture_ref, tile)
    a_tile = jnp.where(even, tile + 1, tile - 1)
    b_tile = jnp.where(even, tile - 1, tile + 1)
    a_at = jnp.where(even, 2 * cx, 0)
    b_at = jnp.where(even, 0, 2 * cx)
    a_here = (a_tile >= 0) & (a_tile < tiles)
    b_here = (b_tile >= 0) & (b_tile < tiles)
    a_on = jnp.where(even, right, left)
    b_on = jnp.where(even, left, right)
    return tile, own, left, right, (a_at, a_here, a_on), (b_at, b_here, b_on)


def difference_matrix(shape, along, across, block, centre):
    ahead = lax.rem(along, block) - lax.rem(across, block)
    first = jnp.zeros(shape, jnp.float32)
    second = jnp.where(ahead == 0, centre, 0.0)
    for k in range(1, 5):
        first = jnp.where(ahead == k, FIRST[k - 1], jnp.where(ahead == -k, -FIRST[k - 1], first))
        second = jnp.where((ahead == k) | (ahead == -k), SECOND[k - 1], second)
    return first, second


def pack_kernel(*refs):
    velocity_ref, density_ref, now_ref, before_ref, end_ref, after_ref, model_ref, a_ref, b_ref, sems = refs
    cx = velocity_ref.shape[0]
    even = lax.rem(lax.axis_index("tile"), 2) == 0
    reach = (STEPS - 1) * HALO
    moves = [(velocity_ref, model_ref.at[0:cx]), (density_ref, model_ref.at[cx : 2 * cx])]
    for side, out_ref in enumerate((a_ref, b_ref)):
        first = jnp.where(even == (side == 0), cx - reach, 0)
        base = 0
        for whole_ref, part_ref in ((now_ref, before_ref), (end_ref, after_ref)):
            moves.append((whole_ref.at[0], out_ref.at[base : base + cx]))
            moves.append((part_ref.at[0, pl.ds(first, reach)], out_ref.at[base + cx : base + cx + reach]))
            base += cx + reach
    copies = [pltpu.make_async_copy(src, dst, sems.at[number]) for number, (src, dst) in enumerate(moves)]
    for copy in copies:
        copy.start()
    for copy in copies:
        copy.wait()


def setup_kernel(cx, cells_ref, traces_ref, *refs):
    parts, (along_z_ref, along_y_ref, add_ref, joined_ref) = refs[:-4], refs[-4:]
    ny, nz = add_ref.shape[2:]
    size = parts[0].shape[0]
    for number, part in enumerate(parts):
        joined_ref[number * size : (number + 1) * size, :] = part[...]

    shape = along_z_ref.shape
    rows, cols = (lax.broadcasted_iota(jnp.int32, shape, d) for d in range(2))
    first, second = difference_matrix(shape, rows, cols, nz, CENTRE_Z)
    along_z_ref[...] = jnp.where(cols < nz, first, second).astype(jnp.bfloat16)
    shape = along_y_ref.shape
    rows, cols = (lax.broadcasted_iota(jnp.int32, shape, d) for d in range(2))
    first, second = difference_matrix(shape, cols, rows, ny, CENTRE_Y)
    here = lax.rem(rows, shape[1]) // ny == cols // ny
    along_y_ref[...] = jnp.where(here, jnp.where(rows < shape[1], first, second), 0.0).astype(jnp.bfloat16)

    tile = lax.axis_index("tile")
    count = cells_ref.shape[1]
    cells = cells_ref[...]
    reach = (STEPS - 1) * HALO
    at_row = cells // nz - (tile * cx - reach) * ny
    at_z = lax.rem(cells, nz)
    depth = lax.broadcasted_iota(jnp.int32, (nz, count), 0)
    deep = depth == at_z
    tile = lax.axis_index("tile")
    count = cells_ref.shape[1]
    cells = cells_ref[...]
    reach = (STEPS - 1) * HALO
    at_row = cells // nz - (tile * cx - reach) * ny
    at_z = lax.rem(cells, nz)
    depth = lax.broadcasted_iota(jnp.int32, (nz, count), 0)
    deep = depth == at_z
    values = []
    for step in range(STEPS):
        trace = traces_ref[0, pl.ds(STEPS - 1 - step, 1), :]
        high = trace.astype(jnp.bfloat16).astype(jnp.float32)
        values += [jnp.where(deep, high, 0.0), jnp.where(deep, trace - high, 0.0)]
    values = jnp.concatenate(values, axis=0).astype(jnp.bfloat16)
    chunk = 2 * HALO
    row = lax.broadcasted_iota(jnp.int32, (chunk * ny, count), 0)

    def body(c, carry):
        hot = jnp.where(at_row == row + c * (chunk * ny), 1.0, 0.0).astype(jnp.bfloat16)
        found = lax.dot_general(hot, values, (((1,), (1,)), ((), ())), preferred_element_type=jnp.float32)
        for step in range(STEPS):
            both = found[:, 2 * step * nz : (2 * step + 1) * nz] + found[:, (2 * step + 1) * nz : (2 * step + 2) * nz]
            add_ref[step, pl.ds(c * chunk, chunk)] = both.reshape(chunk, ny, nz)
        return carry

    lax.fori_loop(0, (cx + 2 * reach) // chunk, body, 0)


def matrix_differences(buf, i0, layers, along_z, along_y):
    ny, nz = buf.shape[1:]
    both = jnp.concatenate(two_terms(buf[pl.ds(i0, layers)].reshape(layers * ny, nz)), axis=1)
    from_z = jnp.dot(both, along_z, preferred_element_type=jnp.float32)
    size = along_y.shape[1]
    half = along_y.shape[0] // 2
    first_y, second = [], []
    for base in range(0, layers * ny, size):
        from_y = jnp.dot(along_y, both[base : base + size], preferred_element_type=jnp.float32)
        first_y.append(from_y[:size, :nz] + from_y[:size, nz:])
        if half == size:
            second.append(from_y[size:, :nz] + from_y[size:, nz:] + from_z[base : base + size, nz:])
    shape = (layers, ny, nz)
    first_y, first_z = jnp.concatenate(first_y, axis=0), from_z[:, :nz]
    if not second:
        return first_y.reshape(shape), first_z.reshape(shape), None
    return first_y.reshape(shape), first_z.reshape(shape), jnp.concatenate(second, axis=0).reshape(shape)


def layer_differences(buf, i, summed):
    first = None
    for k in range(1, 5):
        plus, minus = buf[i + k], buf[i - k]
        if summed is not None:
            summed = summed + SECOND[k - 1] * (plus + minus)
        term = FIRST[k - 1] * (plus - minus)
        first = term if first is None else first + term
    return first, summed


def on_segments(step, left, right, cx, work):
    work(cx, cx, True)
    reach = (STEPS - 1 - step) * HALO
    if reach:

        def body(number, carry):
            base = jnp.where(left & (number == 0), cx - reach, 2 * cx)
            work(pl.multiple_of(base, HALO), reach, False)
            return carry

        lax.fori_loop(0, left.astype(jnp.int32) + right.astype(jnp.int32), body, 0)


def march(cur, prev, slopes_ref, courant_ref, along_z, along_y, i0, layers, use):
    first_y, first_z, second = matrix_differences(cur, i0, layers, along_z, along_y)
    for j in range(layers):
        i = i0 + j
        first_x, applied = layer_differences(cur, i, second[j])
        applied = applied - slopes_ref[0, i] * first_x - slopes_ref[1, i] * first_y[j] - slopes_ref[2, i] * first_z[j]
        prev[i] = use(i, j, applied, 2.0 * cur[i] - prev[i] + courant_ref[i] * applied)


def fill(buf, at, rows_ref, first_row, layers, keep):
    ny, nz = buf.shape[1:]
    part = rows_ref[pl.ds(first_row, layers * ny), :].astype(jnp.float32)
    if keep is not None:
        part = jnp.where(keep, part, 0.0)
    buf[pl.ds(at, layers)] = part.reshape(layers, ny, nz)


def fill_fields(now, before, own_now, own_before, from_a, from_b, base, side_a, side_b, cx, ny):
    fill(now, cx, own_now, 0, cx, None)
    fill(before, cx, own_before, 0, cx, None)
    reach = (STEPS - 1) * HALO
    for ref, (at, here, on) in ((from_a, side_a), (from_b, side_b)):
        fill(now, at, ref, base, cx, here)
        fill(before, jnp.where(at == 0, cx - reach, at), ref, base + cx * ny, reach, on)


def clear_sides(buf, left, right, cx):
    zero = jnp.zeros((HALO,) + buf.shape[1:], jnp.float32)

    @pl.when(jnp.logical_not(left))
    def _():
        buf[cx - HALO : cx] = zero

    @pl.when(jnp.logical_not(right))
    def _():
        buf[2 * cx : 2 * cx + HALO] = zero


def model_kernel(cx, ny, nz, shots, blocks, aperture_ref, *refs):
    model_refs = refs[: len(blocks)]
    along_z_ref, along_y_ref, slopes_ref, courant_ref, gain_ref, log_buf = refs[len(blocks) :]
    tile, own, left, right, side_a, side_b = layout(aperture_ref, cx)
    shot = lax.axis_index("shot")
    sides = ((cx, None), (side_a[0], side_a[1]), (side_b[0], side_b[1]))
    block_rows = ny // shots
    size = cx * block_rows

    @pl.when(own)
    def _():
        for ref, held in zip(model_refs, blocks):
            for number, (mask, place) in enumerate(held):
                y0 = pl.multiple_of((shot ^ mask) * block_rows, block_rows)
                at, here = sides[place]
                base = number * 2 * size
                speed = ref[pl.ds(base, size), :].astype(jnp.float32)
                courant = (speed * speed) * (1.0 / SCALE)
                courant_ref[pl.ds(at, cx), pl.ds(y0, block_rows), :] = courant.reshape(cx, block_rows, nz)
                if here is None:
                    gain = speed * (2.0 / SCALE)
                    gain_ref[:, pl.ds(y0, block_rows), :] = gain.reshape(cx, block_rows, nz)
                logs = jnp.log(ref[pl.ds(base + size, size), :].astype(jnp.float32))
                if here is not None:
                    logs = jnp.where(here, logs, 0.0)
                log_buf[pl.ds(at, cx), pl.ds(y0, block_rows), :] = logs.reshape(cx, block_rows, nz)
        along_z, along_y = along_z_ref[...], along_y_ref[...]

        def slopes(i0, layers, inner):
            first_y, first_z, _ = matrix_differences(log_buf, i0, layers, along_z, along_y)
            for j in range(layers):
                slopes_ref[0, i0 + j] = layer_differences(log_buf, i0 + j, None)[0] * (1.0 / 140.0)
                slopes_ref[1, i0 + j] = first_y[j] * (1.0 / 140.0)
                slopes_ref[2, i0 + j] = first_z[j] * (1.0 / 140.0)

        on_segments(0, left, right, cx, slopes)


def window_kernel(
    cx, ny, nz, order, aperture_ref, source_ref, wavelet_ref, along_z_ref, along_y_ref, slopes_ref, courant_ref, gain_ref, add_ref,
    now_ref, before_ref, end_ref, after_ref, from_a, from_b, sums_ref, wave_ref, adjoint_ref, now, before, end, after, stored, image,
):
    tile, own, left, right, side_a, side_b = layout(aperture_ref, cx)
    shot = lax.axis_index("shot")
    block_rows = ny // len(order)

    @pl.when(jnp.logical_not(own))
    def _():
        wave_ref[...] = jnp.zeros_like(wave_ref)
        adjoint_ref[...] = jnp.zeros_like(adjoint_ref)
        sums_ref[...] = jnp.zeros_like(sums_ref)

    @pl.when(own)
    def _():
        half = from_a.shape[0] // 2
        fill_fields(now, before, now_ref, before_ref, from_a, from_b, 0, side_a, side_b, cx, ny)
        fill_fields(end, after, end_ref, after_ref, from_a, from_b, half, side_a, side_b, cx, ny)
        along_z, along_y = along_z_ref[...], along_y_ref[...]
        cell = source_ref[0]
        layer = cell // (ny * nz) - (tile - 1) * cx
        row = lax.rem(cell // nz, ny)
        depth = lax.rem(cell, nz)
        lanes = lax.broadcasted_iota(jnp.int32, (1, nz), 1)
        bufs = (now, before)
        for step in range(STEPS):
            cur, prev = bufs[step % 2], bufs[(step + 1) % 2]

            def work(i0, layers, inner, cur=cur, prev=prev, step=step):
                def use(i, j, applied, updated):
                    if inner:
                        stored[step, j] = applied
                    return updated

                march(cur, prev, slopes_ref, courant_ref, along_z, along_y, i0, layers, use)

            on_segments(step, left, right, cx, work)
            reach = (STEPS - 1 - step) * HALO
            low = jnp.where(left, cx - reach, cx)
            high = jnp.where(right, 2 * cx + reach, 2 * cx)
            value = wavelet_ref[0, step]

            @pl.when((layer >= low) & (layer < high))
            def _(prev=prev, value=value):
                old = prev[layer, pl.ds(row, 1), :]
                prev[layer, pl.ds(row, 1), :] = old + jnp.where(lanes == depth, value, 0.0)

            if step == 0:
                clear_sides(cur, left, right, cx)
        wave_ref[...] = bufs[STEPS % 2][cx : 2 * cx].reshape(cx * ny, nz)

        bufs = (end, after)
        for step in range(STEPS):
            cur, prev = bufs[step % 2], bufs[(step + 1) % 2]

            def work(i0, layers, inner, cur=cur, prev=prev, step=step):
                def use(i, j, applied, updated):
                    updated = updated + add_ref[step, i - (cx - (STEPS - 1) * HALO)]
                    if inner:
                        term = updated * stored[STEPS - 1 - step, j]
                        image[j] = term if step == 0 else image[j] + term
                    return updated

                march(cur, prev, slopes_ref, courant_ref, along_z, along_y, i0, layers, use)

            on_segments(step, left, right, cx, work)
            if step == 0:
                clear_sides(cur, left, right, cx)
        adjoint_ref[...] = bufs[STEPS % 2][cx : 2 * cx].reshape(cx * ny, nz)
        for place, mask in enumerate(order):
            y0 = pl.multiple_of((shot ^ mask) * block_rows, block_rows)
            gain = gain_ref[:, pl.ds(y0, block_rows), :]
            sums_ref[place] = (gain * image[:, pl.ds(y0, block_rows), :]).reshape(cx * block_rows, nz)


def pairs(axis_sizes, kind):
    tiles, shots = axis_sizes
    found = []
    for tile in range(tiles):
        other = tile ^ 1 if kind == "a" else ((tile + 1) ^ 1) - 1
        for shot in range(shots):
            here = tile * shots + shot
            if 0 <= other < tiles:
                found.append((here, other * shots + shot))
            elif shots % 2 == 0:
                found.append((here, tile * shots + (shot ^ 1)))
    return found


def local(
    velocity, density, wave_now, wave_before, adjoint_end, adjoint_after, source_cell, source_wave, receiver_cell, residual_traces,
    aperture,
):
    cx, _, nz = velocity.shape
    ny = wave_now.shape[2]
    shots = lax.axis_size("shot")
    tiles = lax.axis_size("tile")
    rows = cx * ny
    params = pltpu.CompilerParams(vmem_limit_bytes=VMEM_BYTES)

    def swap(x, kind):
        return lax.ppermute(x, ("tile", "shot"), pairs((tiles, shots), kind))

    def cross(x, mask):
        return lax.ppermute(x, "shot", [(i, i ^ mask) for i in range(shots)])

    fields = [x.reshape(rows, nz) for x in (wave_now, wave_before, adjoint_end, adjoint_after)]
    message = jax.ShapeDtypeStruct((2 * (cx + (STEPS - 1) * HALO), ny, nz), jnp.bfloat16)
    model, to_a, to_b = pl.pallas_call(
        pack_kernel,
        out_shape=(jax.ShapeDtypeStruct((2 * cx,) + velocity.shape[1:], jnp.bfloat16), message, message),
        in_specs=[pl.BlockSpec(memory_space=pltpu.HBM)] * 6,
        out_specs=(pl.BlockSpec(memory_space=pltpu.HBM),) * 3,
        scratch_shapes=[pltpu.SemaphoreType.DMA((10,))],
        compiler_params=pltpu.CompilerParams(vmem_limit_bytes=PACK_BYTES),
        cost_estimate=pl.CostEstimate(flops=0, bytes_accessed=2 * 2**20, transcendentals=0),
        name="pack",
    )(velocity, density, wave_now, wave_before, adjoint_end, adjoint_after)
    model, to_a, to_b = (x.reshape(-1, nz) for x in (model, to_a, to_b))

    model_a, model_b = swap(model, "a"), swap(model, "b")
    high = shots // 2
    near = [([(0, 0)], model), ([(0, 1)], model_a), ([(0, 2)], model_b)]
    late = []
    if high:
        near.append(([(high, 0)], cross(model, high)))
        late.append(([(high, 1), (high, 2)], cross(jnp.concatenate([model_a, model_b], axis=0), high)))
    from_a, from_b = swap(to_a, "a"), swap(to_b, "b")

    along_z, along_y, added, joined = pl.pallas_call(
        lambda *refs: setup_kernel(cx, *refs),
        out_shape=(
            jax.ShapeDtypeStruct((2 * nz, 2 * nz), jnp.bfloat16),
            jax.ShapeDtypeStruct((2 * HALO * ny, HALO * ny), jnp.bfloat16),
            jax.ShapeDtypeStruct((STEPS, cx + 2 * (STEPS - 1) * HALO, ny, nz), jnp.float32),
            jax.ShapeDtypeStruct((len(near) * model.shape[0], nz), jnp.bfloat16),
        ),
        in_specs=[vmem()] * (2 + len(near)),
        out_specs=(vmem(),) * 4,
        compiler_params=params,
        cost_estimate=pl.CostEstimate(flops=2 * 10**9, bytes_accessed=4 * 2**20, transcendentals=0),
        name="receivers",
    )(receiver_cell, residual_traces, *[block for _, block in near])

    near = [([name for names, _ in near for name in names], joined)]
    mask = high // 2
    while mask:
        moved = []
        for group in (near, late):
            names = [(m ^ mask, place) for held, _ in group for m, place in held]
            array = group[0][1] if len(group) == 1 else jnp.concatenate([block for _, block in group], axis=0)
            moved.append((names, cross(array, mask)))
        near, late = near + moved[:1], late + moved[1:]
        mask //= 2
    held = near + late

    field = pltpu.VMEM((3 * cx, ny, nz), jnp.float32)
    blocks = tuple(tuple(names) for names, _ in held)
    slopes, courant, gain = pl.pallas_call(
        lambda *refs: model_kernel(cx, ny, nz, shots, blocks, *refs),
        out_shape=(
            jax.ShapeDtypeStruct((3, 3 * cx, ny, nz), jnp.float32),
            jax.ShapeDtypeStruct((3 * cx, ny, nz), jnp.float32),
            jax.ShapeDtypeStruct((cx, ny, nz), jnp.float32),
        ),
        in_specs=[smem()] + [vmem()] * (len(held) + 2),
        out_specs=(vmem(),) * 3,
        scratch_shapes=[field],
        compiler_params=params,
        cost_estimate=pl.CostEstimate(flops=10**6, bytes_accessed=2**20, transcendentals=0),
        name="model",
    )(aperture, *[block for _, block in held], along_z, along_y)

    bits = []
    mask = 1
    while mask < shots:
        bits.append(mask)
        mask *= 2
    order = [0]
    for bit in reversed(bits):
        order = order + [m | bit for m in order]
    order = tuple(order)
    sums, wave_end, adjoint_start = pl.pallas_call(
        lambda *refs: window_kernel(cx, ny, nz, order, *refs),
        out_shape=(
            jax.ShapeDtypeStruct((shots, cx * (ny // shots), nz), jnp.float32),
            jax.ShapeDtypeStruct((rows, nz), jnp.float32),
            jax.ShapeDtypeStruct((rows, nz), jnp.float32),
        ),
        in_specs=[smem()] * 3 + [vmem()] * 12,
        out_specs=(vmem(),) * 3,
        scratch_shapes=[field] * 4 + [pltpu.VMEM((STEPS, cx, ny, nz), jnp.float32), pltpu.VMEM((cx, ny, nz), jnp.float32)],
        compiler_params=params,
        cost_estimate=pl.CostEstimate(flops=10**10, bytes_accessed=16 * 2**20, transcendentals=0),
        name="window",
    )(aperture, source_cell, source_wave, along_z, along_y, slopes, courant, gain, added, *fields, from_a, from_b)
    for bit in bits:
        half = sums.shape[0] // 2
        sums = sums[:half] + cross(sums[half:], bit)
    gradient = sums[0].reshape(cx, ny // shots, nz)
    ends = [x.astype(jnp.bfloat16).reshape(wave_now.shape) for x in (wave_end, adjoint_start)]
    return gradient, ends[0], ends[1]


def solution(mesh):
    stored = P(("parts", "tile"), "shot", None)
    field = P(("parts", "shot"), "tile", None, None)
    return jax.shard_map(
        local,
        mesh=mesh,
        in_specs=(
            stored, stored, field, field, field, field, P(("parts", "shot")), P(("parts", "shot"), None),
            P(("parts", "shot"), None), P(("parts", "shot"), None, None), P(("parts", "shot"), None),
        ),
        out_specs=(stored, field, field),
        check_vma=False,
    )
```

```python
import jax
import jax.numpy as jnp
from jax import lax
from jax.experimental import pallas as pl
from jax.experimental.pallas import tpu as pltpu
from jax.sharding import PartitionSpec as P

FIRST = (672.0, -168.0, 32.0, -3.0)
SECOND = (8064.0, -1008.0, 128.0, -9.0)
CENTRE_Z = -43008.0
CENTRE_Y = -42.0
SCALE = 5040.0
STEPS = 4
PACK_BYTES = 56 * 1024 * 1024
HALO = 4
VMEM_BYTES = 24 * 1024 * 1024


def vmem():
    return pl.BlockSpec(memory_space=pltpu.VMEM)


def smem():
    return pl.BlockSpec(memory_space=pltpu.SMEM)


def two_terms(values):
    high = values.astype(jnp.bfloat16)
    low = (values - high.astype(jnp.float32)).astype(jnp.bfloat16)
    return high, low


def is_active(aperture_ref, tile):
    found = aperture_ref[0, 0] == tile
    for slot in range(1, aperture_ref.shape[1]):
        found = found | (aperture_ref[0, slot] == tile)
    return found & (tile >= 0)


def layout(aperture_ref, cx):
    tiles = lax.axis_size("tile")
    tile = lax.axis_index("tile")
    even = lax.rem(tile, 2) == 0
    left = is_active(aperture_ref, tile - 1) & (tile > 0)
    right = is_active(aperture_ref, tile + 1) & (tile < tiles - 1)
    own = is_active(aperture_ref, tile)
    a_tile = jnp.where(even, tile + 1, tile - 1)
    b_tile = jnp.where(even, tile - 1, tile + 1)
    a_at = jnp.where(even, 2 * cx, 0)
    b_at = jnp.where(even, 0, 2 * cx)
    a_here = (a_tile >= 0) & (a_tile < tiles)
    b_here = (b_tile >= 0) & (b_tile < tiles)
    a_on = jnp.where(even, right, left)
    b_on = jnp.where(even, left, right)
    return tile, own, left, right, (a_at, a_here, a_on), (b_at, b_here, b_on)


def difference_matrix(shape, along, across, block, centre):
    ahead = lax.rem(along, block) - lax.rem(across, block)
    first = jnp.zeros(shape, jnp.float32)
    second = jnp.where(ahead == 0, centre, 0.0)
    for k in range(1, 5):
        first = jnp.where(ahead == k, FIRST[k - 1], jnp.where(ahead == -k, -FIRST[k - 1], first))
        second = jnp.where((ahead == k) | (ahead == -k), SECOND[k - 1], second)
    return first, second


def pack_kernel(*refs):
    velocity_ref, density_ref, now_ref, before_ref, end_ref, after_ref, model_ref, a_ref, b_ref, sems = refs
    cx = velocity_ref.shape[0]
    even = lax.rem(lax.axis_index("tile"), 2) == 0
    reach = (STEPS - 1) * HALO
    moves = [(velocity_ref, model_ref.at[0:cx]), (density_ref, model_ref.at[cx : 2 * cx])]
    for side, out_ref in enumerate((a_ref, b_ref)):
        first = jnp.where(even == (side == 0), cx - reach, 0)
        base = 0
        for whole_ref, part_ref in ((now_ref, before_ref), (end_ref, after_ref)):
            moves.append((whole_ref.at[0], out_ref.at[base : base + cx]))
            moves.append((part_ref.at[0, pl.ds(first, reach)], out_ref.at[base + cx : base + cx + reach]))
            base += cx + reach
    copies = [pltpu.make_async_copy(src, dst, sems.at[number]) for number, (src, dst) in enumerate(moves)]
    for copy in copies:
        copy.start()
    for copy in copies:
        copy.wait()


def setup_kernel(cx, cells_ref, traces_ref, *refs):
    parts, (along_z_ref, along_y_ref, add_ref, joined_ref) = refs[:-4], refs[-4:]
    ny, nz = add_ref.shape[2:]
    size = parts[0].shape[0]
    for number, part in enumerate(parts):
        joined_ref[number * size : (number + 1) * size, :] = part[...]

    shape = along_z_ref.shape
    rows, cols = (lax.broadcasted_iota(jnp.int32, shape, d) for d in range(2))
    first, second = difference_matrix(shape, rows, cols, nz, CENTRE_Z)
    along_z_ref[...] = jnp.where(cols < nz, first, second).astype(jnp.bfloat16)
    shape = along_y_ref.shape
    rows, cols = (lax.broadcasted_iota(jnp.int32, shape, d) for d in range(2))
    first, second = difference_matrix(shape, cols, rows, ny, CENTRE_Y)
    here = lax.rem(rows, shape[1]) // ny == cols // ny
    along_y_ref[...] = jnp.where(here, jnp.where(rows < shape[1], first, second), 0.0).astype(jnp.bfloat16)

    tile = lax.axis_index("tile")
    count = cells_ref.shape[1]
    cells = cells_ref[...]
    reach = (STEPS - 1) * HALO
    at_row = cells // nz - (tile * cx - reach) * ny
    at_z = lax.rem(cells, nz)
    depth = lax.broadcasted_iota(jnp.int32, (nz, count), 0)
    deep = depth == at_z
    tile = lax.axis_index("tile")
    count = cells_ref.shape[1]
    cells = cells_ref[...]
    reach = (STEPS - 1) * HALO
    at_row = cells // nz - (tile * cx - reach) * ny
    at_z = lax.rem(cells, nz)
    depth = lax.broadcasted_iota(jnp.int32, (nz, count), 0)
    deep = depth == at_z
    values = []
    for step in range(STEPS):
        trace = traces_ref[0, pl.ds(STEPS - 1 - step, 1), :]
        high = trace.astype(jnp.bfloat16).astype(jnp.float32)
        values += [jnp.where(deep, high, 0.0), jnp.where(deep, trace - high, 0.0)]
    values = jnp.concatenate(values, axis=0).astype(jnp.bfloat16)
    chunk = 2 * HALO
    row = lax.broadcasted_iota(jnp.int32, (chunk * ny, count), 0)

    def body(c, carry):
        hot = jnp.where(at_row == row + c * (chunk * ny), 1.0, 0.0).astype(jnp.bfloat16)
        found = lax.dot_general(hot, values, (((1,), (1,)), ((), ())), preferred_element_type=jnp.float32)
        for step in range(STEPS):
            both = found[:, 2 * step * nz : (2 * step + 1) * nz] + found[:, (2 * step + 1) * nz : (2 * step + 2) * nz]
            add_ref[step, pl.ds(c * chunk, chunk)] = both.reshape(chunk, ny, nz)
        return carry

    lax.fori_loop(0, (cx + 2 * reach) // chunk, body, 0)


def matrix_differences(buf, i0, layers, along_z, along_y):
    ny, nz = buf.shape[1:]
    both = jnp.concatenate(two_terms(buf[pl.ds(i0, layers)].reshape(layers * ny, nz)), axis=1)
    from_z = jnp.dot(both, along_z, preferred_element_type=jnp.float32)
    size = along_y.shape[1]
    half = along_y.shape[0] // 2
    first_y, second = [], []
    for base in range(0, layers * ny, size):
        from_y = jnp.dot(along_y, both[base : base + size], preferred_element_type=jnp.float32)
        first_y.append(from_y[:size, :nz] + from_y[:size, nz:])
        if half == size:
            second.append(from_y[size:, :nz] + from_y[size:, nz:] + from_z[base : base + size, nz:])
    shape = (layers, ny, nz)
    first_y, first_z = jnp.concatenate(first_y, axis=0), from_z[:, :nz]
    if not second:
        return first_y.reshape(shape), first_z.reshape(shape), None
    return first_y.reshape(shape), first_z.reshape(shape), jnp.concatenate(second, axis=0).reshape(shape)


def layer_differences(buf, i, summed):
    first = None
    for k in range(1, 5):
        plus, minus = buf[i + k], buf[i - k]
        if summed is not None:
            summed = summed + SECOND[k - 1] * (plus + minus)
        term = FIRST[k - 1] * (plus - minus)
        first = term if first is None else first + term
    return first, summed


def on_segments(step, left, right, cx, work):
    work(cx, cx, True)
    reach = (STEPS - 1 - step) * HALO
    if reach:

        def body(number, carry):
            base = jnp.where(left & (number == 0), cx - reach, 2 * cx)
            work(pl.multiple_of(base, HALO), reach, False)
            return carry

        lax.fori_loop(0, left.astype(jnp.int32) + right.astype(jnp.int32), body, 0)


def march(pairs, slopes_ref, courant_ref, along_z, along_y, i0, layers, use):
    parts = [matrix_differences(cur, i0, layers, along_z, along_y) for cur, _ in pairs]
    for j in range(layers):
        i = i0 + j
        slopes = [slopes_ref[axis, i] for axis in range(3)]
        courant = courant_ref[i]
        steps = []
        for (cur, prev), (first_y, first_z, second) in zip(pairs, parts):
            first_x, applied = layer_differences(cur, i, second[j])
            applied = applied - slopes[0] * first_x - slopes[1] * first_y[j] - slopes[2] * first_z[j]
            steps.append((applied, 2.0 * cur[i] - prev[i] + courant * applied))
        for (_, prev), updated in zip(pairs, use(i, j, steps)):
            prev[i] = updated


def fill(buf, at, rows_ref, first_row, layers, keep):
    ny, nz = buf.shape[1:]
    part = rows_ref[pl.ds(first_row, layers * ny), :].astype(jnp.float32)
    if keep is not None:
        part = jnp.where(keep, part, 0.0)
    buf[pl.ds(at, layers)] = part.reshape(layers, ny, nz)


def fill_fields(now, before, own_now, own_before, from_a, from_b, base, side_a, side_b, cx, ny):
    fill(now, cx, own_now, 0, cx, None)
    fill(before, cx, own_before, 0, cx, None)
    reach = (STEPS - 1) * HALO
    for ref, (at, here, on) in ((from_a, side_a), (from_b, side_b)):
        fill(now, at, ref, base, cx, here)
        fill(before, jnp.where(at == 0, cx - reach, at), ref, base + cx * ny, reach, on)


def clear_sides(buf, left, right, cx):
    zero = jnp.zeros((HALO,) + buf.shape[1:], jnp.float32)

    @pl.when(jnp.logical_not(left))
    def _():
        buf[cx - HALO : cx] = zero

    @pl.when(jnp.logical_not(right))
    def _():
        buf[2 * cx : 2 * cx + HALO] = zero


def model_kernel(cx, ny, nz, shots, blocks, aperture_ref, *refs):
    model_refs = refs[: len(blocks)]
    along_z_ref, along_y_ref, slopes_ref, courant_ref, gain_ref, log_buf = refs[len(blocks) :]
    tile, own, left, right, side_a, side_b = layout(aperture_ref, cx)
    shot = lax.axis_index("shot")
    sides = ((cx, None), (side_a[0], side_a[1]), (side_b[0], side_b[1]))
    block_rows = ny // shots
    size = cx * block_rows

    @pl.when(own)
    def _():
        for ref, held in zip(model_refs, blocks):
            for number, (mask, place) in enumerate(held):
                y0 = pl.multiple_of((shot ^ mask) * block_rows, block_rows)
                at, here = sides[place]
                base = number * 2 * size
                speed = ref[pl.ds(base, size), :].astype(jnp.float32)
                courant = (speed * speed) * (1.0 / SCALE)
                courant_ref[pl.ds(at, cx), pl.ds(y0, block_rows), :] = courant.reshape(cx, block_rows, nz)
                if here is None:
                    gain = speed * (2.0 / SCALE)
                    gain_ref[:, pl.ds(y0, block_rows), :] = gain.reshape(cx, block_rows, nz)
                logs = jnp.log(ref[pl.ds(base + size, size), :].astype(jnp.float32))
                if here is not None:
                    logs = jnp.where(here, logs, 0.0)
                log_buf[pl.ds(at, cx), pl.ds(y0, block_rows), :] = logs.reshape(cx, block_rows, nz)
        along_z, along_y = along_z_ref[...], along_y_ref[...]

        def slopes(i0, layers, inner):
            first_y, first_z, _ = matrix_differences(log_buf, i0, layers, along_z, along_y)
            for j in range(layers):
                slopes_ref[0, i0 + j] = layer_differences(log_buf, i0 + j, None)[0] * (1.0 / 140.0)
                slopes_ref[1, i0 + j] = first_y[j] * (1.0 / 140.0)
                slopes_ref[2, i0 + j] = first_z[j] * (1.0 / 140.0)

        on_segments(0, left, right, cx, slopes)


def window_kernel(
    cx, ny, nz, order, aperture_ref, source_ref, wavelet_ref, along_z_ref, along_y_ref, slopes_ref, courant_ref, gain_ref, add_ref,
    now_ref, before_ref, end_ref, after_ref, from_a, from_b, sums_ref, wave_ref, adjoint_ref, now, before, end, after, applied_held,
    adjoint_held, image,
):
    tile, own, left, right, side_a, side_b = layout(aperture_ref, cx)
    shot = lax.axis_index("shot")
    block_rows = ny // len(order)

    @pl.when(jnp.logical_not(own))
    def _():
        wave_ref[...] = jnp.zeros_like(wave_ref)
        adjoint_ref[...] = jnp.zeros_like(adjoint_ref)
        sums_ref[...] = jnp.zeros_like(sums_ref)

    @pl.when(own)
    def _():
        half = from_a.shape[0] // 2
        fill_fields(now, before, now_ref, before_ref, from_a, from_b, 0, side_a, side_b, cx, ny)
        fill_fields(end, after, end_ref, after_ref, from_a, from_b, half, side_a, side_b, cx, ny)
        along_z, along_y = along_z_ref[...], along_y_ref[...]
        cell = source_ref[0]
        layer = cell // (ny * nz) - (tile - 1) * cx
        row = lax.rem(cell // nz, ny)
        depth = lax.rem(cell, nz)
        lanes = lax.broadcasted_iota(jnp.int32, (1, nz), 1)
        forward, adjoint = (now, before), (end, after)
        for step in range(STEPS):
            here = tuple((bufs[step % 2], bufs[(step + 1) % 2]) for bufs in (forward, adjoint))

            def work(i0, layers, inner, here=here, step=step):
                def use(i, j, steps):
                    (applied, wave), (_, back) = steps
                    back = back + add_ref[step, i - (cx - (STEPS - 1) * HALO)]
                    if inner and 2 * step < STEPS:
                        applied_held[step, j] = applied
                        adjoint_held[step, j] = back
                    elif inner:
                        other = STEPS - 1 - step
                        terms = applied * adjoint_held[other, j] + back * applied_held[other, j]
                        image[j] = terms if 2 * step == STEPS else image[j] + terms
                    return wave, back

                march(here, slopes_ref, courant_ref, along_z, along_y, i0, layers, use)

            on_segments(step, left, right, cx, work)
            reach = (STEPS - 1 - step) * HALO
            low = jnp.where(left, cx - reach, cx)
            high = jnp.where(right, 2 * cx + reach, 2 * cx)
            value = wavelet_ref[0, step]
            made = here[0][1]

            @pl.when((layer >= low) & (layer < high))
            def _(made=made, value=value):
                old = made[layer, pl.ds(row, 1), :]
                made[layer, pl.ds(row, 1), :] = old + jnp.where(lanes == depth, value, 0.0)

            if step == 0:
                clear_sides(now, left, right, cx)
                clear_sides(end, left, right, cx)
        wave_ref[...] = forward[STEPS % 2][cx : 2 * cx].reshape(cx * ny, nz)
        adjoint_ref[...] = adjoint[STEPS % 2][cx : 2 * cx].reshape(cx * ny, nz)
        for place, mask in enumerate(order):
            y0 = pl.multiple_of((shot ^ mask) * block_rows, block_rows)
            gain = gain_ref[:, pl.ds(y0, block_rows), :]
            sums_ref[place] = (gain * image[:, pl.ds(y0, block_rows), :]).reshape(cx * block_rows, nz)


def pairs(axis_sizes, kind):
    tiles, shots = axis_sizes
    found = []
    for tile in range(tiles):
        other = tile ^ 1 if kind == "a" else ((tile + 1) ^ 1) - 1
        for shot in range(shots):
            here = tile * shots + shot
            if 0 <= other < tiles:
                found.append((here, other * shots + shot))
            elif shots % 2 == 0:
                found.append((here, tile * shots + (shot ^ 1)))
    return found


def local(
    velocity, density, wave_now, wave_before, adjoint_end, adjoint_after, source_cell, source_wave, receiver_cell, residual_traces,
    aperture,
):
    cx, _, nz = velocity.shape
    ny = wave_now.shape[2]
    shots = lax.axis_size("shot")
    tiles = lax.axis_size("tile")
    rows = cx * ny
    params = pltpu.CompilerParams(vmem_limit_bytes=VMEM_BYTES)

    def swap(x, kind):
        return lax.ppermute(x, ("tile", "shot"), pairs((tiles, shots), kind))

    def cross(x, mask):
        return lax.ppermute(x, "shot", [(i, i ^ mask) for i in range(shots)])

    fields = [x.reshape(rows, nz) for x in (wave_now, wave_before, adjoint_end, adjoint_after)]
    message = jax.ShapeDtypeStruct((2 * (cx + (STEPS - 1) * HALO), ny, nz), jnp.bfloat16)
    model, to_a, to_b = pl.pallas_call(
        pack_kernel,
        out_shape=(jax.ShapeDtypeStruct((2 * cx,) + velocity.shape[1:], jnp.bfloat16), message, message),
        in_specs=[pl.BlockSpec(memory_space=pltpu.HBM)] * 6,
        out_specs=(vmem(),) * 3,
        scratch_shapes=[pltpu.SemaphoreType.DMA((10,))],
        compiler_params=pltpu.CompilerParams(vmem_limit_bytes=PACK_BYTES),
        cost_estimate=pl.CostEstimate(flops=0, bytes_accessed=2 * 2**20, transcendentals=0),
        name="pack",
    )(velocity, density, wave_now, wave_before, adjoint_end, adjoint_after)
    model, to_a, to_b = (x.reshape(-1, nz) for x in (model, to_a, to_b))

    from_a, from_b = swap(to_a, "a"), swap(to_b, "b")

    model_a, model_b = swap(model, "a"), swap(model, "b")
    high = shots // 2
    near = [([(0, 0)], model), ([(0, 1)], model_a), ([(0, 2)], model_b)]
    late = []
    if high:
        near.append(([(high, 0)], cross(model, high)))
        late.append(([(high, 1), (high, 2)], cross(jnp.concatenate([model_a, model_b], axis=0), high)))

    along_z, along_y, added, joined = pl.pallas_call(
        lambda *refs: setup_kernel(cx, *refs),
        out_shape=(
            jax.ShapeDtypeStruct((2 * nz, 2 * nz), jnp.bfloat16),
            jax.ShapeDtypeStruct((2 * HALO * ny, HALO * ny), jnp.bfloat16),
            jax.ShapeDtypeStruct((STEPS, cx + 2 * (STEPS - 1) * HALO, ny, nz), jnp.float32),
            jax.ShapeDtypeStruct((len(near) * model.shape[0], nz), jnp.bfloat16),
        ),
        in_specs=[vmem()] * (2 + len(near)),
        out_specs=(vmem(),) * 4,
        compiler_params=params,
        cost_estimate=pl.CostEstimate(flops=2 * 10**9, bytes_accessed=4 * 2**20, transcendentals=0),
        name="receivers",
    )(receiver_cell, residual_traces, *[block for _, block in near])

    near = [([name for names, _ in near for name in names], joined)]
    mask = high // 2
    while mask:
        moved = []
        for group in (near, late):
            names = [(m ^ mask, place) for held, _ in group for m, place in held]
            array = group[0][1] if len(group) == 1 else jnp.concatenate([block for _, block in group], axis=0)
            moved.append((names, cross(array, mask)))
        near, late = near + moved[:1], late + moved[1:]
        mask //= 2
    held = near + late

    field = pltpu.VMEM((3 * cx, ny, nz), jnp.float32)
    blocks = tuple(tuple(names) for names, _ in held)
    slopes, courant, gain = pl.pallas_call(
        lambda *refs: model_kernel(cx, ny, nz, shots, blocks, *refs),
        out_shape=(
            jax.ShapeDtypeStruct((3, 3 * cx, ny, nz), jnp.float32),
            jax.ShapeDtypeStruct((3 * cx, ny, nz), jnp.float32),
            jax.ShapeDtypeStruct((cx, ny, nz), jnp.float32),
        ),
        in_specs=[smem()] + [vmem()] * (len(held) + 2),
        out_specs=(vmem(),) * 3,
        scratch_shapes=[field],
        compiler_params=params,
        cost_estimate=pl.CostEstimate(flops=10**6, bytes_accessed=2**20, transcendentals=0),
        name="model",
    )(aperture, *[block for _, block in held], along_z, along_y)

    bits = []
    mask = 1
    while mask < shots:
        bits.append(mask)
        mask *= 2
    order = [0]
    for bit in reversed(bits):
        order = order + [m | bit for m in order]
    order = tuple(order)
    sums, wave_end, adjoint_start = pl.pallas_call(
        lambda *refs: window_kernel(cx, ny, nz, order, *refs),
        out_shape=(
            jax.ShapeDtypeStruct((shots, cx * (ny // shots), nz), jnp.float32),
            jax.ShapeDtypeStruct((rows, nz), jnp.float32),
            jax.ShapeDtypeStruct((rows, nz), jnp.float32),
        ),
        in_specs=[smem()] * 3 + [vmem()] * 12,
        out_specs=(vmem(),) * 3,
        scratch_shapes=[field] * 4 + [pltpu.VMEM((STEPS // 2, cx, ny, nz), jnp.float32)] * 2 + [pltpu.VMEM((cx, ny, nz), jnp.float32)],
        compiler_params=params,
        cost_estimate=pl.CostEstimate(flops=10**10, bytes_accessed=16 * 2**20, transcendentals=0),
        name="window",
    )(aperture, source_cell, source_wave, along_z, along_y, slopes, courant, gain, added, *fields, from_a, from_b)
    for bit in bits:
        half = sums.shape[0] // 2
        sums = sums[:half] + cross(sums[half:], bit)
    gradient = sums[0].reshape(cx, ny // shots, nz)
    ends = [x.astype(jnp.bfloat16).reshape(wave_now.shape) for x in (wave_end, adjoint_start)]
    return gradient, ends[0], ends[1]


def solution(mesh):
    stored = P(("parts", "tile"), "shot", None)
    field = P(("parts", "shot"), "tile", None, None)
    return jax.shard_map(
        local,
        mesh=mesh,
        in_specs=(
            stored, stored, field, field, field, field, P(("parts", "shot")), P(("parts", "shot"), None),
            P(("parts", "shot"), None), P(("parts", "shot"), None, None), P(("parts", "shot"), None),
        ),
        out_specs=(stored, field, field),
        check_vma=False,
    )
```

```python
import jax
import jax.numpy as jnp
from jax import lax
from jax.experimental import pallas as pl
from jax.experimental.pallas import tpu as pltpu
from jax.sharding import PartitionSpec as P

FIRST = (672.0, -168.0, 32.0, -3.0)
SECOND = (8064.0, -1008.0, 128.0, -9.0)
CENTRE_Z = -43008.0
CENTRE_Y = -42.0
SCALE = 5040.0
STEPS = 4
PACK_BYTES = 56 * 1024 * 1024
HALO = 4
VMEM_BYTES = 24 * 1024 * 1024


def vmem():
    return pl.BlockSpec(memory_space=pltpu.VMEM)


def smem():
    return pl.BlockSpec(memory_space=pltpu.SMEM)


def two_terms(values):
    high = values.astype(jnp.bfloat16)
    low = (values - high.astype(jnp.float32)).astype(jnp.bfloat16)
    return high, low


def is_active(aperture_ref, tile):
    found = aperture_ref[0, 0] == tile
    for slot in range(1, aperture_ref.shape[1]):
        found = found | (aperture_ref[0, slot] == tile)
    return found & (tile >= 0)


def layout(aperture_ref, cx):
    tiles = lax.axis_size("tile")
    tile = lax.axis_index("tile")
    even = lax.rem(tile, 2) == 0
    left = is_active(aperture_ref, tile - 1) & (tile > 0)
    right = is_active(aperture_ref, tile + 1) & (tile < tiles - 1)
    own = is_active(aperture_ref, tile)
    a_tile = jnp.where(even, tile + 1, tile - 1)
    b_tile = jnp.where(even, tile - 1, tile + 1)
    a_at = jnp.where(even, 2 * cx, 0)
    b_at = jnp.where(even, 0, 2 * cx)
    a_here = (a_tile >= 0) & (a_tile < tiles)
    b_here = (b_tile >= 0) & (b_tile < tiles)
    a_on = jnp.where(even, right, left)
    b_on = jnp.where(even, left, right)
    return tile, own, left, right, (a_at, a_here, a_on), (b_at, b_here, b_on)


def difference_matrix(shape, along, across, block, centre):
    ahead = lax.rem(along, block) - lax.rem(across, block)
    first = jnp.zeros(shape, jnp.float32)
    second = jnp.where(ahead == 0, centre, 0.0)
    for k in range(1, 5):
        first = jnp.where(ahead == k, FIRST[k - 1], jnp.where(ahead == -k, -FIRST[k - 1], first))
        second = jnp.where((ahead == k) | (ahead == -k), SECOND[k - 1], second)
    return first, second


def pack_kernel(*refs):
    (velocity_ref, density_ref, now_ref, before_ref, end_ref, after_ref, model_ref, a_ref, b_ref, model_buf, now_buf, before_buf,
     end_buf, after_buf, in_sems, out_sems) = refs
    cx = velocity_ref.shape[0]
    even = lax.rem(lax.axis_index("tile"), 2) == 0
    reach = (STEPS - 1) * HALO
    loads = [
        (velocity_ref, model_buf.at[0:cx]), (density_ref, model_buf.at[cx : 2 * cx]), (now_ref.at[0], now_buf),
        (before_ref.at[0], before_buf), (end_ref.at[0], end_buf), (after_ref.at[0], after_buf),
    ]
    loads = [pltpu.make_async_copy(src, dst, in_sems.at[number]) for number, (src, dst) in enumerate(loads)]
    for load in loads:
        load.start()
    stores = [[], [(model_buf, model_ref)], [], [], [], []]
    for side, out_ref in enumerate((a_ref, b_ref)):
        first = jnp.where(even == (side == 0), cx - reach, 0)
        base = 0
        for number, (whole, part) in ((2, (now_buf, before_buf)), (4, (end_buf, after_buf))):
            stores[number].append((whole, out_ref.at[base : base + cx]))
            stores[number + 1].append((part.at[pl.ds(first, reach)], out_ref.at[base + cx : base + cx + reach]))
            base += cx + reach
    started = []
    for load, after in zip(loads, stores):
        load.wait()
        for src, dst in after:
            copy = pltpu.make_async_copy(src, dst, out_sems.at[len(started)])
            copy.start()
            started.append(copy)
    for copy in started:
        copy.wait()


def setup_kernel(cx, receivers_ref, *refs):
    parts, (along_z_ref, along_y_ref, add_ref, joined_ref) = refs[:-4], refs[-4:]
    ny, nz = add_ref.shape[2:]
    size = parts[0].shape[0]
    for number, part in enumerate(parts):
        joined_ref[number * size : (number + 1) * size, :] = part[...]

    shape = along_z_ref.shape
    rows, cols = (lax.broadcasted_iota(jnp.int32, shape, d) for d in range(2))
    first, second = difference_matrix(shape, rows, cols, nz, CENTRE_Z)
    along_z_ref[...] = jnp.where(cols < nz, first, second).astype(jnp.bfloat16)
    shape = along_y_ref.shape
    rows, cols = (lax.broadcasted_iota(jnp.int32, shape, d) for d in range(2))
    first, second = difference_matrix(shape, cols, rows, ny, CENTRE_Y)
    here = lax.rem(rows, shape[1]) // ny == cols // ny
    along_y_ref[...] = jnp.where(here, jnp.where(rows < shape[1], first, second), 0.0).astype(jnp.bfloat16)

    tile = lax.axis_index("tile")
    count = receivers_ref.shape[1]
    cells = receivers_ref[STEPS : STEPS + 1, :].astype(jnp.int32)
    reach = (STEPS - 1) * HALO
    at_row = cells // nz - (tile * cx - reach) * ny
    at_z = lax.rem(cells, nz)
    depth = lax.broadcasted_iota(jnp.int32, (nz, count), 0)
    deep = depth == at_z
    tile = lax.axis_index("tile")
    count = receivers_ref.shape[1]
    cells = receivers_ref[STEPS : STEPS + 1, :].astype(jnp.int32)
    reach = (STEPS - 1) * HALO
    at_row = cells // nz - (tile * cx - reach) * ny
    at_z = lax.rem(cells, nz)
    depth = lax.broadcasted_iota(jnp.int32, (nz, count), 0)
    deep = depth == at_z
    values = []
    for step in range(STEPS):
        trace = receivers_ref[pl.ds(STEPS - 1 - step, 1), :]
        high = trace.astype(jnp.bfloat16).astype(jnp.float32)
        values += [jnp.where(deep, high, 0.0), jnp.where(deep, trace - high, 0.0)]
    values = jnp.concatenate(values, axis=0).astype(jnp.bfloat16)
    chunk = 2 * HALO
    row = lax.broadcasted_iota(jnp.int32, (chunk * ny, count), 0)

    def body(c, carry):
        hot = jnp.where(at_row == row + c * (chunk * ny), 1.0, 0.0).astype(jnp.bfloat16)
        found = lax.dot_general(hot, values, (((1,), (1,)), ((), ())), preferred_element_type=jnp.float32)
        for step in range(STEPS):
            both = found[:, 2 * step * nz : (2 * step + 1) * nz] + found[:, (2 * step + 1) * nz : (2 * step + 2) * nz]
            add_ref[step, pl.ds(c * chunk, chunk)] = both.reshape(chunk, ny, nz)
        return carry

    lax.fori_loop(0, (cx + 2 * reach) // chunk, body, 0)


def matrix_differences(buf, i0, layers, along_z, along_y):
    ny, nz = buf.shape[1:]
    both = jnp.concatenate(two_terms(buf[pl.ds(i0, layers)].reshape(layers * ny, nz)), axis=1)
    from_z = jnp.dot(both, along_z, preferred_element_type=jnp.float32)
    size = along_y.shape[1]
    half = along_y.shape[0] // 2
    first_y, second = [], []
    for base in range(0, layers * ny, size):
        from_y = jnp.dot(along_y, both[base : base + size], preferred_element_type=jnp.float32)
        first_y.append(from_y[:size, :nz] + from_y[:size, nz:])
        if half == size:
            second.append(from_y[size:, :nz] + from_y[size:, nz:] + from_z[base : base + size, nz:])
    shape = (layers, ny, nz)
    first_y, first_z = jnp.concatenate(first_y, axis=0), from_z[:, :nz]
    if not second:
        return first_y.reshape(shape), first_z.reshape(shape), None
    return first_y.reshape(shape), first_z.reshape(shape), jnp.concatenate(second, axis=0).reshape(shape)


def first_along_x(buf, i):
    first = None
    for k in range(1, 5):
        term = FIRST[k - 1] * (buf[i + k] - buf[i - k])
        first = term if first is None else first + term
    return first


def on_segments(step, left, right, cx, work):
    work(cx, cx, True)
    reach = (STEPS - 1 - step) * HALO
    if reach:

        def body(number, carry):
            base = jnp.where(left & (number == 0), cx - reach, 2 * cx)
            work(pl.multiple_of(base, HALO), reach, False)
            return carry

        lax.fori_loop(0, left.astype(jnp.int32) + right.astype(jnp.int32), body, 0)


def march(pairs, ahead_ref, slopes_ref, courant_ref, along_z, along_y, i0, layers, use):
    parts = [matrix_differences(cur, i0, layers, along_z, along_y) for cur, _ in pairs]
    for j in range(layers):
        i = i0 + j
        applied = [second[j] for _, _, second in parts]
        for k in range(1, 5):
            for side, offset in enumerate((k, -k)):
                factor = ahead_ref[2 * (k - 1) + side, i]
                applied = [value + factor * cur[i + offset] for value, (cur, _) in zip(applied, pairs)]
        along = [slopes_ref[axis, i] for axis in range(2)]
        courant = courant_ref[i]
        steps = []
        for value, (cur, prev), (first_y, first_z, _) in zip(applied, pairs, parts):
            value = value - along[0] * first_y[j] - along[1] * first_z[j]
            steps.append((value, 2.0 * cur[i] - prev[i] + courant * value))
        for (_, prev), updated in zip(pairs, use(i, j, steps)):
            prev[i] = updated


def fill(buf, at, rows_ref, first_row, layers, keep):
    ny, nz = buf.shape[1:]
    part = rows_ref[pl.ds(first_row, layers * ny), :].astype(jnp.float32)
    if keep is not None:
        part = jnp.where(keep, part, 0.0)
    buf[pl.ds(at, layers)] = part.reshape(layers, ny, nz)


def fill_fields(now, before, own_now, own_before, from_a, from_b, base, side_a, side_b, cx, ny):
    fill(now, cx, own_now, 0, cx, None)
    fill(before, cx, own_before, 0, cx, None)
    reach = (STEPS - 1) * HALO
    for ref, (at, here, on) in ((from_a, side_a), (from_b, side_b)):
        fill(now, at, ref, base, cx, here)
        fill(before, jnp.where(at == 0, cx - reach, at), ref, base + cx * ny, reach, on)


def clear_sides(buf, left, right, cx):
    zero = jnp.zeros((HALO,) + buf.shape[1:], jnp.float32)

    @pl.when(jnp.logical_not(left))
    def _():
        buf[cx - HALO : cx] = zero

    @pl.when(jnp.logical_not(right))
    def _():
        buf[2 * cx : 2 * cx + HALO] = zero


def model_kernel(cx, ny, nz, shots, blocks, aperture_ref, *refs):
    model_refs = refs[: len(blocks)]
    along_z_ref, along_y_ref, ahead_ref, slopes_ref, courant_ref, gain_ref, log_buf = refs[len(blocks) :]
    tile, own, left, right, side_a, side_b = layout(aperture_ref, cx)
    shot = lax.axis_index("shot")
    sides = ((cx, None), (side_a[0], side_a[1]), (side_b[0], side_b[1]))
    block_rows = ny // shots
    size = cx * block_rows

    @pl.when(own)
    def _():
        for ref, held in zip(model_refs, blocks):
            for number, (mask, place) in enumerate(held):
                y0 = pl.multiple_of((shot ^ mask) * block_rows, block_rows)
                at, here = sides[place]
                base = number * 2 * size
                speed = ref[pl.ds(base, size), :].astype(jnp.float32)
                courant = (speed * speed) * (1.0 / SCALE)
                courant_ref[pl.ds(at, cx), pl.ds(y0, block_rows), :] = courant.reshape(cx, block_rows, nz)
                if here is None:
                    gain = speed * (2.0 / SCALE)
                    gain_ref[:, pl.ds(y0, block_rows), :] = gain.reshape(cx, block_rows, nz)
                logs = jnp.log(ref[pl.ds(base + size, size), :].astype(jnp.float32))
                if here is not None:
                    logs = jnp.where(here, logs, 0.0)
                log_buf[pl.ds(at, cx), pl.ds(y0, block_rows), :] = logs.reshape(cx, block_rows, nz)
        along_z, along_y = along_z_ref[...], along_y_ref[...]

        def slopes(i0, layers, inner):
            first_y, first_z, _ = matrix_differences(log_buf, i0, layers, along_z, along_y)
            for j in range(layers):
                i = i0 + j
                along_x = first_along_x(log_buf, i) * (1.0 / 140.0)
                for k in range(1, 5):
                    ahead_ref[2 * k - 2, i] = SECOND[k - 1] - FIRST[k - 1] * along_x
                    ahead_ref[2 * k - 1, i] = SECOND[k - 1] + FIRST[k - 1] * along_x
                slopes_ref[0, i] = first_y[j] * (1.0 / 140.0)
                slopes_ref[1, i] = first_z[j] * (1.0 / 140.0)

        on_segments(0, left, right, cx, slopes)


def window_kernel(
    cx, ny, nz, order, aperture_ref, source_ref, wavelet_ref, along_z_ref, along_y_ref, ahead_ref, slopes_ref, courant_ref, gain_ref, add_ref,
    now_ref, before_ref, end_ref, after_ref, from_a, from_b, sums_ref, wave_ref, adjoint_ref, now, before, end, after, applied_held,
    adjoint_held, image,
):
    tile, own, left, right, side_a, side_b = layout(aperture_ref, cx)
    shot = lax.axis_index("shot")
    block_rows = ny // len(order)

    @pl.when(jnp.logical_not(own))
    def _():
        wave_ref[...] = jnp.zeros_like(wave_ref)
        adjoint_ref[...] = jnp.zeros_like(adjoint_ref)
        sums_ref[...] = jnp.zeros_like(sums_ref)

    @pl.when(own)
    def _():
        half = from_a.shape[0] // 2
        fill_fields(now, before, now_ref, before_ref, from_a, from_b, 0, side_a, side_b, cx, ny)
        fill_fields(end, after, end_ref, after_ref, from_a, from_b, half, side_a, side_b, cx, ny)
        along_z, along_y = along_z_ref[...], along_y_ref[...]
        cell = source_ref[0]
        layer = cell // (ny * nz) - (tile - 1) * cx
        row = lax.rem(cell // nz, ny)
        depth = lax.rem(cell, nz)
        lanes = lax.broadcasted_iota(jnp.int32, (1, nz), 1)
        forward, adjoint = (now, before), (end, after)
        for step in range(STEPS):
            here = tuple((bufs[step % 2], bufs[(step + 1) % 2]) for bufs in (forward, adjoint))

            def work(i0, layers, inner, here=here, step=step):
                def use(i, j, steps):
                    (applied, wave), (_, back) = steps
                    back = back + add_ref[step, i - (cx - (STEPS - 1) * HALO)]
                    if inner and 2 * step < STEPS:
                        applied_held[step, j] = applied
                        adjoint_held[step, j] = back
                    elif inner:
                        other = STEPS - 1 - step
                        terms = applied * adjoint_held[other, j] + back * applied_held[other, j]
                        image[j] = terms if 2 * step == STEPS else image[j] + terms
                    return wave, back

                march(here, ahead_ref, slopes_ref, courant_ref, along_z, along_y, i0, layers, use)

            on_segments(step, left, right, cx, work)
            reach = (STEPS - 1 - step) * HALO
            low = jnp.where(left, cx - reach, cx)
            high = jnp.where(right, 2 * cx + reach, 2 * cx)
            value = wavelet_ref[0, step]
            made = here[0][1]

            @pl.when((layer >= low) & (layer < high))
            def _(made=made, value=value):
                old = made[layer, pl.ds(row, 1), :]
                made[layer, pl.ds(row, 1), :] = old + jnp.where(lanes == depth, value, 0.0)

            if step == 0:
                clear_sides(now, left, right, cx)
                clear_sides(end, left, right, cx)
        wave_ref[...] = forward[STEPS % 2][cx : 2 * cx].reshape(cx * ny, nz)
        adjoint_ref[...] = adjoint[STEPS % 2][cx : 2 * cx].reshape(cx * ny, nz)
        for place, mask in enumerate(order):
            y0 = pl.multiple_of((shot ^ mask) * block_rows, block_rows)
            gain = gain_ref[:, pl.ds(y0, block_rows), :]
            sums_ref[place] = (gain * image[:, pl.ds(y0, block_rows), :]).reshape(cx * block_rows, nz)


def pairs(axis_sizes, kind):
    tiles, shots = axis_sizes
    found = []
    for tile in range(tiles):
        other = tile ^ 1 if kind == "a" else ((tile + 1) ^ 1) - 1
        for shot in range(shots):
            here = tile * shots + shot
            if 0 <= other < tiles:
                found.append((here, other * shots + shot))
            elif shots % 2 == 0:
                found.append((here, tile * shots + (shot ^ 1)))
    return found


def local(
    velocity, density, wave_now, wave_before, adjoint_end, adjoint_after, source_cell, source_wave, receiver_cell, residual_traces,
    aperture,
):
    cx, _, nz = velocity.shape
    ny = wave_now.shape[2]
    shots = lax.axis_size("shot")
    tiles = lax.axis_size("tile")
    rows = cx * ny
    params = pltpu.CompilerParams(vmem_limit_bytes=VMEM_BYTES)

    def swap(x, kind):
        return lax.ppermute(x, ("tile", "shot"), pairs((tiles, shots), kind))

    def cross(x, mask):
        return lax.ppermute(x, "shot", [(i, i ^ mask) for i in range(shots)])

    fields = [x.reshape(rows, nz) for x in (wave_now, wave_before, adjoint_end, adjoint_after)]
    message = jax.ShapeDtypeStruct((2 * (cx + (STEPS - 1) * HALO), ny, nz), jnp.bfloat16)
    model, to_a, to_b = pl.pallas_call(
        pack_kernel,
        out_shape=(jax.ShapeDtypeStruct((2 * cx,) + velocity.shape[1:], jnp.bfloat16), message, message),
        in_specs=[pl.BlockSpec(memory_space=pltpu.HBM)] * 6,
        out_specs=(pl.BlockSpec(memory_space=pltpu.HBM),) * 3,
        scratch_shapes=[pltpu.VMEM((2 * cx,) + velocity.shape[1:], jnp.bfloat16)]
        + [pltpu.VMEM((cx, ny, nz), jnp.bfloat16)] * 4
        + [pltpu.SemaphoreType.DMA((6,)), pltpu.SemaphoreType.DMA((9,))],
        compiler_params=pltpu.CompilerParams(vmem_limit_bytes=PACK_BYTES),
        cost_estimate=pl.CostEstimate(flops=0, bytes_accessed=2 * 2**20, transcendentals=0),
        name="pack",
    )(velocity, density, wave_now, wave_before, adjoint_end, adjoint_after)
    model, to_a, to_b = (x.reshape(-1, nz) for x in (model, to_a, to_b))

    from_a, from_b = swap(to_a, "a"), swap(to_b, "b")

    model_a, model_b = swap(model, "a"), swap(model, "b")
    high = shots // 2
    near = [([(0, 0)], model), ([(0, 1)], model_a), ([(0, 2)], model_b)]
    late = []
    if high:
        late.append(([(high, 1), (high, 2)], cross(jnp.concatenate([model_a, model_b], axis=0), high)))
        late.append(([(high, 0)], cross(model, high)))

    receivers = jnp.concatenate([residual_traces[0], receiver_cell.astype(jnp.float32)], axis=0)
    along_z, along_y, added, joined = pl.pallas_call(
        lambda *refs: setup_kernel(cx, *refs),
        out_shape=(
            jax.ShapeDtypeStruct((2 * nz, 2 * nz), jnp.bfloat16),
            jax.ShapeDtypeStruct((2 * HALO * ny, HALO * ny), jnp.bfloat16),
            jax.ShapeDtypeStruct((STEPS, cx + 2 * (STEPS - 1) * HALO, ny, nz), jnp.float32),
            jax.ShapeDtypeStruct((len(near) * model.shape[0], nz), jnp.bfloat16),
        ),
        in_specs=[vmem()] * (1 + len(near)),
        out_specs=(vmem(),) * 4,
        compiler_params=params,
        cost_estimate=pl.CostEstimate(flops=2 * 10**9, bytes_accessed=4 * 2**20, transcendentals=0),
        name="receivers",
    )(receivers, *[block for _, block in near])

    near = [([name for names, _ in near for name in names], joined)]
    mask = high // 2
    while mask:
        moved = []
        for group in (near, late):
            names = [(m ^ mask, place) for held, _ in group for m, place in held]
            array = group[0][1] if len(group) == 1 else jnp.concatenate([block for _, block in group], axis=0)
            moved.append((names, cross(array, mask)))
        near, late = near + moved[:1], late + moved[1:]
        mask //= 2
    held = near + late

    field = pltpu.VMEM((3 * cx, ny, nz), jnp.float32)
    blocks = tuple(tuple(names) for names, _ in held)
    ahead, slopes, courant, gain = pl.pallas_call(
        lambda *refs: model_kernel(cx, ny, nz, shots, blocks, *refs),
        out_shape=(
            jax.ShapeDtypeStruct((8, 3 * cx, ny, nz), jnp.float32),
            jax.ShapeDtypeStruct((2, 3 * cx, ny, nz), jnp.float32),
            jax.ShapeDtypeStruct((3 * cx, ny, nz), jnp.float32),
            jax.ShapeDtypeStruct((cx, ny, nz), jnp.float32),
        ),
        in_specs=[smem()] + [vmem()] * (len(held) + 2),
        out_specs=(vmem(),) * 4,
        scratch_shapes=[field],
        compiler_params=params,
        cost_estimate=pl.CostEstimate(flops=10**6, bytes_accessed=2**20, transcendentals=0),
        name="model",
    )(aperture, *[block for _, block in held], along_z, along_y)

    bits = []
    mask = 1
    while mask < shots:
        bits.append(mask)
        mask *= 2
    order = [0]
    for bit in reversed(bits):
        order = order + [m | bit for m in order]
    order = tuple(order)
    sums, wave_end, adjoint_start = pl.pallas_call(
        lambda *refs: window_kernel(cx, ny, nz, order, *refs),
        out_shape=(
            jax.ShapeDtypeStruct((shots, cx * (ny // shots), nz), jnp.float32),
            jax.ShapeDtypeStruct((rows, nz), jnp.float32),
            jax.ShapeDtypeStruct((rows, nz), jnp.float32),
        ),
        in_specs=[smem()] * 3 + [vmem()] * 13,
        out_specs=(vmem(),) * 3,
        scratch_shapes=[field] * 4 + [pltpu.VMEM((STEPS // 2, cx, ny, nz), jnp.float32)] * 2 + [pltpu.VMEM((cx, ny, nz), jnp.float32)],
        compiler_params=params,
        cost_estimate=pl.CostEstimate(flops=10**10, bytes_accessed=16 * 2**20, transcendentals=0),
        name="window",
    )(aperture, source_cell, source_wave, along_z, along_y, ahead, slopes, courant, gain, added, *fields, from_a, from_b)
    for bit in bits:
        half = sums.shape[0] // 2
        sums = sums[:half] + cross(sums[half:], bit)
    gradient = sums[0].reshape(cx, ny // shots, nz)
    ends = [x.astype(jnp.bfloat16).reshape(wave_now.shape) for x in (wave_end, adjoint_start)]
    return gradient, ends[0], ends[1]


def solution(mesh):
    stored = P(("parts", "tile"), "shot", None)
    field = P(("parts", "shot"), "tile", None, None)
    return jax.shard_map(
        local,
        mesh=mesh,
        in_specs=(
            stored, stored, field, field, field, field, P(("parts", "shot")), P(("parts", "shot"), None),
            P(("parts", "shot"), None), P(("parts", "shot"), None, None), P(("parts", "shot"), None),
        ),
        out_specs=(stored, field, field),
        check_vma=False,
    )
```

```python
import jax
import jax.numpy as jnp
from jax import lax
from jax.experimental import pallas as pl
from jax.experimental.pallas import tpu as pltpu
from jax.sharding import PartitionSpec as P

FIRST = (672.0, -168.0, 32.0, -3.0)
SECOND = (8064.0, -1008.0, 128.0, -9.0)
CENTRE_Z = -43008.0
CENTRE_Y = -42.0
SCALE = 5040.0
STEPS = 4
PACK_BYTES = 56 * 1024 * 1024
HALO = 4
VMEM_BYTES = 24 * 1024 * 1024


def vmem():
    return pl.BlockSpec(memory_space=pltpu.VMEM)


def smem():
    return pl.BlockSpec(memory_space=pltpu.SMEM)


def two_terms(values):
    high = values.astype(jnp.bfloat16)
    low = (values - high.astype(jnp.float32)).astype(jnp.bfloat16)
    return high, low


def is_active(aperture_ref, tile):
    found = aperture_ref[0, 0] == tile
    for slot in range(1, aperture_ref.shape[1]):
        found = found | (aperture_ref[0, slot] == tile)
    return found & (tile >= 0)


def layout(aperture_ref, cx):
    tiles = lax.axis_size("tile")
    tile = lax.axis_index("tile")
    even = lax.rem(tile, 2) == 0
    left = is_active(aperture_ref, tile - 1) & (tile > 0)
    right = is_active(aperture_ref, tile + 1) & (tile < tiles - 1)
    own = is_active(aperture_ref, tile)
    a_tile = jnp.where(even, tile + 1, tile - 1)
    b_tile = jnp.where(even, tile - 1, tile + 1)
    a_at = jnp.where(even, 2 * cx, 0)
    b_at = jnp.where(even, 0, 2 * cx)
    a_here = (a_tile >= 0) & (a_tile < tiles)
    b_here = (b_tile >= 0) & (b_tile < tiles)
    a_on = jnp.where(even, right, left)
    b_on = jnp.where(even, left, right)
    return tile, own, left, right, (a_at, a_here, a_on), (b_at, b_here, b_on)


def difference_matrix(shape, along, across, block, centre):
    ahead = lax.rem(along, block) - lax.rem(across, block)
    first = jnp.zeros(shape, jnp.float32)
    second = jnp.where(ahead == 0, centre, 0.0)
    for k in range(1, 5):
        first = jnp.where(ahead == k, FIRST[k - 1], jnp.where(ahead == -k, -FIRST[k - 1], first))
        second = jnp.where((ahead == k) | (ahead == -k), SECOND[k - 1], second)
    return first, second


def pack_kernel(*refs):
    (velocity_ref, density_ref, now_ref, before_ref, end_ref, after_ref, model_ref, a_ref, b_ref, model_buf, now_buf, before_buf,
     end_buf, after_buf, in_sems, out_sems) = refs
    cx = velocity_ref.shape[0]
    even = lax.rem(lax.axis_index("tile"), 2) == 0
    reach = (STEPS - 1) * HALO
    loads = [
        (velocity_ref, model_buf.at[0:cx]), (density_ref, model_buf.at[cx : 2 * cx]), (now_ref.at[0], now_buf),
        (before_ref.at[0], before_buf), (end_ref.at[0], end_buf), (after_ref.at[0], after_buf),
    ]
    loads = [pltpu.make_async_copy(src, dst, in_sems.at[number]) for number, (src, dst) in enumerate(loads)]
    for load in loads:
        load.start()
    stores = [[], [(model_buf, model_ref)], [], [], [], []]
    for side, out_ref in enumerate((a_ref, b_ref)):
        first = jnp.where(even == (side == 0), cx - reach, 0)
        base = 0
        for number, (whole, part) in ((2, (now_buf, before_buf)), (4, (end_buf, after_buf))):
            stores[number].append((whole, out_ref.at[base : base + cx]))
            stores[number + 1].append((part.at[pl.ds(first, reach)], out_ref.at[base + cx : base + cx + reach]))
            base += cx + reach
    started = []
    for load, after in zip(loads, stores):
        load.wait()
        for src, dst in after:
            copy = pltpu.make_async_copy(src, dst, out_sems.at[len(started)])
            copy.start()
            started.append(copy)
    for copy in started:
        copy.wait()


def setup_kernel(cx, cells_ref, traces_ref, *refs):
    parts, (along_z_ref, along_y_ref, add_ref, joined_ref) = refs[:-4], refs[-4:]
    ny, nz = add_ref.shape[2:]
    size = parts[0].shape[0]
    for number, part in enumerate(parts):
        joined_ref[number * size : (number + 1) * size, :] = part[...]

    shape = along_z_ref.shape
    rows, cols = (lax.broadcasted_iota(jnp.int32, shape, d) for d in range(2))
    first, second = difference_matrix(shape, rows, cols, nz, CENTRE_Z)
    along_z_ref[...] = jnp.where(cols < nz, first, second).astype(jnp.bfloat16)
    shape = along_y_ref.shape
    rows, cols = (lax.broadcasted_iota(jnp.int32, shape, d) for d in range(2))
    first, second = difference_matrix(shape, cols, rows, ny, CENTRE_Y)
    here = lax.rem(rows, shape[1]) // ny == cols // ny
    along_y_ref[...] = jnp.where(here, jnp.where(rows < shape[1], first, second), 0.0).astype(jnp.bfloat16)

    tile = lax.axis_index("tile")
    count = cells_ref.shape[1]
    cells = cells_ref[...]
    reach = (STEPS - 1) * HALO
    at_row = cells // nz - (tile * cx - reach) * ny
    at_z = lax.rem(cells, nz)
    depth = lax.broadcasted_iota(jnp.int32, (nz, count), 0)
    deep = depth == at_z
    tile = lax.axis_index("tile")
    count = cells_ref.shape[1]
    cells = cells_ref[...]
    reach = (STEPS - 1) * HALO
    at_row = cells // nz - (tile * cx - reach) * ny
    at_z = lax.rem(cells, nz)
    depth = lax.broadcasted_iota(jnp.int32, (nz, count), 0)
    deep = depth == at_z
    values = []
    for step in range(STEPS):
        trace = traces_ref[0, pl.ds(STEPS - 1 - step, 1), :]
        high = trace.astype(jnp.bfloat16).astype(jnp.float32)
        values += [jnp.where(deep, high, 0.0), jnp.where(deep, trace - high, 0.0)]
    values = jnp.concatenate(values, axis=0).astype(jnp.bfloat16)
    chunk = 2 * HALO
    row = lax.broadcasted_iota(jnp.int32, (chunk * ny, count), 0)

    def body(c, carry):
        hot = jnp.where(at_row == row + c * (chunk * ny), 1.0, 0.0).astype(jnp.bfloat16)
        found = lax.dot_general(hot, values, (((1,), (1,)), ((), ())), preferred_element_type=jnp.float32)
        for step in range(STEPS):
            both = found[:, 2 * step * nz : (2 * step + 1) * nz] + found[:, (2 * step + 1) * nz : (2 * step + 2) * nz]
            add_ref[step, pl.ds(c * chunk, chunk)] = both.reshape(chunk, ny, nz)
        return carry

    lax.fori_loop(0, (cx + 2 * reach) // chunk, body, 0)


def matrix_differences(buf, i0, layers, along_z, along_y):
    ny, nz = buf.shape[1:]
    both = jnp.concatenate(two_terms(buf[pl.ds(i0, layers)].reshape(layers * ny, nz)), axis=1)
    from_z = jnp.dot(both, along_z, preferred_element_type=jnp.float32)
    size = along_y.shape[1]
    half = along_y.shape[0] // 2
    first_y, second = [], []
    for base in range(0, layers * ny, size):
        from_y = jnp.dot(along_y, both[base : base + size], preferred_element_type=jnp.float32)
        first_y.append(from_y[:size, :nz] + from_y[:size, nz:])
        if half == size:
            second.append(from_y[size:, :nz] + from_y[size:, nz:] + from_z[base : base + size, nz:])
    shape = (layers, ny, nz)
    first_y, first_z = jnp.concatenate(first_y, axis=0), from_z[:, :nz]
    if not second:
        return first_y.reshape(shape), first_z.reshape(shape), None
    return first_y.reshape(shape), first_z.reshape(shape), jnp.concatenate(second, axis=0).reshape(shape)


def layer_differences(buf, i, summed):
    first = None
    for k in range(1, 5):
        plus, minus = buf[i + k], buf[i - k]
        if summed is not None:
            summed = summed + SECOND[k - 1] * (plus + minus)
        term = FIRST[k - 1] * (plus - minus)
        first = term if first is None else first + term
    return first, summed


def on_segments(step, left, right, cx, work):
    work(cx, cx, True)
    reach = (STEPS - 1 - step) * HALO
    if reach:

        def body(number, carry):
            base = jnp.where(left & (number == 0), cx - reach, 2 * cx)
            work(pl.multiple_of(base, HALO), reach, False)
            return carry

        lax.fori_loop(0, left.astype(jnp.int32) + right.astype(jnp.int32), body, 0)


def march(pairs, slopes_ref, courant_ref, along_z, along_y, i0, layers, use):
    parts = [matrix_differences(cur, i0, layers, along_z, along_y) for cur, _ in pairs]
    for j in range(layers):
        i = i0 + j
        slopes = [slopes_ref[axis, i] for axis in range(3)]
        courant = courant_ref[i]
        steps = []
        for (cur, prev), (first_y, first_z, second) in zip(pairs, parts):
            first_x, applied = layer_differences(cur, i, second[j])
            applied = applied - slopes[0] * first_x - slopes[1] * first_y[j] - slopes[2] * first_z[j]
            steps.append((applied, 2.0 * cur[i] - prev[i] + courant * applied))
        for (_, prev), updated in zip(pairs, use(i, j, steps)):
            prev[i] = updated


def fill(buf, at, rows_ref, first_row, layers, keep):
    ny, nz = buf.shape[1:]
    part = rows_ref[pl.ds(first_row, layers * ny), :].astype(jnp.float32)
    if keep is not None:
        part = jnp.where(keep, part, 0.0)
    buf[pl.ds(at, layers)] = part.reshape(layers, ny, nz)


def fill_fields(now, before, own_now, own_before, from_a, from_b, base, side_a, side_b, cx, ny):
    fill(now, cx, own_now, 0, cx, None)
    fill(before, cx, own_before, 0, cx, None)
    reach = (STEPS - 1) * HALO
    for ref, (at, here, on) in ((from_a, side_a), (from_b, side_b)):
        fill(now, at, ref, base, cx, here)
        fill(before, jnp.where(at == 0, cx - reach, at), ref, base + cx * ny, reach, on)


def clear_sides(buf, left, right, cx):
    zero = jnp.zeros((HALO,) + buf.shape[1:], jnp.float32)

    @pl.when(jnp.logical_not(left))
    def _():
        buf[cx - HALO : cx] = zero

    @pl.when(jnp.logical_not(right))
    def _():
        buf[2 * cx : 2 * cx + HALO] = zero


def model_kernel(cx, ny, nz, shots, blocks, aperture_ref, *refs):
    model_refs = refs[: len(blocks)]
    along_z_ref, along_y_ref, slopes_ref, courant_ref, gain_ref, log_buf = refs[len(blocks) :]
    tile, own, left, right, side_a, side_b = layout(aperture_ref, cx)
    shot = lax.axis_index("shot")
    sides = ((cx, None), (side_a[0], side_a[1]), (side_b[0], side_b[1]))
    block_rows = ny // shots
    size = cx * block_rows

    @pl.when(own)
    def _():
        for ref, held in zip(model_refs, blocks):
            for number, (mask, place) in enumerate(held):
                y0 = pl.multiple_of((shot ^ mask) * block_rows, block_rows)
                at, here = sides[place]
                base = number * 2 * size
                speed = ref[pl.ds(base, size), :].astype(jnp.float32)
                courant = (speed * speed) * (1.0 / SCALE)
                courant_ref[pl.ds(at, cx), pl.ds(y0, block_rows), :] = courant.reshape(cx, block_rows, nz)
                if here is None:
                    gain = speed * (2.0 / SCALE)
                    gain_ref[:, pl.ds(y0, block_rows), :] = gain.reshape(cx, block_rows, nz)
                logs = jnp.log(ref[pl.ds(base + size, size), :].astype(jnp.float32))
                if here is not None:
                    logs = jnp.where(here, logs, 0.0)
                log_buf[pl.ds(at, cx), pl.ds(y0, block_rows), :] = logs.reshape(cx, block_rows, nz)
        along_z, along_y = along_z_ref[...], along_y_ref[...]

        def slopes(i0, layers, inner):
            first_y, first_z, _ = matrix_differences(log_buf, i0, layers, along_z, along_y)
            for j in range(layers):
                slopes_ref[0, i0 + j] = layer_differences(log_buf, i0 + j, None)[0] * (1.0 / 140.0)
                slopes_ref[1, i0 + j] = first_y[j] * (1.0 / 140.0)
                slopes_ref[2, i0 + j] = first_z[j] * (1.0 / 140.0)

        on_segments(0, left, right, cx, slopes)


def window_kernel(
    cx, ny, nz, order, aperture_ref, source_ref, wavelet_ref, along_z_ref, along_y_ref, slopes_ref, courant_ref, gain_ref, add_ref,
    now_ref, before_ref, end_ref, after_ref, from_a, from_b, sums_ref, wave_ref, adjoint_ref, now, before, end, after, applied_held,
    adjoint_held, image,
):
    tile, own, left, right, side_a, side_b = layout(aperture_ref, cx)
    shot = lax.axis_index("shot")
    block_rows = ny // len(order)

    @pl.when(jnp.logical_not(own))
    def _():
        wave_ref[...] = jnp.zeros_like(wave_ref)
        adjoint_ref[...] = jnp.zeros_like(adjoint_ref)
        sums_ref[...] = jnp.zeros_like(sums_ref)

    @pl.when(own)
    def _():
        half = from_a.shape[0] // 2
        fill_fields(now, before, now_ref, before_ref, from_a, from_b, 0, side_a, side_b, cx, ny)
        fill_fields(end, after, end_ref, after_ref, from_a, from_b, half, side_a, side_b, cx, ny)
        along_z, along_y = along_z_ref[...], along_y_ref[...]
        cell = source_ref[0]
        layer = cell // (ny * nz) - (tile - 1) * cx
        row = lax.rem(cell // nz, ny)
        depth = lax.rem(cell, nz)
        lanes = lax.broadcasted_iota(jnp.int32, (1, nz), 1)
        forward, adjoint = (now, before), (end, after)
        for step in range(STEPS):
            here = tuple((bufs[step % 2], bufs[(step + 1) % 2]) for bufs in (forward, adjoint))

            def work(i0, layers, inner, here=here, step=step):
                def use(i, j, steps):
                    (applied, wave), (_, back) = steps
                    back = back + add_ref[step, i - (cx - (STEPS - 1) * HALO)]
                    if inner and 2 * step < STEPS:
                        applied_held[step, j] = applied
                        adjoint_held[step, j] = back
                    elif inner:
                        other = STEPS - 1 - step
                        terms = applied * adjoint_held[other, j] + back * applied_held[other, j]
                        image[j] = terms if 2 * step == STEPS else image[j] + terms
                    return wave, back

                march(here, slopes_ref, courant_ref, along_z, along_y, i0, layers, use)

            on_segments(step, left, right, cx, work)
            reach = (STEPS - 1 - step) * HALO
            low = jnp.where(left, cx - reach, cx)
            high = jnp.where(right, 2 * cx + reach, 2 * cx)
            value = wavelet_ref[0, step]
            made = here[0][1]

            @pl.when((layer >= low) & (layer < high))
            def _(made=made, value=value):
                old = made[layer, pl.ds(row, 1), :]
                made[layer, pl.ds(row, 1), :] = old + jnp.where(lanes == depth, value, 0.0)

            if step == 0:
                clear_sides(now, left, right, cx)
                clear_sides(end, left, right, cx)
        wave_ref[...] = forward[STEPS % 2][cx : 2 * cx].reshape(cx * ny, nz)
        adjoint_ref[...] = adjoint[STEPS % 2][cx : 2 * cx].reshape(cx * ny, nz)
        for place, mask in enumerate(order):
            y0 = pl.multiple_of((shot ^ mask) * block_rows, block_rows)
            gain = gain_ref[:, pl.ds(y0, block_rows), :]
            sums_ref[place] = (gain * image[:, pl.ds(y0, block_rows), :]).reshape(cx * block_rows, nz)


def pairs(axis_sizes, kind):
    tiles, shots = axis_sizes
    found = []
    for tile in range(tiles):
        other = tile ^ 1 if kind == "a" else ((tile + 1) ^ 1) - 1
        for shot in range(shots):
            here = tile * shots + shot
            if 0 <= other < tiles:
                found.append((here, other * shots + shot))
            elif shots % 2 == 0:
                found.append((here, tile * shots + (shot ^ 1)))
    return found


def local(
    velocity, density, wave_now, wave_before, adjoint_end, adjoint_after, source_cell, source_wave, receiver_cell, residual_traces,
    aperture,
):
    cx, _, nz = velocity.shape
    ny = wave_now.shape[2]
    shots = lax.axis_size("shot")
    tiles = lax.axis_size("tile")
    rows = cx * ny
    params = pltpu.CompilerParams(vmem_limit_bytes=VMEM_BYTES)

    def swap(x, kind):
        return lax.ppermute(x, ("tile", "shot"), pairs((tiles, shots), kind))

    def cross(x, mask):
        return lax.ppermute(x, "shot", [(i, i ^ mask) for i in range(shots)])

    fields = [x.reshape(rows, nz) for x in (wave_now, wave_before, adjoint_end, adjoint_after)]
    message = jax.ShapeDtypeStruct((2 * (cx + (STEPS - 1) * HALO), ny, nz), jnp.bfloat16)
    model, to_a, to_b = pl.pallas_call(
        pack_kernel,
        out_shape=(jax.ShapeDtypeStruct((2 * cx,) + velocity.shape[1:], jnp.bfloat16), message, message),
        in_specs=[pl.BlockSpec(memory_space=pltpu.HBM)] * 6,
        out_specs=(pl.BlockSpec(memory_space=pltpu.HBM),) * 3,
        scratch_shapes=[pltpu.VMEM((2 * cx,) + velocity.shape[1:], jnp.bfloat16)]
        + [pltpu.VMEM((cx, ny, nz), jnp.bfloat16)] * 4
        + [pltpu.SemaphoreType.DMA((6,)), pltpu.SemaphoreType.DMA((9,))],
        compiler_params=pltpu.CompilerParams(vmem_limit_bytes=PACK_BYTES),
        cost_estimate=pl.CostEstimate(flops=0, bytes_accessed=2 * 2**20, transcendentals=0),
        name="pack",
    )(velocity, density, wave_now, wave_before, adjoint_end, adjoint_after)
    model, to_a, to_b = (x.reshape(-1, nz) for x in (model, to_a, to_b))

    from_a, from_b = swap(to_a, "a"), swap(to_b, "b")

    model_a, model_b = swap(model, "a"), swap(model, "b")
    high = shots // 2
    near = [([(0, 0)], model), ([(0, 1)], model_a), ([(0, 2)], model_b)]
    late = []
    if high:
        near.append(([(high, 0)], cross(model, high)))
        late.append(([(high, 1), (high, 2)], cross(jnp.concatenate([model_a, model_b], axis=0), high)))

    along_z, along_y, added, joined = pl.pallas_call(
        lambda *refs: setup_kernel(cx, *refs),
        out_shape=(
            jax.ShapeDtypeStruct((2 * nz, 2 * nz), jnp.bfloat16),
            jax.ShapeDtypeStruct((2 * HALO * ny, HALO * ny), jnp.bfloat16),
            jax.ShapeDtypeStruct((STEPS, cx + 2 * (STEPS - 1) * HALO, ny, nz), jnp.float32),
            jax.ShapeDtypeStruct((len(near) * model.shape[0], nz), jnp.bfloat16),
        ),
        in_specs=[vmem()] * (2 + len(near)),
        out_specs=(vmem(),) * 4,
        compiler_params=params,
        cost_estimate=pl.CostEstimate(flops=2 * 10**9, bytes_accessed=4 * 2**20, transcendentals=0),
        name="receivers",
    )(receiver_cell, residual_traces, *[block for _, block in near])

    near = [([name for names, _ in near for name in names], joined)]
    mask = high // 2
    while mask:
        moved = []
        for group in (near, late):
            names = [(m ^ mask, place) for held, _ in group for m, place in held]
            array = group[0][1] if len(group) == 1 else jnp.concatenate([block for _, block in group], axis=0)
            moved.append((names, cross(array, mask)))
        near, late = near + moved[:1], late + moved[1:]
        mask //= 2
    held = near + late

    field = pltpu.VMEM((3 * cx, ny, nz), jnp.float32)
    blocks = tuple(tuple(names) for names, _ in held)
    slopes, courant, gain = pl.pallas_call(
        lambda *refs: model_kernel(cx, ny, nz, shots, blocks, *refs),
        out_shape=(
            jax.ShapeDtypeStruct((3, 3 * cx, ny, nz), jnp.float32),
            jax.ShapeDtypeStruct((3 * cx, ny, nz), jnp.float32),
            jax.ShapeDtypeStruct((cx, ny, nz), jnp.float32),
        ),
        in_specs=[smem()] + [vmem()] * (len(held) + 2),
        out_specs=(vmem(),) * 3,
        scratch_shapes=[field],
        compiler_params=params,
        cost_estimate=pl.CostEstimate(flops=10**6, bytes_accessed=2**20, transcendentals=0),
        name="model",
    )(aperture, *[block for _, block in held], along_z, along_y)

    bits = []
    mask = 1
    while mask < shots:
        bits.append(mask)
        mask *= 2
    order = [0]
    for bit in reversed(bits):
        order = order + [m | bit for m in order]
    order = tuple(order)
    sums, wave_end, adjoint_start = pl.pallas_call(
        lambda *refs: window_kernel(cx, ny, nz, order, *refs),
        out_shape=(
            jax.ShapeDtypeStruct((shots, cx * (ny // shots), nz), jnp.float32),
            jax.ShapeDtypeStruct((rows, nz), jnp.float32),
            jax.ShapeDtypeStruct((rows, nz), jnp.float32),
        ),
        in_specs=[smem()] * 3 + [vmem()] * 12,
        out_specs=(vmem(),) * 3,
        scratch_shapes=[field] * 4 + [pltpu.VMEM((STEPS // 2, cx, ny, nz), jnp.float32)] * 2 + [pltpu.VMEM((cx, ny, nz), jnp.float32)],
        compiler_params=params,
        cost_estimate=pl.CostEstimate(flops=10**10, bytes_accessed=16 * 2**20, transcendentals=0),
        name="window",
    )(aperture, source_cell, source_wave, along_z, along_y, slopes, courant, gain, added, *fields, from_a, from_b)
    for bit in bits:
        half = sums.shape[0] // 2
        sums = sums[:half] + cross(sums[half:], bit)
    gradient = sums[0].reshape(cx, ny // shots, nz)
    ends = [x.astype(jnp.bfloat16).reshape(wave_now.shape) for x in (wave_end, adjoint_start)]
    return gradient, ends[0], ends[1]


def solution(mesh):
    stored = P(("parts", "tile"), "shot", None)
    field = P(("parts", "shot"), "tile", None, None)
    return jax.shard_map(
        local,
        mesh=mesh,
        in_specs=(
            stored, stored, field, field, field, field, P(("parts", "shot")), P(("parts", "shot"), None),
            P(("parts", "shot"), None), P(("parts", "shot"), None, None), P(("parts", "shot"), None),
        ),
        out_specs=(stored, field, field),
        check_vma=False,
    )
```

```python
import jax
import jax.numpy as jnp
from jax import lax
from jax.experimental import pallas as pl
from jax.experimental.pallas import tpu as pltpu
from jax.sharding import PartitionSpec as P

FIRST = (672.0, -168.0, 32.0, -3.0)
SECOND = (8064.0, -1008.0, 128.0, -9.0)
CENTRE_Z = -43008.0
CENTRE_Y = -42.0
SCALE = 5040.0
STEPS = 4
PACK_BYTES = 56 * 1024 * 1024
HALO = 4
VMEM_BYTES = 24 * 1024 * 1024


def vmem():
    return pl.BlockSpec(memory_space=pltpu.VMEM)


def smem():
    return pl.BlockSpec(memory_space=pltpu.SMEM)


def two_terms(values):
    high = values.astype(jnp.bfloat16)
    low = (values - high.astype(jnp.float32)).astype(jnp.bfloat16)
    return high, low


def is_active(aperture_ref, tile):
    found = aperture_ref[0, 0] == tile
    for slot in range(1, aperture_ref.shape[1]):
        found = found | (aperture_ref[0, slot] == tile)
    return found & (tile >= 0)


def layout(aperture_ref, cx):
    tiles = lax.axis_size("tile")
    tile = lax.axis_index("tile")
    even = lax.rem(tile, 2) == 0
    left = is_active(aperture_ref, tile - 1) & (tile > 0)
    right = is_active(aperture_ref, tile + 1) & (tile < tiles - 1)
    own = is_active(aperture_ref, tile)
    a_tile = jnp.where(even, tile + 1, tile - 1)
    b_tile = jnp.where(even, tile - 1, tile + 1)
    a_at = jnp.where(even, 2 * cx, 0)
    b_at = jnp.where(even, 0, 2 * cx)
    a_here = (a_tile >= 0) & (a_tile < tiles)
    b_here = (b_tile >= 0) & (b_tile < tiles)
    a_on = jnp.where(even, right, left)
    b_on = jnp.where(even, left, right)
    return tile, own, left, right, (a_at, a_here, a_on), (b_at, b_here, b_on)


def difference_matrix(shape, along, across, block, centre):
    ahead = lax.rem(along, block) - lax.rem(across, block)
    first = jnp.zeros(shape, jnp.float32)
    second = jnp.where(ahead == 0, centre, 0.0)
    for k in range(1, 5):
        first = jnp.where(ahead == k, FIRST[k - 1], jnp.where(ahead == -k, -FIRST[k - 1], first))
        second = jnp.where((ahead == k) | (ahead == -k), SECOND[k - 1], second)
    return first, second


def pack_kernel(*refs):
    (velocity_ref, density_ref, now_ref, before_ref, end_ref, after_ref, cells_ref, traces_ref, model_ref, a_ref, b_ref,
     receivers_ref, model_buf, now_buf, before_buf, end_buf, after_buf, cells_buf, traces_buf, receivers_buf, in_sems,
     out_sems) = refs
    cx = velocity_ref.shape[0]
    even = lax.rem(lax.axis_index("tile"), 2) == 0
    reach = (STEPS - 1) * HALO
    loads = [
        (velocity_ref, model_buf.at[0:cx]), (density_ref, model_buf.at[cx : 2 * cx]), (now_ref.at[0], now_buf),
        (before_ref.at[0], before_buf), (end_ref.at[0], end_buf), (after_ref.at[0], after_buf), (cells_ref, cells_buf),
        (traces_ref, traces_buf),
    ]
    loads = [pltpu.make_async_copy(src, dst, in_sems.at[number]) for number, (src, dst) in enumerate(loads)]
    for load in loads:
        load.start()
    stores = [[], [(model_buf, model_ref)], [], [], [], [], [], [(receivers_buf, receivers_ref)]]
    for side, out_ref in enumerate((a_ref, b_ref)):
        first = jnp.where(even == (side == 0), cx - reach, 0)
        base = 0
        for number, (whole, part) in ((2, (now_buf, before_buf)), (4, (end_buf, after_buf))):
            stores[number].append((whole, out_ref.at[base : base + cx]))
            stores[number + 1].append((part.at[pl.ds(first, reach)], out_ref.at[base + cx : base + cx + reach]))
            base += cx + reach
    started = []
    for number, (load, after) in enumerate(zip(loads, stores)):
        load.wait()
        if number == len(loads) - 1:
            receivers_buf[0:STEPS, :] = traces_buf[0]
            receivers_buf[STEPS : 2 * STEPS, :] = jnp.broadcast_to(cells_buf[...], traces_buf.shape[1:]).astype(jnp.float32)
        for src, dst in after:
            copy = pltpu.make_async_copy(src, dst, out_sems.at[len(started)])
            copy.start()
            started.append(copy)
    for copy in started:
        copy.wait()


def setup_kernel(cx, receivers_ref, *refs):
    parts, (along_z_ref, along_y_ref, add_ref, joined_ref) = refs[:-4], refs[-4:]
    ny, nz = add_ref.shape[2:]
    size = joined_ref.shape[0] // len(parts)
    for number, part in enumerate(parts):
        joined_ref[number * size : (number + 1) * size, :] = part[0:size, :]

    shape = along_z_ref.shape
    rows, cols = (lax.broadcasted_iota(jnp.int32, shape, d) for d in range(2))
    first, second = difference_matrix(shape, rows, cols, nz, CENTRE_Z)
    along_z_ref[...] = jnp.where(cols < nz, first, second).astype(jnp.bfloat16)
    shape = along_y_ref.shape
    rows, cols = (lax.broadcasted_iota(jnp.int32, shape, d) for d in range(2))
    first, second = difference_matrix(shape, cols, rows, ny, CENTRE_Y)
    here = lax.rem(rows, shape[1]) // ny == cols // ny
    along_y_ref[...] = jnp.where(here, jnp.where(rows < shape[1], first, second), 0.0).astype(jnp.bfloat16)

    tile = lax.axis_index("tile")
    count = receivers_ref.shape[1]
    cells = receivers_ref[STEPS : STEPS + 1, :].astype(jnp.int32)
    reach = (STEPS - 1) * HALO
    at_row = cells // nz - (tile * cx - reach) * ny
    at_z = lax.rem(cells, nz)
    depth = lax.broadcasted_iota(jnp.int32, (nz, count), 0)
    deep = depth == at_z
    tile = lax.axis_index("tile")
    count = receivers_ref.shape[1]
    cells = receivers_ref[STEPS : STEPS + 1, :].astype(jnp.int32)
    reach = (STEPS - 1) * HALO
    at_row = cells // nz - (tile * cx - reach) * ny
    at_z = lax.rem(cells, nz)
    depth = lax.broadcasted_iota(jnp.int32, (nz, count), 0)
    deep = depth == at_z
    values = []
    for step in range(STEPS):
        trace = receivers_ref[pl.ds(STEPS - 1 - step, 1), :]
        high = trace.astype(jnp.bfloat16).astype(jnp.float32)
        values += [jnp.where(deep, high, 0.0), jnp.where(deep, trace - high, 0.0)]
    values = jnp.concatenate(values, axis=0).astype(jnp.bfloat16)
    chunk = 2 * HALO
    row = lax.broadcasted_iota(jnp.int32, (chunk * ny, count), 0)

    def body(c, carry):
        hot = jnp.where(at_row == row + c * (chunk * ny), 1.0, 0.0).astype(jnp.bfloat16)
        found = lax.dot_general(hot, values, (((1,), (1,)), ((), ())), preferred_element_type=jnp.float32)
        for step in range(STEPS):
            both = found[:, 2 * step * nz : (2 * step + 1) * nz] + found[:, (2 * step + 1) * nz : (2 * step + 2) * nz]
            add_ref[step, pl.ds(c * chunk, chunk)] = both.reshape(chunk, ny, nz)
        return carry

    lax.fori_loop(0, (cx + 2 * reach) // chunk, body, 0)


def matrix_differences(buf, i0, layers, along_z, along_y):
    ny, nz = buf.shape[1:]
    both = jnp.concatenate(two_terms(buf[pl.ds(i0, layers)].reshape(layers * ny, nz)), axis=1)
    from_z = jnp.dot(both, along_z, preferred_element_type=jnp.float32)
    size = along_y.shape[1]
    half = along_y.shape[0] // 2
    first_y, second = [], []
    for base in range(0, layers * ny, size):
        from_y = jnp.dot(along_y, both[base : base + size], preferred_element_type=jnp.float32)
        first_y.append(from_y[:size, :nz] + from_y[:size, nz:])
        if half == size:
            second.append(from_y[size:, :nz] + from_y[size:, nz:] + from_z[base : base + size, nz:])
    shape = (layers, ny, nz)
    first_y, first_z = jnp.concatenate(first_y, axis=0), from_z[:, :nz]
    if not second:
        return first_y.reshape(shape), first_z.reshape(shape), None
    return first_y.reshape(shape), first_z.reshape(shape), jnp.concatenate(second, axis=0).reshape(shape)


def layer_differences(buf, i, summed):
    first = None
    for k in range(1, 5):
        plus, minus = buf[i + k], buf[i - k]
        if summed is not None:
            summed = summed + SECOND[k - 1] * (plus + minus)
        term = FIRST[k - 1] * (plus - minus)
        first = term if first is None else first + term
    return first, summed


def on_segments(step, left, right, cx, work):
    work(cx, cx, True)
    reach = (STEPS - 1 - step) * HALO
    if reach:

        def body(number, carry):
            base = jnp.where(left & (number == 0), cx - reach, 2 * cx)
            work(pl.multiple_of(base, HALO), reach, False)
            return carry

        lax.fori_loop(0, left.astype(jnp.int32) + right.astype(jnp.int32), body, 0)


def march(pairs, slopes_ref, courant_ref, along_z, along_y, i0, layers, use):
    parts = [matrix_differences(cur, i0, layers, along_z, along_y) for cur, _ in pairs]
    for j in range(layers):
        i = i0 + j
        slopes = [slopes_ref[axis, i] for axis in range(3)]
        courant = courant_ref[i]
        steps = []
        for (cur, prev), (first_y, first_z, second) in zip(pairs, parts):
            first_x, applied = layer_differences(cur, i, second[j])
            applied = applied - slopes[0] * first_x - slopes[1] * first_y[j] - slopes[2] * first_z[j]
            steps.append((applied, 2.0 * cur[i] - prev[i] + courant * applied))
        for (_, prev), updated in zip(pairs, use(i, j, steps)):
            prev[i] = updated


def fill(buf, at, rows_ref, first_row, layers, keep):
    ny, nz = buf.shape[1:]
    part = rows_ref[pl.ds(first_row, layers * ny), :].astype(jnp.float32)
    if keep is not None:
        part = jnp.where(keep, part, 0.0)
    buf[pl.ds(at, layers)] = part.reshape(layers, ny, nz)


def fill_fields(now, before, own_now, own_before, from_a, from_b, base, side_a, side_b, cx, ny):
    fill(now, cx, own_now, 0, cx, None)
    fill(before, cx, own_before, 0, cx, None)
    reach = (STEPS - 1) * HALO
    for ref, (at, here, on) in ((from_a, side_a), (from_b, side_b)):
        fill(now, at, ref, base, cx, here)
        fill(before, jnp.where(at == 0, cx - reach, at), ref, base + cx * ny, reach, on)


def clear_sides(buf, left, right, cx):
    zero = jnp.zeros((HALO,) + buf.shape[1:], jnp.float32)

    @pl.when(jnp.logical_not(left))
    def _():
        buf[cx - HALO : cx] = zero

    @pl.when(jnp.logical_not(right))
    def _():
        buf[2 * cx : 2 * cx + HALO] = zero


def model_kernel(cx, ny, nz, shots, blocks, aperture_ref, *refs):
    model_refs = refs[: len(blocks)]
    along_z_ref, along_y_ref, slopes_ref, courant_ref, gain_ref, log_buf = refs[len(blocks) :]
    tile, own, left, right, side_a, side_b = layout(aperture_ref, cx)
    shot = lax.axis_index("shot")
    sides = ((cx, None), (side_a[0], side_a[1]), (side_b[0], side_b[1]))
    block_rows = ny // shots
    size = cx * block_rows

    @pl.when(own)
    def _():
        for ref, held in zip(model_refs, blocks):
            for number, (mask, place) in enumerate(held):
                y0 = pl.multiple_of((shot ^ mask) * block_rows, block_rows)
                at, here = sides[place]
                base = number * 2 * size
                speed = ref[pl.ds(base, size), :].astype(jnp.float32)
                courant = (speed * speed) * (1.0 / SCALE)
                courant_ref[pl.ds(at, cx), pl.ds(y0, block_rows), :] = courant.reshape(cx, block_rows, nz)
                if here is None:
                    gain = speed * (2.0 / SCALE)
                    gain_ref[:, pl.ds(y0, block_rows), :] = gain.reshape(cx, block_rows, nz)
                logs = jnp.log(ref[pl.ds(base + size, size), :].astype(jnp.float32))
                if here is not None:
                    logs = jnp.where(here, logs, 0.0)
                log_buf[pl.ds(at, cx), pl.ds(y0, block_rows), :] = logs.reshape(cx, block_rows, nz)
        along_z, along_y = along_z_ref[...], along_y_ref[...]

        def slopes(i0, layers, inner):
            first_y, first_z, _ = matrix_differences(log_buf, i0, layers, along_z, along_y)
            for j in range(layers):
                slopes_ref[0, i0 + j] = layer_differences(log_buf, i0 + j, None)[0] * (1.0 / 140.0)
                slopes_ref[1, i0 + j] = first_y[j] * (1.0 / 140.0)
                slopes_ref[2, i0 + j] = first_z[j] * (1.0 / 140.0)

        on_segments(0, left, right, cx, slopes)


def window_kernel(
    cx, ny, nz, order, aperture_ref, source_ref, wavelet_ref, along_z_ref, along_y_ref, slopes_ref, courant_ref, gain_ref, add_ref,
    now_ref, before_ref, end_ref, after_ref, from_a, from_b, sums_ref, wave_ref, adjoint_ref, now, before, end, after, applied_held,
    adjoint_held, image,
):
    tile, own, left, right, side_a, side_b = layout(aperture_ref, cx)
    shot = lax.axis_index("shot")
    block_rows = ny // len(order)

    @pl.when(jnp.logical_not(own))
    def _():
        wave_ref[...] = jnp.zeros_like(wave_ref)
        adjoint_ref[...] = jnp.zeros_like(adjoint_ref)
        sums_ref[...] = jnp.zeros_like(sums_ref)

    @pl.when(own)
    def _():
        half = from_a.shape[0] // 2
        fill_fields(now, before, now_ref, before_ref, from_a, from_b, 0, side_a, side_b, cx, ny)
        fill_fields(end, after, end_ref, after_ref, from_a, from_b, half, side_a, side_b, cx, ny)
        along_z, along_y = along_z_ref[...], along_y_ref[...]
        cell = source_ref[0]
        layer = cell // (ny * nz) - (tile - 1) * cx
        row = lax.rem(cell // nz, ny)
        depth = lax.rem(cell, nz)
        lanes = lax.broadcasted_iota(jnp.int32, (1, nz), 1)
        forward, adjoint = (now, before), (end, after)
        for step in range(STEPS):
            here = tuple((bufs[step % 2], bufs[(step + 1) % 2]) for bufs in (forward, adjoint))

            def work(i0, layers, inner, here=here, step=step):
                def use(i, j, steps):
                    (applied, wave), (_, back) = steps
                    back = back + add_ref[step, i - (cx - (STEPS - 1) * HALO)]
                    if inner and 2 * step < STEPS:
                        applied_held[step, j] = applied
                        adjoint_held[step, j] = back
                    elif inner:
                        other = STEPS - 1 - step
                        terms = applied * adjoint_held[other, j] + back * applied_held[other, j]
                        image[j] = terms if 2 * step == STEPS else image[j] + terms
                    return wave, back

                march(here, slopes_ref, courant_ref, along_z, along_y, i0, layers, use)

            on_segments(step, left, right, cx, work)
            reach = (STEPS - 1 - step) * HALO
            low = jnp.where(left, cx - reach, cx)
            high = jnp.where(right, 2 * cx + reach, 2 * cx)
            value = wavelet_ref[0, step]
            made = here[0][1]

            @pl.when((layer >= low) & (layer < high))
            def _(made=made, value=value):
                old = made[layer, pl.ds(row, 1), :]
                made[layer, pl.ds(row, 1), :] = old + jnp.where(lanes == depth, value, 0.0)

            if step == 0:
                clear_sides(now, left, right, cx)
                clear_sides(end, left, right, cx)
        wave_ref[...] = forward[STEPS % 2][cx : 2 * cx].reshape(cx * ny, nz)
        adjoint_ref[...] = adjoint[STEPS % 2][cx : 2 * cx].reshape(cx * ny, nz)
        for place, mask in enumerate(order):
            y0 = pl.multiple_of((shot ^ mask) * block_rows, block_rows)
            gain = gain_ref[:, pl.ds(y0, block_rows), :]
            sums_ref[place] = (gain * image[:, pl.ds(y0, block_rows), :]).reshape(cx * block_rows, nz)


def pairs(axis_sizes, kind):
    tiles, shots = axis_sizes
    found = []
    for tile in range(tiles):
        other = tile ^ 1 if kind == "a" else ((tile + 1) ^ 1) - 1
        for shot in range(shots):
            here = tile * shots + shot
            if 0 <= other < tiles:
                found.append((here, other * shots + shot))
            elif shots % 2 == 0:
                found.append((here, tile * shots + (shot ^ 1)))
    return found


def local(
    velocity, density, wave_now, wave_before, adjoint_end, adjoint_after, source_cell, source_wave, receiver_cell, residual_traces,
    aperture,
):
    cx, _, nz = velocity.shape
    ny = wave_now.shape[2]
    shots = lax.axis_size("shot")
    tiles = lax.axis_size("tile")
    rows = cx * ny
    params = pltpu.CompilerParams(vmem_limit_bytes=VMEM_BYTES)

    def swap(x, kind):
        return lax.ppermute(x, ("tile", "shot"), pairs((tiles, shots), kind))

    def cross(x, mask):
        return lax.ppermute(x, "shot", [(i, i ^ mask) for i in range(shots)])

    fields = [x.reshape(rows, nz) for x in (wave_now, wave_before, adjoint_end, adjoint_after)]
    message = jax.ShapeDtypeStruct((2 * (cx + (STEPS - 1) * HALO), ny, nz), jnp.bfloat16)
    model, to_a, to_b, receivers = pl.pallas_call(
        pack_kernel,
        out_shape=(
            jax.ShapeDtypeStruct((2 * cx,) + velocity.shape[1:], jnp.bfloat16), message, message,
            jax.ShapeDtypeStruct((2 * STEPS, receiver_cell.shape[1]), jnp.float32),
        ),
        in_specs=[pl.BlockSpec(memory_space=pltpu.HBM)] * 8,
        out_specs=(pl.BlockSpec(memory_space=pltpu.HBM),) * 4,
        scratch_shapes=[pltpu.VMEM((2 * cx,) + velocity.shape[1:], jnp.bfloat16)]
        + [pltpu.VMEM((cx, ny, nz), jnp.bfloat16)] * 4
        + [
            pltpu.VMEM(receiver_cell.shape, jnp.int32),
            pltpu.VMEM(residual_traces.shape, jnp.float32),
            pltpu.VMEM((2 * STEPS, receiver_cell.shape[1]), jnp.float32),
            pltpu.SemaphoreType.DMA((8,)),
            pltpu.SemaphoreType.DMA((10,)),
        ],
        compiler_params=pltpu.CompilerParams(vmem_limit_bytes=PACK_BYTES),
        cost_estimate=pl.CostEstimate(flops=0, bytes_accessed=2 * 2**20, transcendentals=0),
        name="pack",
    )(velocity, density, wave_now, wave_before, adjoint_end, adjoint_after, receiver_cell, residual_traces)
    model, to_a, to_b = (x.reshape(-1, nz) for x in (model, to_a, to_b))

    from_a, from_b = swap(to_a, "a"), swap(to_b, "b")

    model_a, model_b = swap(model, "a"), swap(model, "b")
    high = shots // 2
    block_rows = model.shape[0]
    own = jnp.concatenate([model, model_a[: 2 * HALO * 2]], axis=0)
    near = [([(0, 0)], own), ([(0, 1)], model_a), ([(0, 2)], model_b)]
    late = []
    if high:
        late.append(([(high, 1), (high, 2)], cross(jnp.concatenate([model_a, model_b], axis=0), high)))
        late.append(([(high, 0)], cross(own, high)[:block_rows]))

    along_z, along_y, added, joined = pl.pallas_call(
        lambda *refs: setup_kernel(cx, *refs),
        out_shape=(
            jax.ShapeDtypeStruct((2 * nz, 2 * nz), jnp.bfloat16),
            jax.ShapeDtypeStruct((2 * HALO * ny, HALO * ny), jnp.bfloat16),
            jax.ShapeDtypeStruct((STEPS, cx + 2 * (STEPS - 1) * HALO, ny, nz), jnp.float32),
            jax.ShapeDtypeStruct((len(near) * block_rows, nz), jnp.bfloat16),
        ),
        in_specs=[vmem()] * (1 + len(near)),
        out_specs=(vmem(),) * 4,
        compiler_params=params,
        cost_estimate=pl.CostEstimate(flops=2 * 10**9, bytes_accessed=4 * 2**20, transcendentals=0),
        name="receivers",
    )(receivers, *[block for _, block in near])

    near = [([name for names, _ in near for name in names], joined)]
    mask = high // 2
    while mask:
        moved = []
        for group in (near, late):
            names = [(m ^ mask, place) for held, _ in group for m, place in held]
            array = group[0][1] if len(group) == 1 else jnp.concatenate([block for _, block in group], axis=0)
            moved.append((names, cross(array, mask)))
        near, late = near + moved[:1], late + moved[1:]
        mask //= 2
    held = near + late

    field = pltpu.VMEM((3 * cx, ny, nz), jnp.float32)
    blocks = tuple(tuple(names) for names, _ in held)
    slopes, courant, gain = pl.pallas_call(
        lambda *refs: model_kernel(cx, ny, nz, shots, blocks, *refs),
        out_shape=(
            jax.ShapeDtypeStruct((3, 3 * cx, ny, nz), jnp.float32),
            jax.ShapeDtypeStruct((3 * cx, ny, nz), jnp.float32),
            jax.ShapeDtypeStruct((cx, ny, nz), jnp.float32),
        ),
        in_specs=[smem()] + [vmem()] * (len(held) + 2),
        out_specs=(vmem(),) * 3,
        scratch_shapes=[field],
        compiler_params=params,
        cost_estimate=pl.CostEstimate(flops=10**6, bytes_accessed=2**20, transcendentals=0),
        name="model",
    )(aperture, *[block for _, block in held], along_z, along_y)

    bits = []
    mask = 1
    while mask < shots:
        bits.append(mask)
        mask *= 2
    order = [0]
    for bit in reversed(bits):
        order = order + [m | bit for m in order]
    order = tuple(order)
    sums, wave_end, adjoint_start = pl.pallas_call(
        lambda *refs: window_kernel(cx, ny, nz, order, *refs),
        out_shape=(
            jax.ShapeDtypeStruct((shots, cx * (ny // shots), nz), jnp.float32),
            jax.ShapeDtypeStruct((rows, nz), jnp.float32),
            jax.ShapeDtypeStruct((rows, nz), jnp.float32),
        ),
        in_specs=[smem()] * 3 + [vmem()] * 12,
        out_specs=(vmem(),) * 3,
        scratch_shapes=[field] * 4 + [pltpu.VMEM((STEPS // 2, cx, ny, nz), jnp.float32)] * 2 + [pltpu.VMEM((cx, ny, nz), jnp.float32)],
        compiler_params=params,
        cost_estimate=pl.CostEstimate(flops=10**10, bytes_accessed=16 * 2**20, transcendentals=0),
        name="window",
    )(aperture, source_cell, source_wave, along_z, along_y, slopes, courant, gain, added, *fields, from_a, from_b)
    for bit in bits:
        half = sums.shape[0] // 2
        sums = sums[:half] + cross(sums[half:], bit)
    gradient = sums[0].reshape(cx, ny // shots, nz)
    ends = [x.astype(jnp.bfloat16).reshape(wave_now.shape) for x in (wave_end, adjoint_start)]
    return gradient, ends[0], ends[1]


def solution(mesh):
    stored = P(("parts", "tile"), "shot", None)
    field = P(("parts", "shot"), "tile", None, None)
    return jax.shard_map(
        local,
        mesh=mesh,
        in_specs=(
            stored, stored, field, field, field, field, P(("parts", "shot")), P(("parts", "shot"), None),
            P(("parts", "shot"), None), P(("parts", "shot"), None, None), P(("parts", "shot"), None),
        ),
        out_specs=(stored, field, field),
        check_vma=False,
    )
```

```python
import jax
import jax.numpy as jnp
from jax import lax
from jax.experimental import pallas as pl
from jax.experimental.pallas import tpu as pltpu
from jax.sharding import PartitionSpec as P

FIRST = (672.0, -168.0, 32.0, -3.0)
SECOND = (8064.0, -1008.0, 128.0, -9.0)
CENTRE_Z = -43008.0
CENTRE_Y = -42.0
SCALE = 5040.0
STEPS = 4
RIDERS = 16
PACK_BYTES = 56 * 1024 * 1024
HALO = 4
VMEM_BYTES = 24 * 1024 * 1024


def vmem():
    return pl.BlockSpec(memory_space=pltpu.VMEM)


def smem():
    return pl.BlockSpec(memory_space=pltpu.SMEM)


def two_terms(values):
    high = values.astype(jnp.bfloat16)
    low = (values - high.astype(jnp.float32)).astype(jnp.bfloat16)
    return high, low


def is_active(aperture_ref, tile):
    found = aperture_ref[0, 0] == tile
    for slot in range(1, aperture_ref.shape[1]):
        found = found | (aperture_ref[0, slot] == tile)
    return found & (tile >= 0)


def layout(aperture_ref, cx):
    tiles = lax.axis_size("tile")
    tile = lax.axis_index("tile")
    even = lax.rem(tile, 2) == 0
    left = is_active(aperture_ref, tile - 1) & (tile > 0)
    right = is_active(aperture_ref, tile + 1) & (tile < tiles - 1)
    own = is_active(aperture_ref, tile)
    a_tile = jnp.where(even, tile + 1, tile - 1)
    b_tile = jnp.where(even, tile - 1, tile + 1)
    a_at = jnp.where(even, 2 * cx, 0)
    b_at = jnp.where(even, 0, 2 * cx)
    a_here = (a_tile >= 0) & (a_tile < tiles)
    b_here = (b_tile >= 0) & (b_tile < tiles)
    a_on = jnp.where(even, right, left)
    b_on = jnp.where(even, left, right)
    return tile, own, left, right, (a_at, a_here, a_on), (b_at, b_here, b_on)


def difference_matrix(shape, along, across, block, centre):
    ahead = lax.rem(along, block) - lax.rem(across, block)
    first = jnp.zeros(shape, jnp.float32)
    second = jnp.where(ahead == 0, centre, 0.0)
    for k in range(1, 5):
        first = jnp.where(ahead == k, FIRST[k - 1], jnp.where(ahead == -k, -FIRST[k - 1], first))
        second = jnp.where((ahead == k) | (ahead == -k), SECOND[k - 1], second)
    return first, second


def pack_kernel(*refs):
    (velocity_ref, density_ref, now_ref, before_ref, end_ref, after_ref, cells_ref, traces_ref, model_ref, a_ref, b_ref,
     receivers_ref, model_buf, now_buf, before_buf, end_buf, after_buf, cells_buf, traces_buf, receivers_buf, in_sems,
     out_sems) = refs
    cx = velocity_ref.shape[0]
    even = lax.rem(lax.axis_index("tile"), 2) == 0
    reach = (STEPS - 1) * HALO
    loads = [
        (velocity_ref, model_buf.at[0:cx]), (density_ref, model_buf.at[cx : 2 * cx]), (now_ref.at[0], now_buf),
        (before_ref.at[0], before_buf), (end_ref.at[0], end_buf), (after_ref.at[0], after_buf), (cells_ref, cells_buf),
        (traces_ref, traces_buf),
    ]
    loads = [pltpu.make_async_copy(src, dst, in_sems.at[number]) for number, (src, dst) in enumerate(loads)]
    for load in loads:
        load.start()
    stores = [[], [(model_buf, model_ref)], [], [], [], [], [], [(receivers_buf, receivers_ref)]]
    for side, out_ref in enumerate((a_ref, b_ref)):
        first = jnp.where(even == (side == 0), cx - reach, 0)
        base = 0
        for number, (whole, part) in ((2, (now_buf, before_buf)), (4, (end_buf, after_buf))):
            stores[number].append((whole, out_ref.at[base : base + cx]))
            stores[number + 1].append((part.at[pl.ds(first, reach)], out_ref.at[base + cx : base + cx + reach]))
            base += cx + reach
    started = []
    for number, (load, after) in enumerate(zip(loads, stores)):
        load.wait()
        if number == len(loads) - 1:
            receivers_buf[0:STEPS, :] = traces_buf[0]
            receivers_buf[STEPS : 2 * STEPS, :] = jnp.broadcast_to(cells_buf[...], traces_buf.shape[1:]).astype(jnp.float32)
        for src, dst in after:
            copy = pltpu.make_async_copy(src, dst, out_sems.at[len(started)])
            copy.start()
            started.append(copy)
    for copy in started:
        copy.wait()


def setup_kernel(cx, receivers_ref, *refs):
    parts, (along_z_ref, along_y_ref, add_ref, joined_ref) = refs[:-4], refs[-4:]
    ny, nz = add_ref.shape[2:]
    size = joined_ref.shape[0] // len(parts)
    for number, part in enumerate(parts):
        joined_ref[number * size : (number + 1) * size, :] = part[0:size, :]

    shape = along_z_ref.shape
    rows, cols = (lax.broadcasted_iota(jnp.int32, shape, d) for d in range(2))
    first, second = difference_matrix(shape, rows, cols, nz, CENTRE_Z)
    along_z_ref[...] = jnp.where(cols < nz, first, second).astype(jnp.bfloat16)
    shape = along_y_ref.shape
    rows, cols = (lax.broadcasted_iota(jnp.int32, shape, d) for d in range(2))
    first, second = difference_matrix(shape, cols, rows, ny, CENTRE_Y)
    here = lax.rem(rows, shape[1]) // ny == cols // ny
    along_y_ref[...] = jnp.where(here, jnp.where(rows < shape[1], first, second), 0.0).astype(jnp.bfloat16)

    tile = lax.axis_index("tile")
    count = receivers_ref.shape[1]
    cells = receivers_ref[STEPS : STEPS + 1, :].astype(jnp.int32)
    reach = (STEPS - 1) * HALO
    at_row = cells // nz - (tile * cx - reach) * ny
    at_z = lax.rem(cells, nz)
    depth = lax.broadcasted_iota(jnp.int32, (nz, count), 0)
    deep = depth == at_z
    tile = lax.axis_index("tile")
    count = receivers_ref.shape[1]
    cells = receivers_ref[STEPS : STEPS + 1, :].astype(jnp.int32)
    reach = (STEPS - 1) * HALO
    at_row = cells // nz - (tile * cx - reach) * ny
    at_z = lax.rem(cells, nz)
    depth = lax.broadcasted_iota(jnp.int32, (nz, count), 0)
    deep = depth == at_z
    values = []
    for step in range(STEPS):
        trace = receivers_ref[pl.ds(STEPS - 1 - step, 1), :]
        high = trace.astype(jnp.bfloat16).astype(jnp.float32)
        values += [jnp.where(deep, high, 0.0), jnp.where(deep, trace - high, 0.0)]
    values = jnp.concatenate(values, axis=0).astype(jnp.bfloat16)
    chunk = 2 * HALO
    row = lax.broadcasted_iota(jnp.int32, (chunk * ny, count), 0)

    def body(c, carry):
        hot = jnp.where(at_row == row + c * (chunk * ny), 1.0, 0.0).astype(jnp.bfloat16)
        found = lax.dot_general(hot, values, (((1,), (1,)), ((), ())), preferred_element_type=jnp.float32)
        for step in range(STEPS):
            both = found[:, 2 * step * nz : (2 * step + 1) * nz] + found[:, (2 * step + 1) * nz : (2 * step + 2) * nz]
            add_ref[step, pl.ds(c * chunk, chunk)] = both.reshape(chunk, ny, nz)
        return carry

    lax.fori_loop(0, (cx + 2 * reach) // chunk, body, 0)


def matrix_differences(buf, i0, layers, along_z, along_y):
    ny, nz = buf.shape[1:]
    both = jnp.concatenate(two_terms(buf[pl.ds(i0, layers)].reshape(layers * ny, nz)), axis=1)
    from_z = jnp.dot(both, along_z, preferred_element_type=jnp.float32)
    size = along_y.shape[1]
    half = along_y.shape[0] // 2
    first_y, second = [], []
    for base in range(0, layers * ny, size):
        from_y = jnp.dot(along_y, both[base : base + size], preferred_element_type=jnp.float32)
        first_y.append(from_y[:size, :nz] + from_y[:size, nz:])
        if half == size:
            second.append(from_y[size:, :nz] + from_y[size:, nz:] + from_z[base : base + size, nz:])
    shape = (layers, ny, nz)
    first_y, first_z = jnp.concatenate(first_y, axis=0), from_z[:, :nz]
    if not second:
        return first_y.reshape(shape), first_z.reshape(shape), None
    return first_y.reshape(shape), first_z.reshape(shape), jnp.concatenate(second, axis=0).reshape(shape)


def layer_differences(buf, i, summed):
    first = None
    for k in range(1, 5):
        plus, minus = buf[i + k], buf[i - k]
        if summed is not None:
            summed = summed + SECOND[k - 1] * (plus + minus)
        term = FIRST[k - 1] * (plus - minus)
        first = term if first is None else first + term
    return first, summed


def on_segments(step, left, right, cx, work):
    work(cx, cx, True)
    reach = (STEPS - 1 - step) * HALO
    if reach:

        def body(number, carry):
            base = jnp.where(left & (number == 0), cx - reach, 2 * cx)
            work(pl.multiple_of(base, HALO), reach, False)
            return carry

        lax.fori_loop(0, left.astype(jnp.int32) + right.astype(jnp.int32), body, 0)


def march(pairs, slopes_ref, courant_ref, along_z, along_y, i0, layers, use):
    parts = [matrix_differences(cur, i0, layers, along_z, along_y) for cur, _ in pairs]
    for j in range(layers):
        i = i0 + j
        slopes = [slopes_ref[axis, i] for axis in range(3)]
        courant = courant_ref[i]
        steps = []
        for (cur, prev), (first_y, first_z, second) in zip(pairs, parts):
            first_x, applied = layer_differences(cur, i, second[j])
            applied = applied - slopes[0] * first_x - slopes[1] * first_y[j] - slopes[2] * first_z[j]
            steps.append((applied, 2.0 * cur[i] - prev[i] + courant * applied))
        for (_, prev), updated in zip(pairs, use(i, j, steps)):
            prev[i] = updated


def fill(buf, at, rows_ref, first_row, layers, keep):
    ny, nz = buf.shape[1:]
    part = rows_ref[pl.ds(first_row, layers * ny), :].astype(jnp.float32)
    if keep is not None:
        part = jnp.where(keep, part, 0.0)
    buf[pl.ds(at, layers)] = part.reshape(layers, ny, nz)


def fill_fields(now, before, own_now, own_before, from_a, from_b, base, side_a, side_b, cx, ny):
    fill(now, cx, own_now, 0, cx, None)
    fill(before, cx, own_before, 0, cx, None)
    reach = (STEPS - 1) * HALO
    for ref, (at, here, on) in ((from_a, side_a), (from_b, side_b)):
        fill(now, at, ref, base, cx, here)
        fill(before, jnp.where(at == 0, cx - reach, at), ref, base + cx * ny, reach, on)


def clear_sides(buf, left, right, cx):
    zero = jnp.zeros((HALO,) + buf.shape[1:], jnp.float32)

    @pl.when(jnp.logical_not(left))
    def _():
        buf[cx - HALO : cx] = zero

    @pl.when(jnp.logical_not(right))
    def _():
        buf[2 * cx : 2 * cx + HALO] = zero


def model_kernel(cx, ny, nz, shots, blocks, aperture_ref, *refs):
    model_refs = refs[: len(blocks)]
    along_z_ref, along_y_ref, slopes_ref, courant_ref, gain_ref, log_buf = refs[len(blocks) :]
    tile, own, left, right, side_a, side_b = layout(aperture_ref, cx)
    shot = lax.axis_index("shot")
    sides = ((cx, None), (side_a[0], side_a[1]), (side_b[0], side_b[1]))
    block_rows = ny // shots
    size = cx * block_rows

    @pl.when(own)
    def _():
        for ref, held in zip(model_refs, blocks):
            for number, (mask, place) in enumerate(held):
                y0 = pl.multiple_of((shot ^ mask) * block_rows, block_rows)
                at, here = sides[place]
                base = number * 2 * size
                speed = ref[pl.ds(base, size), :].astype(jnp.float32)
                courant = (speed * speed) * (1.0 / SCALE)
                courant_ref[pl.ds(at, cx), pl.ds(y0, block_rows), :] = courant.reshape(cx, block_rows, nz)
                if here is None:
                    gain = speed * (2.0 / SCALE)
                    gain_ref[:, pl.ds(y0, block_rows), :] = gain.reshape(cx, block_rows, nz)
                logs = jnp.log(ref[pl.ds(base + size, size), :].astype(jnp.float32))
                if here is not None:
                    logs = jnp.where(here, logs, 0.0)
                log_buf[pl.ds(at, cx), pl.ds(y0, block_rows), :] = logs.reshape(cx, block_rows, nz)
        along_z, along_y = along_z_ref[...], along_y_ref[...]

        def slopes(i0, layers, inner):
            first_y, first_z, _ = matrix_differences(log_buf, i0, layers, along_z, along_y)
            for j in range(layers):
                slopes_ref[0, i0 + j] = layer_differences(log_buf, i0 + j, None)[0] * (1.0 / 140.0)
                slopes_ref[1, i0 + j] = first_y[j] * (1.0 / 140.0)
                slopes_ref[2, i0 + j] = first_z[j] * (1.0 / 140.0)

        on_segments(0, left, right, cx, slopes)


def window_kernel(
    cx, ny, nz, order, aperture_ref, source_ref, wavelet_ref, along_z_ref, along_y_ref, slopes_ref, courant_ref, gain_ref, add_ref,
    now_ref, before_ref, end_ref, after_ref, from_a, from_b, sums_ref, wave_ref, adjoint_ref, now, before, end, after, applied_held,
    adjoint_held, image,
):
    tile, own, left, right, side_a, side_b = layout(aperture_ref, cx)
    shot = lax.axis_index("shot")
    block_rows = ny // len(order)

    @pl.when(jnp.logical_not(own))
    def _():
        wave_ref[...] = jnp.zeros_like(wave_ref)
        adjoint_ref[...] = jnp.zeros_like(adjoint_ref)
        sums_ref[...] = jnp.zeros_like(sums_ref)

    @pl.when(own)
    def _():
        half = from_a.shape[0] // 2
        fill_fields(now, before, now_ref, before_ref, from_a, from_b, 0, side_a, side_b, cx, ny)
        fill_fields(end, after, end_ref, after_ref, from_a, from_b, half, side_a, side_b, cx, ny)
        along_z, along_y = along_z_ref[...], along_y_ref[...]
        cell = source_ref[0]
        layer = cell // (ny * nz) - (tile - 1) * cx
        row = lax.rem(cell // nz, ny)
        depth = lax.rem(cell, nz)
        lanes = lax.broadcasted_iota(jnp.int32, (1, nz), 1)
        forward, adjoint = (now, before), (end, after)
        for step in range(STEPS):
            here = tuple((bufs[step % 2], bufs[(step + 1) % 2]) for bufs in (forward, adjoint))

            def work(i0, layers, inner, here=here, step=step):
                def use(i, j, steps):
                    (applied, wave), (_, back) = steps
                    back = back + add_ref[step, i - (cx - (STEPS - 1) * HALO)]
                    if inner and 2 * step < STEPS:
                        applied_held[step, j] = applied
                        adjoint_held[step, j] = back
                    elif inner:
                        other = STEPS - 1 - step
                        terms = applied * adjoint_held[other, j] + back * applied_held[other, j]
                        image[j] = terms if 2 * step == STEPS else image[j] + terms
                    return wave, back

                march(here, slopes_ref, courant_ref, along_z, along_y, i0, layers, use)

            on_segments(step, left, right, cx, work)
            reach = (STEPS - 1 - step) * HALO
            low = jnp.where(left, cx - reach, cx)
            high = jnp.where(right, 2 * cx + reach, 2 * cx)
            value = wavelet_ref[0, step]
            made = here[0][1]

            @pl.when((layer >= low) & (layer < high))
            def _(made=made, value=value):
                old = made[layer, pl.ds(row, 1), :]
                made[layer, pl.ds(row, 1), :] = old + jnp.where(lanes == depth, value, 0.0)

            if step == 0:
                clear_sides(now, left, right, cx)
                clear_sides(end, left, right, cx)
        wave_ref[...] = forward[STEPS % 2][cx : 2 * cx].reshape(cx * ny, nz)
        adjoint_ref[...] = adjoint[STEPS % 2][cx : 2 * cx].reshape(cx * ny, nz)
        for place, mask in enumerate(order):
            y0 = pl.multiple_of((shot ^ mask) * block_rows, block_rows)
            gain = gain_ref[:, pl.ds(y0, block_rows), :]
            sums_ref[place] = (gain * image[:, pl.ds(y0, block_rows), :]).reshape(cx * block_rows, nz)


def pairs(axis_sizes, kind):
    tiles, shots = axis_sizes
    found = []
    for tile in range(tiles):
        other = tile ^ 1 if kind == "a" else ((tile + 1) ^ 1) - 1
        for shot in range(shots):
            here = tile * shots + shot
            if 0 <= other < tiles:
                found.append((here, other * shots + shot))
            elif shots % 2 == 0:
                found.append((here, tile * shots + (shot ^ 1)))
    return found


def local(
    velocity, density, wave_now, wave_before, adjoint_end, adjoint_after, source_cell, source_wave, receiver_cell, residual_traces,
    aperture,
):
    cx, _, nz = velocity.shape
    ny = wave_now.shape[2]
    shots = lax.axis_size("shot")
    tiles = lax.axis_size("tile")
    rows = cx * ny
    params = pltpu.CompilerParams(vmem_limit_bytes=VMEM_BYTES)

    def swap(x, kind):
        return lax.ppermute(x, ("tile", "shot"), pairs((tiles, shots), kind))

    def cross(x, mask):
        return lax.ppermute(x, "shot", [(i, i ^ mask) for i in range(shots)])

    fields = [x.reshape(rows, nz) for x in (wave_now, wave_before, adjoint_end, adjoint_after)]
    message = jax.ShapeDtypeStruct((2 * (cx + (STEPS - 1) * HALO), ny, nz), jnp.bfloat16)
    model, to_a, to_b, receivers = pl.pallas_call(
        pack_kernel,
        out_shape=(
            jax.ShapeDtypeStruct((2 * cx,) + velocity.shape[1:], jnp.bfloat16), message, message,
            jax.ShapeDtypeStruct((2 * STEPS, receiver_cell.shape[1]), jnp.float32),
        ),
        in_specs=[pl.BlockSpec(memory_space=pltpu.HBM)] * 8,
        out_specs=(pl.BlockSpec(memory_space=pltpu.HBM),) * 4,
        scratch_shapes=[pltpu.VMEM((2 * cx,) + velocity.shape[1:], jnp.bfloat16)]
        + [pltpu.VMEM((cx, ny, nz), jnp.bfloat16)] * 4
        + [
            pltpu.VMEM(receiver_cell.shape, jnp.int32),
            pltpu.VMEM(residual_traces.shape, jnp.float32),
            pltpu.VMEM((2 * STEPS, receiver_cell.shape[1]), jnp.float32),
            pltpu.SemaphoreType.DMA((8,)),
            pltpu.SemaphoreType.DMA((10,)),
        ],
        compiler_params=pltpu.CompilerParams(vmem_limit_bytes=PACK_BYTES),
        cost_estimate=pl.CostEstimate(flops=0, bytes_accessed=2 * 2**20, transcendentals=0),
        name="pack",
    )(velocity, density, wave_now, wave_before, adjoint_end, adjoint_after, receiver_cell, residual_traces)
    model, to_a, to_b = (x.reshape(-1, nz) for x in (model, to_a, to_b))

    from_a, from_b = swap(to_a, "a"), swap(to_b, "b")

    model_a, model_b = swap(model, "a"), swap(model, "b")
    high = shots // 2
    block_rows = model.shape[0]
    own = jnp.concatenate([model, model_b[:RIDERS]], axis=0)
    near = [([(0, 0)], own), ([(0, 1)], model_a), ([(0, 2)], model_b)]
    late = []
    if high:
        late.append(([(high, 1), (high, 2)], cross(jnp.concatenate([model_a, model_b], axis=0), high)))
        late.append(([(high, 0)], cross(own, high)[:block_rows]))

    along_z, along_y, added, joined = pl.pallas_call(
        lambda *refs: setup_kernel(cx, *refs),
        out_shape=(
            jax.ShapeDtypeStruct((2 * nz, 2 * nz), jnp.bfloat16),
            jax.ShapeDtypeStruct((2 * HALO * ny, HALO * ny), jnp.bfloat16),
            jax.ShapeDtypeStruct((STEPS, cx + 2 * (STEPS - 1) * HALO, ny, nz), jnp.float32),
            jax.ShapeDtypeStruct((len(near) * block_rows, nz), jnp.bfloat16),
        ),
        in_specs=[vmem()] * (1 + len(near)),
        out_specs=(vmem(),) * 4,
        compiler_params=params,
        cost_estimate=pl.CostEstimate(flops=2 * 10**9, bytes_accessed=4 * 2**20, transcendentals=0),
        name="receivers",
    )(receivers, *[block for _, block in near])

    near = [([name for names, _ in near for name in names], joined)]
    mask = high // 2
    while mask:
        moved = []
        for group in (near, late):
            names = [(m ^ mask, place) for held, _ in group for m, place in held]
            array = group[0][1] if len(group) == 1 else jnp.concatenate([block for _, block in group], axis=0)
            moved.append((names, cross(array, mask)))
        near, late = near + moved[:1], late + moved[1:]
        mask //= 2
    held = near + late

    field = pltpu.VMEM((3 * cx, ny, nz), jnp.float32)
    blocks = tuple(tuple(names) for names, _ in held)
    slopes, courant, gain = pl.pallas_call(
        lambda *refs: model_kernel(cx, ny, nz, shots, blocks, *refs),
        out_shape=(
            jax.ShapeDtypeStruct((3, 3 * cx, ny, nz), jnp.float32),
            jax.ShapeDtypeStruct((3 * cx, ny, nz), jnp.float32),
            jax.ShapeDtypeStruct((cx, ny, nz), jnp.float32),
        ),
        in_specs=[smem()] + [vmem()] * (len(held) + 2),
        out_specs=(vmem(),) * 3,
        scratch_shapes=[field],
        compiler_params=params,
        cost_estimate=pl.CostEstimate(flops=10**6, bytes_accessed=2**20, transcendentals=0),
        name="model",
    )(aperture, *[block for _, block in held], along_z, along_y)

    order = tuple(range(shots))
    sums, wave_end, adjoint_start = pl.pallas_call(
        lambda *refs: window_kernel(cx, ny, nz, order, *refs),
        out_shape=(
            jax.ShapeDtypeStruct((shots, cx * (ny // shots), nz), jnp.float32),
            jax.ShapeDtypeStruct((rows, nz), jnp.float32),
            jax.ShapeDtypeStruct((rows, nz), jnp.float32),
        ),
        in_specs=[smem()] * 3 + [vmem()] * 12,
        out_specs=(vmem(),) * 3,
        scratch_shapes=[field] * 4 + [pltpu.VMEM((STEPS // 2, cx, ny, nz), jnp.float32)] * 2 + [pltpu.VMEM((cx, ny, nz), jnp.float32)],
        compiler_params=params,
        cost_estimate=pl.CostEstimate(flops=10**10, bytes_accessed=16 * 2**20, transcendentals=0),
        name="window",
    )(aperture, source_cell, source_wave, along_z, along_y, slopes, courant, gain, added, *fields, from_a, from_b)
    total = sums[0]
    for place, mask in enumerate(order):
        if mask:
            total = total + cross(sums[place], mask)
    gradient = total.reshape(cx, ny // shots, nz)
    ends = [x.astype(jnp.bfloat16).reshape(wave_now.shape) for x in (wave_end, adjoint_start)]
    return gradient, ends[0], ends[1]


def solution(mesh):
    stored = P(("parts", "tile"), "shot", None)
    field = P(("parts", "shot"), "tile", None, None)
    return jax.shard_map(
        local,
        mesh=mesh,
        in_specs=(
            stored, stored, field, field, field, field, P(("parts", "shot")), P(("parts", "shot"), None),
            P(("parts", "shot"), None), P(("parts", "shot"), None, None), P(("parts", "shot"), None),
        ),
        out_specs=(stored, field, field),
        check_vma=False,
    )
```
